128 devices in a mesh: group: 2 (over z_lo), tensor: 16 (over y, x), seq: 4 (over z_hi, core).
Axes of the slice: x: 4, y: 4, z: 4 (z_hi: 2, z_lo: 2; z = z_hi * 2 + z_lo), core: 2. Of those that a mesh axis runs over, the one named last changes fastest.
Arguments:
- context: bfloat16 [1024, 3, 8192], P(('group', 'seq'), None, 'tensor'), may hold values from -6 to 6
- resid_in: bfloat16 [1024, 3, 8192], P('tensor', None, ('group', 'seq')), may hold values from -6 to 6
- target_out_w: bfloat16 [3, 8192, 8192], P(None, 'tensor', ('group', 'seq')), may hold values from -0.0625 to 0.0625
- embedded: bfloat16 [1024, 8192], P(('group', 'seq'), 'tensor'), may hold values from -6 to 6
- join_w: bfloat16 [3, 8192, 8192], P(None, ('group', 'seq'), 'tensor'), may hold values from -0.0390625 to 0.0390625
- embed_gain: bfloat16 [8192], P('tensor'), may hold values from 0.5 to 1.5
- joined_gain: bfloat16 [8192], P('tensor'), may hold values from 0.5 to 1.5
- query_w: bfloat16 [2, 8192, 8192], P(None, 'tensor', ('group', 'seq')), may hold values from -0.046875 to 0.046875
- key_w: bfloat16 [2, 8192, 1024], P(None, 'tensor', ('group', 'seq')), may hold values from -0.046875 to 0.046875
- value_w: bfloat16 [2, 8192, 1024], P(None, 'tensor', ('group', 'seq')), may hold values from -0.046875 to 0.046875
- out_w: bfloat16 [8192, 8192], P(('group', 'seq'), 'tensor'), may hold values from -0.0625 to 0.0625
- segment_ids: int32 [2, 512], replicated, may hold values from 0 to 7, never falling along the last dimension, each value on 1 to 128 neighbouring positions
- grad_hidden: bfloat16 [1024, 8192], P(('group', 'seq'), 'tensor'), may hold values from -0.1875 to 0.1875
Outputs:
- draft_hidden: bfloat16 [1024, 8192], P(('group', 'seq'), 'tensor')
- grad_join_w: bfloat16 [3, 8192, 8192], P(None, ('group', 'seq'), 'tensor')
- grad_query_w: bfloat16 [2, 8192, 8192], P(None, 'tensor', ('group', 'seq'))
- grad_key_w: bfloat16 [2, 8192, 1024], P(None, 'tensor', ('group', 'seq'))
- grad_value_w: bfloat16 [2, 8192, 1024], P(None, 'tensor', ('group', 'seq'))
- grad_out_w: bfloat16 [8192, 8192], P(('group', 'seq'), 'tensor')
The draws below stay inside these ranges and needn't reach their ends.
Inputs may be any that keep to these rules, and one draw needn't show every extreme that they name: `segment_ids`: ids never fall along a sequence; each run of one id is a packed document.
All inputs are finite; a program needn't handle non-finite values.
Results may differ from the reference program's by a relative error of at most 0.035.
Values may be sent and summed in bfloat16 or wider, within the bound.
A program may use at most 128 MiB of HBM per device.

```python
import math
import jax
import jax.numpy as jnp
import numpy as np
from jax import lax

D = 8192
HEADS = 64
KV_HEADS = 8
HEAD_DIM = 128
LEVELS = 3
LEN = 512
SEQS = 2
TOKENS = 1024
N_TENSOR = 16


def shard_levels(stream_key, shape, cuts, least, largest):
    level, own = 1.0, jax.random.fold_in(stream_key, 6)
    for axis_at, shards_of in cuts:
        heights = jnp.exp(jax.random.uniform(jax.random.fold_in(own, axis_at), (shards_of,), jnp.float32, least / len(cuts), largest / len(cuts)))
        level = level * jnp.repeat(heights, shape[axis_at] // shards_of).reshape([-1 if axis == axis_at else 1 for axis in range(len(shape))])
    return level


def profile(number_of, total, reach, skew):
    weights = [(1 << 20) // math.isqrt(rank ** skew) + 1 for rank in range(2, number_of + 1)]
    spare, counts = total - reach - (number_of - 1), [1] * (number_of - 1)
    while spare > 0:
        free = [i for i in range(number_of - 1) if counts[i] < reach]
        whole, left = sum([weights[i] for i in free]), spare
        for i in free:
            addition = min(reach - counts[i], max(1, left * weights[i] // whole), spare)
            counts[i] = counts[i] + addition
            spare = spare - addition
    return np.array([reach] + counts)


def ragged_sizes(key, count, total, reach, slope):
    if count == 2:
        one = jax.random.randint(key, (), max(1, total - reach), min(reach, total - 1) + 1)
        return jnp.stack([one, total - one])
    sizes = jnp.asarray(profile(count, total, reach, slope), jnp.int32)
    twos = (count - 1) // 2
    source_of, receiver = sizes[1:1 + 2 * twos:2], sizes[2:2 + 2 * twos:2]
    room = jnp.minimum(source_of - 1, reach - receiver)
    moved = jax.random.randint(jax.random.fold_in(key, 1), (twos,), 0, 1 << 20) % (room + 1)
    sizes = sizes.at[1:1 + 2 * twos:2].set(source_of - moved).at[2:2 + 2 * twos:2].set(receiver + moved)
    return sizes[jax.random.permutation(jax.random.fold_in(key, 2), count)]


def gaussian(stream_key, extent, width, most, shards=(), kind=jnp.bfloat16):
    level = shard_levels(stream_key, extent, shards, -0.22, 0.18) if shards else 1.0
    drawn = jax.random.normal(stream_key, extent, jnp.float32) * width * level
    return jnp.minimum(jnp.maximum(drawn, -most), most).astype(kind)


def setup_inputs(seed: int = 0) -> dict:
    splits = jax.random.split(jax.random.key(seed), 14)
    return {
        "context": gaussian(splits[0], (TOKENS, LEVELS, D), 1.0, 6.0, ((0, 8), (2, 16))),
        "resid_in": gaussian(splits[1], (TOKENS, LEVELS, D), 1.0, 6.0, ((0, 16), (2, 8))),
        "target_out_w": gaussian(splits[2], (LEVELS, D, D), D ** -0.5, 0.0625, ((1, 16), (2, 8))),
        "embedded": gaussian(splits[3], (TOKENS, D), 1.0, 6.0, ((0, 8), (1, 16))),
        "join_w": gaussian(splits[4], (LEVELS, D, D), (LEVELS * D) ** -0.5, 0.0390625, ((1, 8), (2, 16))),
        "embed_gain": jnp.clip(1.0 + 0.1 * jax.random.normal(splits[5], (D,), jnp.float32), 0.5, 1.5).astype(jnp.bfloat16),
        "joined_gain": jnp.clip(1.0 + 0.1 * jax.random.normal(splits[6], (D,), jnp.float32), 0.5, 1.5).astype(jnp.bfloat16),
        "query_w": gaussian(splits[7], (2, D, D), (2 * D) ** -0.5, 0.046875, ((1, 16), (2, 8))),
        "key_w": gaussian(splits[8], (2, D, KV_HEADS * HEAD_DIM), (2 * D) ** -0.5, 0.046875, ((1, 16), (2, 8))),
        "value_w": gaussian(splits[9], (2, D, KV_HEADS * HEAD_DIM), (2 * D) ** -0.5, 0.046875, ((1, 16), (2, 8))),
        "out_w": gaussian(splits[10], (D, D), D ** -0.5, 0.0625, ((0, 8), (1, 16))),
        "segment_ids": jax.vmap(lambda own: jnp.searchsorted(jnp.cumsum(ragged_sizes(own, 8, LEN, LEN // 4, 1)), jnp.arange(LEN), side="right"))(jax.random.split(splits[11], SEQS)).reshape((SEQS, LEN)).astype(jnp.int32),
        "grad_hidden": gaussian(splits[12], (TOKENS, D), (TOKENS ** -0.5), 0.1875, ((0, 8), (1, 16))),
    }


epsilon = 1e-05

def tensor_shard_sum(left_side, right_side):
    token_count, halves, inner_width = left_side.shape
    outer_width = right_side.shape[2]
    pieces = inner_width // N_TENSOR
    left_blocks = left_side.reshape(token_count, halves, N_TENSOR, pieces)
    right_blocks = right_side.reshape(halves, N_TENSOR, pieces, outer_width)

    def add_shard(running_sum, shard_index):
        left_piece = lax.dynamic_index_in_dim(left_blocks, shard_index, 2, keepdims=False)
        right_piece = lax.dynamic_index_in_dim(right_blocks, shard_index, 1, keepdims=False)
        product = jnp.einsum('thk,hkm->tm', left_piece.astype(jnp.float32), right_piece.astype(jnp.float32))
        rounded = lax.optimization_barrier(product.astype(jnp.bfloat16))
        return (running_sum + rounded.astype(jnp.float32), None)
    initial = jnp.zeros((token_count, outer_width), jnp.float32)
    result, unused = lax.scan(add_shard, initial, jnp.arange(N_TENSOR, dtype=jnp.int32))
    return result

def reference(context, resid_in, target_out_w, embedded, join_w, embed_gain, joined_gain, query_w, key_w, value_w, out_w, segment_ids, grad_hidden):
    level_rows = []
    for level_idx in range(LEVELS):
        summed = tensor_shard_sum(context[:, level_idx:level_idx + 1, :], target_out_w[level_idx:level_idx + 1])
        level_rows.append((resid_in[:, level_idx, :].astype(jnp.float32) + summed).astype(jnp.bfloat16))
    features = jnp.stack(level_rows, 1)
    joined = jnp.zeros((TOKENS, D), jnp.float32)
    for level_idx in range(LEVELS):
        joined = joined + jnp.dot(features[:, level_idx], join_w[level_idx], preferred_element_type=jnp.float32)
    joined_rate = lax.rsqrt(lax.optimization_barrier(jnp.mean(joined * joined, -1, keepdims=True)) + epsilon)
    joined_scale = joined_gain.astype(jnp.float32)
    hidden_norm = (joined * joined_rate * joined_scale).astype(jnp.bfloat16)
    embed_float = embedded.astype(jnp.float32)
    embed_rate = lax.rsqrt(lax.optimization_barrier(jnp.mean(embed_float * embed_float, -1, keepdims=True)) + epsilon)
    embed_norm = (embed_float * embed_rate * embed_gain.astype(jnp.float32)).astype(jnp.bfloat16)
    inputs = jnp.stack([embed_norm, hidden_norm], 1)
    query = tensor_shard_sum(inputs, query_w).astype(jnp.bfloat16)
    key = (jnp.dot(embed_norm, key_w[0], preferred_element_type=jnp.float32) + jnp.dot(hidden_norm, key_w[1], preferred_element_type=jnp.float32)).astype(jnp.bfloat16)
    value = (jnp.dot(embed_norm, value_w[0], preferred_element_type=jnp.float32) + jnp.dot(hidden_norm, value_w[1], preferred_element_type=jnp.float32)).astype(jnp.bfloat16)
    group_size = HEADS // KV_HEADS
    score_scale = HEAD_DIM ** (-0.5)
    queries = query.astype(jnp.float32).reshape(SEQS, LEN, KV_HEADS, group_size, HEAD_DIM)
    keys = key.astype(jnp.float32).reshape(SEQS, LEN, KV_HEADS, HEAD_DIM)
    values = value.astype(jnp.float32).reshape(SEQS, LEN, KV_HEADS, HEAD_DIM)
    position = jnp.arange(LEN, dtype=jnp.int32)
    allowed = (segment_ids[:, :, None] == segment_ids[:, None, :]) & (position[None, None, :] <= position[None, :, None])
    scores = jnp.einsum('bikgd,bjkd->bkgij', queries, keys) * score_scale
    scores = jnp.where(allowed[:, None, None], scores, -1e+30)
    probs = jax.nn.softmax(scores, axis=-1)
    probs_low = probs.astype(jnp.bfloat16)
    attended = jnp.einsum('bkgij,bjkd->bikgd', probs_low.astype(jnp.float32), values).reshape(TOKENS, D).astype(jnp.bfloat16)
    draft_hidden = (joined + jnp.dot(attended, out_w, preferred_element_type=jnp.float32)).astype(jnp.bfloat16)
    grad_out = jnp.dot(attended.T, grad_hidden, preferred_element_type=jnp.float32).astype(jnp.bfloat16)
    attended_grad = tensor_shard_sum(grad_hidden[:, None, :], out_w.T[None]).astype(jnp.bfloat16)
    grad_heads = attended_grad.astype(jnp.float32).reshape(SEQS, LEN, KV_HEADS, group_size, HEAD_DIM)
    probs_grad = jnp.einsum('bikgd,bjkd->bkgij', grad_heads, values)
    score_grad = (probs * (probs_grad - lax.optimization_barrier(jnp.sum(probs_grad * probs, -1, keepdims=True))) * score_scale).astype(jnp.bfloat16)
    score_float = score_grad.astype(jnp.float32)
    query_grad = jnp.einsum('bkgij,bjkd->bikgd', score_float, keys).reshape(TOKENS, D).astype(jnp.bfloat16)
    key_grad = jnp.einsum('bkgij,bikgd->bjkd', score_float, queries).reshape(TOKENS, KV_HEADS * HEAD_DIM).astype(jnp.bfloat16)
    value_grad = jnp.einsum('bkgij,bikgd->bjkd', probs_low.astype(jnp.float32), grad_heads).reshape(TOKENS, KV_HEADS * HEAD_DIM).astype(jnp.bfloat16)
    grad_query = jnp.stack([jnp.dot(inputs[:, half].T, query_grad, preferred_element_type=jnp.float32) for half in range(2)]).astype(jnp.bfloat16)
    grad_key = jnp.stack([jnp.dot(inputs[:, half].T, key_grad, preferred_element_type=jnp.float32) for half in range(2)]).astype(jnp.bfloat16)
    grad_value = jnp.stack([jnp.dot(inputs[:, half].T, value_grad, preferred_element_type=jnp.float32) for half in range(2)]).astype(jnp.bfloat16)
    hidden_grad = jnp.dot(query_grad, query_w[1].T, preferred_element_type=jnp.float32)
    hidden_grad = hidden_grad + jnp.dot(key_grad, key_w[1].T, preferred_element_type=jnp.float32)
    hidden_grad = hidden_grad + jnp.dot(value_grad, value_w[1].T, preferred_element_type=jnp.float32)
    scaled_grad = hidden_grad * joined_scale
    inner_mean = lax.optimization_barrier(jnp.mean(scaled_grad * joined, -1, keepdims=True))
    joined_grad = (grad_hidden.astype(jnp.float32) + joined_rate * scaled_grad - joined * (joined_rate * joined_rate * joined_rate) * inner_mean).astype(jnp.bfloat16)
    grad_join = jnp.stack([jnp.dot(features[:, level_idx].T, joined_grad, preferred_element_type=jnp.float32) for level_idx in range(LEVELS)]).astype(jnp.bfloat16)
    return (draft_hidden, grad_join, grad_query, grad_key, grad_value, grad_out)
```

```python
import functools

import jax
import jax.numpy as jnp
from jax import lax
from jax.experimental import pallas as pl
from jax.experimental.pallas import tpu as pltpu
from jax.sharding import PartitionSpec as P

epsilon = 1e-05
F32 = jnp.float32
BF16 = jnp.bfloat16
NEAR = (1, 3, 2)
VMEM_LIMIT = 60 * 2**20


def rem(value, count):
    return lax.rem(value, jnp.int32(count))


def group_of(z):
    return rem(z, 2) * 2 + lax.div(z, jnp.int32(2))


class Place:
    def __init__(self):
        self.t = lax.axis_index("tensor")
        seq = lax.axis_index("seq")
        self.x, self.y = rem(self.t, 4), lax.div(self.t, jnp.int32(4))
        self.z = lax.div(seq, jnp.int32(2)) * 2 + lax.axis_index("group")
        self.c = rem(seq, 2)

    def at(self, x=None, y=None, z=None, c=None):
        x = self.x if x is None else x
        y = self.y if y is None else y
        z = self.z if z is None else z
        c = self.c if c is None else c
        return (rem(z, 2), y * 4 + x, lax.div(z, jnp.int32(2)) * 2 + c)

    def to_x(self, d):
        return self.at(x=rem(self.x + d, 4))

    def to_y(self, d):
        return self.at(y=rem(self.y + d, 4))

    def to_z(self, d):
        return self.at(z=rem(self.z + d, 4))

    def sibling(self):
        return self.at(c=1 - self.c)


def greet(devices):
    barrier = pltpu.get_barrier_semaphore()
    for device in devices:
        pl.semaphore_signal(barrier, inc=1, device_id=device, device_id_type=pl.DeviceIdType.MESH)
    pl.semaphore_wait(barrier, len(devices))


def remote(src, dst, send, recv, device):
    return pltpu.make_async_remote_copy(
        src_ref=src,
        dst_ref=dst,
        send_sem=send,
        recv_sem=recv,
        device_id=device,
        device_id_type=pl.DeviceIdType.MESH,
    )


def rows(first, count):
    return pl.ds(pl.multiple_of(first, count), count)


def line_partners(place):
    return (
        [place.to_x(d) for d in NEAR]
        + [place.to_y(d) for d in NEAR]
        + [place.to_z(d) for d in NEAR]
        + [place.sibling()]
    )


def features_kernel(
    ctx, resid, wt, wj, joined, feats,
    ca, sb, rx, ry, s0, s1, r2x, r2y, fa, js, jx, j2, jz,
    s_z, r_z, s_c, r_c, s_x, r_x, s_y, r_y, s_2x, r_2x, s_2y, r_2y,
    s_f1, r_f1, s_f2, r_f2, s_jx, r_jx, s_jz, r_jz, s_out,
):
    me = Place()
    x, y, z, c = me.x, me.y, me.z, me.c
    sib = me.sibling()
    group = [group_of(rem(z + e, 4)) for e in range(4)]
    half = rows(c * 128, 128)
    mine = rows(x * 64, 64)
    greet(line_partners(me))
    sends = []

    def send(src, dst, ss, rs, device):
        copy = remote(src, dst, ss, rs, device)
        copy.start()
        sends.append(copy)

    def arrived(dst, rs):
        remote(dst, dst, s_c.at[0], rs, sib).wait_recv()

    send(ctx, ca.at[group[0], :, half, :], s_c.at[0], r_c.at[0], sib)
    for d in NEAR:
        send(ctx, ca.at[group[0], :, half, :], s_z.at[d - 1], r_z.at[3 - d], me.to_z(d))
    ca[group[0], :, half, :] = ctx[...]

    def target(e):
        def level(l, carry):
            for j in range(4):
                part = jnp.dot(
                    ca[group[e], l], wt[l, :, j * 256 : (j + 1) * 256], preferred_element_type=F32
                )
                sb[j // 2, e, l, :, (j % 2) * 256 : (j % 2 + 1) * 256] = part.astype(BF16)
            return carry

        lax.fori_loop(0, 3, level, 0)
        for d in NEAR:
            to = rem(x + d, 4)
            send(sb.at[0, e, :, rows(to * 64, 64), :], rx.at[e, 3 - d], s_x.at[e, d - 1], r_x.at[e, 3 - d], me.at(x=to))
        slot = rem(y - group[e] + 4, 4)

        @pl.when(slot != 0)
        def _():
            remote(sb.at[1, e], ry.at[slot - 1], s_y.at[e], r_y.at[slot - 1], me.at(y=group[e])).start()

    def collect_x(e):
        for d in NEAR:
            arrived(rx.at[e, d - 1], r_x.at[e, d - 1])

        def level(l, carry):
            total = sb[0, e, l, mine, :].astype(F32)
            for d in range(3):
                total = total + rx[e, d, l].astype(F32)
            s0[e, l] = total.astype(BF16)
            return carry

        lax.fori_loop(0, 3, level, 0)
        slot = rem(y - group[e] + 4, 4)

        @pl.when(slot != 0)
        def _():
            remote(s0.at[e], r2x.at[slot - 1], s_2x.at[e], r_2x.at[slot - 1], me.at(y=group[e])).start()

    other = rows((1 - c) * 128, 128)

    def context_in(e):
        if e:
            arrived(ca.at[group[e], :, half, :], r_z.at[e - 1])
            send(ca.at[group[e], :, half, :], ca.at[group[e], :, half, :], s_c.at[e], r_c.at[e], sib)
        arrived(ca.at[group[e], :, other, :], r_c.at[e])

    for e in (0, 1, 3):
        context_in(e)
        target(e)
    collect_x(0)
    context_in(2)
    target(2)
    for e in (1, 3, 2):
        collect_x(e)
    own = rem(group_of(y) - z + 4, 4)
    for d in NEAR:
        arrived(ry.at[d - 1], r_y.at[d - 1])

    def fold(i, carry):
        l, part = lax.div(i, jnp.int32(4)), rows(rem(i, 4) * 64, 64)
        total = sb[1, own, l, part, :].astype(F32)
        for d in range(3):
            total = total + ry[d, l, part, :].astype(F32)
        s1[l, part, :] = total.astype(BF16)
        return carry

    lax.fori_loop(0, 12, fold, 0)
    for d in NEAR:
        to = rem(x + d, 4)
        send(s1.at[:, rows(to * 64, 64), :], r2y.at[3 - d], s_2y.at[d - 1], r_2y.at[3 - d], me.at(x=to))
    for d in NEAR:
        arrived(r2x.at[d - 1], r_2x.at[d - 1])

    def finish(h, part, got):
        def level(l, carry):
            total = part(l).astype(F32)
            for d in range(3):
                total = total + got[d, l].astype(F32)
            fa[h, y, l, mine, :] = (resid[l, :, h * 512 : (h + 1) * 512].astype(F32) + total).astype(BF16)
            return carry

        lax.fori_loop(0, 3, level, 0)

    def block(h, q, p):
        return fa.at[h, q, :, rows(p * 64, 64), :]

    def spread_x(h, q, p, ss, rs):
        for d in NEAR:
            send(block(h, q, p), block(h, q, p), ss(d - 1), rs(3 - d), me.to_x(d))

    def spread_y(h, q, p, ss, rs):
        for d in NEAR:
            send(block(h, q, p), block(h, q, p), ss(d - 1), rs(3 - d), me.to_y(d))

    finish(0, lambda l: s0[own, l], r2x)
    spread_x(0, y, x, lambda i: s_f1.at[0, i], lambda i: r_f1.at[0, i])
    spread_y(0, y, x, lambda i: s_f2.at[0, i, 0], lambda i: r_f2.at[0, i, 0])
    for d in NEAR:
        arrived(r2y.at[d - 1], r_2y.at[d - 1])
    finish(1, lambda l: s1[l, mine, :], r2y)
    spread_y(1, y, x, lambda i: s_f1.at[1, i], lambda i: r_f1.at[1, i])
    spread_x(1, y, x, lambda i: s_f2.at[1, i, 0], lambda i: r_f2.at[1, i, 0])
    for e in NEAR:
        p, q = rem(x + e, 4), rem(y + e, 4)
        arrived(block(0, y, p), r_f1.at[0, e - 1])
        spread_y(0, y, p, lambda i: s_f2.at[0, i, e], lambda i: r_f2.at[0, i, e])
        arrived(block(1, q, x), r_f1.at[1, e - 1])
        spread_x(1, q, x, lambda i: s_f2.at[1, i, e], lambda i: r_f2.at[1, i, e])

    def join(e):
        q = rem(y + e, 4)
        if e:
            for p in range(4):
                arrived(block(0, q, rem(x + p, 4)), r_f2.at[0, e - 1, p])
        for p in NEAR:
            arrived(block(1, q, rem(x + p, 4)), r_f2.at[1, p - 1, e])
        for h in range(2):
            pltpu.make_async_copy(fa.at[h, q], feats.at[h, q], s_out.at[h, e]).start()
        for j in range(2):
            columns = slice(j * 256, (j + 1) * 256)
            total = jnp.zeros((256, 256), F32)
            for l in range(3):
                for h in range(2):
                    total = total + jnp.dot(
                        fa[h, q, l], wj[l, h * 512 : (h + 1) * 512, columns], preferred_element_type=F32
                    )
            js[e, :, columns] = total.astype(BF16)
        send(js.at[e, other, :], jx.at[e], s_jx.at[e], r_jx.at[e], sib)

    def pair(e):
        q = rem(y + e, 4)
        arrived(jx.at[e], r_jx.at[e])
        j2[e] = (js[e, half, :].astype(F32) + jx[e].astype(F32)).astype(BF16)
        to = group_of(q)
        slot = rem(z - to + 4, 4)

        @pl.when(slot != 0)
        def _():
            remote(j2.at[e], jz.at[slot - 1], s_jz.at[e], r_jz.at[slot - 1], me.at(z=to)).start()

    join(0)
    join(1)
    pair(0)
    join(3)
    pair(1)
    join(2)
    pair(3)
    pair(2)
    for d in NEAR:
        arrived(jz.at[d - 1], r_jz.at[d - 1])
    kept = rem(group_of(z) - y + 4, 4)
    total = j2[kept].astype(F32)
    for d in range(3):
        total = total + jz[d].astype(F32)
    joined[...] = total

    for copy in sends:
        copy.wait_send()
    for e in range(4):

        @pl.when(rem(y - group[e] + 4, 4) != 0)
        def _():
            remote(sb.at[1, e], ry.at[0], s_y.at[e], r_y.at[0], sib).wait_send()
            remote(s0.at[e], r2x.at[0], s_2x.at[e], r_2x.at[0], sib).wait_send()

        @pl.when(group_of(rem(y + e, 4)) != z)
        def _():
            remote(j2.at[e], jz.at[0], s_jz.at[e], r_jz.at[0], sib).wait_send()

        for h in range(2):
            q = rem(y + e, 4)
            pltpu.make_async_copy(fa.at[h, q], feats.at[h, q], s_out.at[h, e]).wait()


def vmem(*shape, dtype=BF16):
    return pltpu.VMEM(shape, dtype)


def dma(*shape):
    return pltpu.SemaphoreType.DMA(shape)


IN_VMEM = pl.BlockSpec(memory_space=pltpu.VMEM)
ANYWHERE = pl.BlockSpec(memory_space=pl.ANY)


def features_call(ctx, resid, wt, wj):
    return pl.pallas_call(
        features_kernel,
        name="features",
        out_shape=(
            jax.ShapeDtypeStruct((128, 512), F32),
            jax.ShapeDtypeStruct((2, 4, 3, 256, 512), BF16),
        ),
        in_specs=[IN_VMEM] * 4,
        out_specs=(IN_VMEM, ANYWHERE),
        scratch_shapes=[
            vmem(4, 3, 256, 512),
            vmem(2, 4, 3, 256, 512),
            vmem(4, 3, 3, 64, 512),
            vmem(3, 3, 256, 512),
            vmem(4, 3, 64, 512),
            vmem(3, 256, 512),
            vmem(3, 3, 64, 512),
            vmem(3, 3, 64, 512),
            vmem(2, 4, 3, 256, 512),
            vmem(4, 256, 512),
            vmem(4, 128, 512),
            vmem(4, 128, 512),
            vmem(3, 128, 512),
            dma(3), dma(3), dma(4), dma(4), dma(4, 3), dma(4, 3), dma(4), dma(3),
            dma(4), dma(3), dma(3), dma(3),
            dma(2, 3), dma(2, 3), dma(2, 3, 4), dma(2, 3, 4), dma(4), dma(4), dma(4), dma(3), dma(2, 4),
        ],
        compiler_params=pltpu.CompilerParams(
            collective_id=0, has_side_effects=True, vmem_limit_bytes=VMEM_LIMIT
        ),
        cost_estimate=pl.CostEstimate(flops=6500000000, bytes_accessed=14000000, transcendentals=0),
    )(ctx, resid, wt, wj)


def gather_groups(values):
    return lax.all_gather(values, ("group", "seq"), axis=0, tiled=True)


def gather_tensor(values):
    return lax.all_gather(values, "tensor", axis=0, tiled=True)


def partial_tensor(builder, row_count):
    return lax.psum_scatter(
        builder(jnp.int32(0), row_count * lax.axis_size("tensor")).astype(jnp.bfloat16),
        "tensor",
        scatter_dimension=0,
        tiled=True,
    ).astype(jnp.float32)


def partial_groups(builder, row_count):
    return lax.psum_scatter(
        builder(jnp.int32(0), row_count * lax.axis_size(("group", "seq"))),
        ("group", "seq"),
        scatter_dimension=0,
        tiled=True,
    )


def totals_tensor(values):
    return lax.psum(values, "tensor")


def local(
    context,
    resid_in,
    target_out_w,
    embedded,
    join_w,
    embed_gain,
    joined_gain,
    query_w,
    key_w,
    value_w,
    out_w,
    segment_ids,
    grad_hidden,
):
    tensor_count = lax.axis_size("tensor")
    group_count = lax.axis_size(("group", "seq"))
    tensor_index = lax.axis_index("tensor")
    group_rows = embedded.shape[0]
    token_count = group_rows * group_count
    tensor_rows = token_count // tensor_count
    model_width = embedded.shape[1] * tensor_count
    head_dim = key_w.shape[2]
    group_heads = query_w.shape[2] // head_dim
    seq_len = segment_ids.shape[1]
    score_scale = head_dim ** (-0.5)
    joined, feats = features_call(
        context.transpose(1, 0, 2), resid_in.transpose(1, 0, 2), target_out_w, join_w
    )
    embed_float = embedded.astype(jnp.float32)
    joined_squares, embed_squares = totals_tensor(
        (jnp.sum(joined * joined, -1), jnp.sum(embed_float * embed_float, -1))
    )
    joined_rate = lax.rsqrt(joined_squares / model_width + epsilon)[:, None]
    embed_rate = lax.rsqrt(embed_squares / model_width + epsilon)[:, None]
    joined_scale = joined_gain.astype(jnp.float32)
    hidden_norm = (joined * joined_rate * joined_scale).astype(jnp.bfloat16)
    embed_norm = (embed_float * embed_rate * embed_gain.astype(jnp.float32)).astype(jnp.bfloat16)
    inputs_all = gather_groups(jnp.stack([embed_norm, hidden_norm], 1))

    def query_term(first_row, row_count):
        return jnp.einsum("thk,hkm->tm", inputs_all, query_w, preferred_element_type=jnp.float32)

    query = partial_tensor(query_term, tensor_rows).astype(jnp.bfloat16)
    key_part = jnp.einsum("thk,hkm->tm", inputs_all, key_w, preferred_element_type=jnp.float32)
    value_part = jnp.einsum("thk,hkm->tm", inputs_all, value_w, preferred_element_type=jnp.float32)
    key_sum, value_sum = totals_tensor((key_part, value_part))
    key_full = key_sum.astype(jnp.bfloat16)
    value_full = value_sum.astype(jnp.bfloat16)
    first_query = tensor_index * tensor_rows
    seq_start = first_query // seq_len * seq_len
    flat_segments = segment_ids.reshape(-1)
    query_segment = lax.dynamic_slice_in_dim(flat_segments, first_query, tensor_rows, 0)
    key_segment = lax.dynamic_slice_in_dim(flat_segments, seq_start, seq_len, 0)
    query_pos = first_query + jnp.arange(tensor_rows, dtype=jnp.int32)
    key_pos = seq_start + jnp.arange(seq_len, dtype=jnp.int32)
    allowed = (query_segment[:, None] == key_segment[None, :]) & (
        key_pos[None, :] <= query_pos[:, None]
    )
    keys_local = lax.dynamic_slice_in_dim(key_full, seq_start, seq_len, 0)
    values_local = lax.dynamic_slice_in_dim(value_full, seq_start, seq_len, 0)
    query_heads = query.reshape(tensor_rows, group_heads, head_dim)
    scores = (
        jnp.einsum("igd,jd->gij", query_heads, keys_local, preferred_element_type=jnp.float32)
        * score_scale
    )
    scores = jnp.where(allowed[None], scores, -1e30)
    probs = jax.nn.softmax(scores, axis=-1)
    probs_low = probs.astype(jnp.bfloat16)
    attended = jnp.einsum(
        "gij,jd->igd", probs_low, values_local, preferred_element_type=jnp.float32
    )
    attended = attended.reshape(tensor_rows, group_heads * head_dim).astype(jnp.bfloat16)
    attended_all = gather_tensor(attended)

    def output_term(first_row, row_count):
        return jnp.dot(attended_all, out_w, preferred_element_type=jnp.float32)

    attn_sum = partial_groups(output_term, group_rows)
    draft_hidden = (joined + attn_sum).astype(jnp.bfloat16)
    cotangent_all = gather_groups(grad_hidden)
    grad_out = jnp.einsum(
        "tm,tn->mn", attended_all, cotangent_all, preferred_element_type=jnp.float32
    ).astype(jnp.bfloat16)

    def back_term(first_row, row_count):
        return jnp.einsum("tn,mn->tm", cotangent_all, out_w, preferred_element_type=jnp.float32)

    attended_grad = partial_tensor(back_term, tensor_rows).astype(jnp.bfloat16)
    grad_heads = attended_grad.reshape(tensor_rows, group_heads, head_dim)
    probs_grad = jnp.einsum(
        "igd,jd->gij", grad_heads, values_local, preferred_element_type=jnp.float32
    )
    score_grad = (
        probs * (probs_grad - jnp.sum(probs_grad * probs, -1, keepdims=True)) * score_scale
    ).astype(jnp.bfloat16)
    query_grad = jnp.einsum(
        "gij,jd->igd", score_grad, keys_local, preferred_element_type=jnp.float32
    )
    query_grad = query_grad.reshape(tensor_rows, group_heads * head_dim).astype(jnp.bfloat16)
    key_local = jnp.einsum(
        "gij,igd->jd", score_grad, query_heads, preferred_element_type=jnp.float32
    )
    value_local = jnp.einsum(
        "gij,igd->jd", probs_low, grad_heads, preferred_element_type=jnp.float32
    )
    zeros_full = jnp.zeros((token_count, head_dim), jnp.float32)
    key_grad_sum, value_grad_sum = totals_tensor(
        (
            lax.dynamic_update_slice_in_dim(zeros_full, key_local, seq_start, 0),
            lax.dynamic_update_slice_in_dim(zeros_full, value_local, seq_start, 0),
        )
    )
    key_grad = key_grad_sum.astype(jnp.bfloat16)
    value_grad = value_grad_sum.astype(jnp.bfloat16)
    query_grad_all = gather_tensor(query_grad)
    grad_query = jnp.einsum(
        "thk,tm->hkm", inputs_all, query_grad_all, preferred_element_type=jnp.float32
    ).astype(jnp.bfloat16)
    grad_key = jnp.einsum(
        "thk,tm->hkm", inputs_all, key_grad, preferred_element_type=jnp.float32
    ).astype(jnp.bfloat16)
    grad_value = jnp.einsum(
        "thk,tm->hkm", inputs_all, value_grad, preferred_element_type=jnp.float32
    ).astype(jnp.bfloat16)

    def input_term(first_row, row_count):
        running = jnp.einsum(
            "tm,km->tk", query_grad_all, query_w[1], preferred_element_type=jnp.float32
        )
        running = running + jnp.einsum(
            "tm,km->tk", key_grad, key_w[1], preferred_element_type=jnp.float32
        )
        return running + jnp.einsum(
            "tm,km->tk", value_grad, value_w[1], preferred_element_type=jnp.float32
        )

    hidden_grad = partial_groups(input_term, group_rows)
    scaled_grad = hidden_grad * joined_scale
    inner_sum = totals_tensor(jnp.sum(scaled_grad * joined, -1))
    joined_grad = (
        grad_hidden.astype(jnp.float32)
        + joined_rate * scaled_grad
        - joined * (joined_rate * joined_rate * joined_rate) * (inner_sum / model_width)[:, None]
    )
    joined_grad_all = gather_groups(joined_grad.astype(jnp.bfloat16))
    grad_join = jnp.einsum(
        "hqltk,qtm->lhkm",
        feats,
        joined_grad_all.reshape(4, 256, -1),
        preferred_element_type=jnp.float32,
    ).astype(jnp.bfloat16)
    grad_join = grad_join.reshape(join_w.shape)
    return (draft_hidden, grad_join, grad_query, grad_key, grad_value, grad_out)


def solution(mesh):
    in_specs = (
        P(("group", "seq"), None, "tensor"),
        P("tensor", None, ("group", "seq")),
        P(None, "tensor", ("group", "seq")),
        P(("group", "seq"), "tensor"),
        P(None, ("group", "seq"), "tensor"),
        P("tensor"),
        P("tensor"),
        P(None, "tensor", ("group", "seq")),
        P(None, "tensor", ("group", "seq")),
        P(None, "tensor", ("group", "seq")),
        P(("group", "seq"), "tensor"),
        P(),
        P(("group", "seq"), "tensor"),
    )
    out_specs = (
        P(("group", "seq"), "tensor"),
        P(None, ("group", "seq"), "tensor"),
        P(None, "tensor", ("group", "seq")),
        P(None, "tensor", ("group", "seq")),
        P(None, "tensor", ("group", "seq")),
        P(("group", "seq"), "tensor"),
    )
    return jax.shard_map(local, mesh=mesh, in_specs=in_specs, out_specs=out_specs, check_vma=False)
```

```python
import functools

import jax
import jax.numpy as jnp
from jax import lax
from jax.experimental import pallas as pl
from jax.experimental.pallas import tpu as pltpu
from jax.sharding import PartitionSpec as P

epsilon = 1e-05
F32 = jnp.float32
BF16 = jnp.bfloat16
NEAR = (1, 3, 2)
VMEM_LIMIT = 60 * 2**20


def rem(value, count):
    return lax.rem(value, jnp.int32(count))


def group_of(z):
    return rem(z, 2) * 2 + lax.div(z, jnp.int32(2))


class Place:
    def __init__(self):
        self.t = lax.axis_index("tensor")
        seq = lax.axis_index("seq")
        self.x, self.y = rem(self.t, 4), lax.div(self.t, jnp.int32(4))
        self.z = lax.div(seq, jnp.int32(2)) * 2 + lax.axis_index("group")
        self.c = rem(seq, 2)

    def at(self, x=None, y=None, z=None, c=None):
        x = self.x if x is None else x
        y = self.y if y is None else y
        z = self.z if z is None else z
        c = self.c if c is None else c
        return (rem(z, 2), y * 4 + x, lax.div(z, jnp.int32(2)) * 2 + c)

    def to_x(self, d):
        return self.at(x=rem(self.x + d, 4))

    def to_y(self, d):
        return self.at(y=rem(self.y + d, 4))

    def to_z(self, d):
        return self.at(z=rem(self.z + d, 4))

    def sibling(self):
        return self.at(c=1 - self.c)


def greet(devices):
    barrier = pltpu.get_barrier_semaphore()
    for device in devices:
        pl.semaphore_signal(barrier, inc=1, device_id=device, device_id_type=pl.DeviceIdType.MESH)
    pl.semaphore_wait(barrier, len(devices))


def remote(src, dst, send, recv, device):
    return pltpu.make_async_remote_copy(
        src_ref=src,
        dst_ref=dst,
        send_sem=send,
        recv_sem=recv,
        device_id=device,
        device_id_type=pl.DeviceIdType.MESH,
    )


def rows(first, count):
    return pl.ds(pl.multiple_of(first, count), count)


def line_partners(place):
    return (
        [place.to_x(d) for d in NEAR]
        + [place.to_y(d) for d in NEAR]
        + [place.to_z(d) for d in NEAR]
        + [place.sibling()]
    )


def vmem(*shape, dtype=BF16):
    return pltpu.VMEM(shape, dtype)


def dma(*shape):
    return pltpu.SemaphoreType.DMA(shape)


IN_VMEM = pl.BlockSpec(memory_space=pltpu.VMEM)
ANYWHERE = pl.BlockSpec(memory_space=pl.ANY)


def nt(a, b):
    return lax.dot_general(a, b, (((1,), (1,)), ((), ())), preferred_element_type=F32)


def tn(a, b):
    return lax.dot_general(a, b, (((0,), (0,)), ((), ())), preferred_element_type=F32)


def dot(a, b):
    return jnp.dot(a, b, preferred_element_type=F32)


class Mover:
    def __init__(self, me, dummy):
        self.me, self.dummy, self.sends, self.guarded = me, dummy, [], []

    def send(self, src, dst, ss, rs, device, when=None):
        copy = remote(src, dst, ss, rs, device)
        if when is None:
            copy.start()
            self.sends.append(copy)
        else:
            pl.when(when)(copy.start)
            self.guarded.append((when, src, ss))

    def arrived(self, dst, rs):
        remote(dst, dst, self.dummy, rs, self.me.sibling()).wait_recv()

    def drain(self):
        for copy in self.sends:
            copy.wait_send()
        for when, src, ss in self.guarded:
            pl.when(when)(remote(src, src, ss, self.dummy, self.me.sibling()).wait_send)


class GatherG:
    def __init__(self, mv, block, s_z, r_z, s_c, r_c):
        me = mv.me
        self.mv, self.block, self.sems = mv, block, (s_z, r_z, s_c, r_c)
        self.group = [group_of(rem(me.z + e, 4)) for e in range(4)]

    def to_sibling(self, e, src=None):
        me, (_, _, s_c, r_c) = self.mv.me, self.sems
        place = self.block(self.group[e], me.c)
        self.mv.send(place if src is None else src, place, s_c.at[e], r_c.at[e], me.sibling())

    def along_z(self, src=None):
        me, (s_z, r_z, _, _) = self.mv.me, self.sems
        place = self.block(self.group[0], me.c)
        for d in NEAR:
            self.mv.send(place if src is None else src, place, s_z.at[d - 1], r_z.at[3 - d], me.to_z(d))

    def forward(self, e):
        me, (_, r_z, _, _) = self.mv.me, self.sems
        self.mv.arrived(self.block(self.group[e], me.c), r_z.at[e - 1])
        self.to_sibling(e)

    def whole(self, e):
        me, (_, _, _, r_c) = self.mv.me, self.sems
        self.mv.arrived(self.block(self.group[e], 1 - me.c), r_c.at[e])


class GatherT:
    def __init__(self, mv, block, s_1, r_1, s_2, r_2):
        self.mv, self.block, self.sems = mv, block, (s_1, r_1, s_2, r_2)

    def spread(self, along_x, h, q, p, ss, rs):
        me = self.mv.me
        for d in NEAR:
            to = me.to_x(d) if along_x else me.to_y(d)
            self.mv.send(self.block(h, q, p), self.block(h, q, p), ss(d - 1), rs(3 - d), to)

    def start(self, h):
        me, (s_1, r_1, s_2, r_2) = self.mv.me, self.sems
        self.spread(h == 0, h, me.y, me.x, lambda i: s_1.at[h, i], lambda i: r_1.at[h, i])
        self.spread(h == 1, h, me.y, me.x, lambda i: s_2.at[h, i, 0], lambda i: r_2.at[h, i, 0])

    def forward(self):
        me, (s_1, r_1, s_2, r_2) = self.mv.me, self.sems
        for e in NEAR:
            p, q = rem(me.x + e, 4), rem(me.y + e, 4)
            self.mv.arrived(self.block(0, me.y, p), r_1.at[0, e - 1])
            self.spread(False, 0, me.y, p, lambda i: s_2.at[0, i, e], lambda i: r_2.at[0, i, e])
            self.mv.arrived(self.block(1, q, me.x), r_1.at[1, e - 1])
            self.spread(True, 1, q, me.x, lambda i: s_2.at[1, i, e], lambda i: r_2.at[1, i, e])

    def group(self, e):
        me, (_, _, _, r_2) = self.mv.me, self.sems
        q = rem(me.y + e, 4)
        if e:
            for p in range(4):
                self.mv.arrived(self.block(0, q, rem(me.x + p, 4)), r_2.at[0, e - 1, p])
        for p in NEAR:
            self.mv.arrived(self.block(1, q, rem(me.x + p, 4)), r_2.at[1, p - 1, e])
        return q


class SumG:
    def __init__(self, mv, js, jx, j2, jz, s_x, r_x, s_z, r_z):
        self.mv, self.refs, self.sems = mv, (js, jx, j2, jz), (s_x, r_x, s_z, r_z)

    def swap(self, e):
        (js, jx, _, _), (s_x, r_x, _, _), me = self.refs, self.sems, self.mv.me
        self.mv.send(js.at[e, rows((1 - me.c) * 128, 128), :], jx.at[e], s_x.at[e], r_x.at[e], me.sibling())

    def pair(self, e):
        (js, jx, j2, jz), (_, r_x, s_z, r_z), me = self.refs, self.sems, self.mv.me
        self.mv.arrived(jx.at[e], r_x.at[e])
        j2[e] = (js[e, rows(me.c * 128, 128), :].astype(F32) + jx[e].astype(F32)).astype(BF16)
        to = group_of(rem(me.y + e, 4))
        slot = rem(me.z - to + 4, 4)
        at = jnp.maximum(slot - 1, 0)
        self.mv.send(j2.at[e], jz.at[at], s_z.at[e], r_z.at[at], me.at(z=to), when=slot != 0)

    def total(self):
        (_, _, j2, jz), (_, _, _, r_z), me = self.refs, self.sems, self.mv.me
        for d in NEAR:
            self.mv.arrived(jz.at[d - 1], r_z.at[d - 1])
        total = j2[rem(group_of(me.z) - me.y + 4, 4)].astype(F32)
        for d in range(3):
            total = total + jz[d].astype(F32)
        return total

    @staticmethod
    def scratch():
        return [vmem(4, 256, 512), vmem(4, 128, 512), vmem(4, 128, 512), vmem(3, 128, 512), dma(4), dma(4), dma(4), dma(3)]


class SumT:
    def __init__(self, mv, ps, rx, ry, s0, s1, r2x, r2y, *sems):
        self.mv, self.ps, self.rx, self.ry, self.s0, self.s1, self.r2x, self.r2y = mv, ps, rx, ry, s0, s1, r2x, r2y
        self.sems = sems

    def issue(self, e):
        mv, me = self.mv, self.mv.me
        s_x, r_x, s_y, r_y = self.sems[:4]
        for d in NEAR:
            to = rem(me.x + d, 4)
            mv.send(self.ps.at[0, e, rows(to * 64, 64), :], self.rx.at[e, 3 - d], s_x.at[e, d - 1], r_x.at[e, 3 - d], me.at(x=to))
        if e:
            mv.send(self.ps.at[1, e], self.ry.at[3 - e], s_y.at[e], r_y.at[3 - e], me.to_y(e))

    def collect_x(self, e):
        mv, me = self.mv, self.mv.me
        r_x, s_2x, r_2x = self.sems[1], self.sems[4], self.sems[5]
        for d in NEAR:
            mv.arrived(self.rx.at[e, d - 1], r_x.at[e, d - 1])
        total = self.ps[0, e, rows(me.x * 64, 64), :].astype(F32)
        for d in range(3):
            total = total + self.rx[e, d].astype(F32)
        self.s0[e] = total.astype(BF16)
        if e:
            mv.send(self.s0.at[e], self.r2x.at[3 - e], s_2x.at[e], r_2x.at[3 - e], me.to_y(e))

    def fold(self):
        mv, me = self.mv, self.mv.me
        r_y, s_2y, r_2y = self.sems[3], self.sems[6], self.sems[7]
        for d in NEAR:
            mv.arrived(self.ry.at[d - 1], r_y.at[d - 1])
        for d in (2, 1, 3, 0):
            to = rem(me.x + d, 4)
            part = rows(to * 64, 64)
            total = self.ps[1, 0, part, :].astype(F32)
            for i in range(3):
                total = total + self.ry[i, part, :].astype(F32)
            self.s1[part, :] = total.astype(BF16)
            if d:
                mv.send(self.s1.at[part, :], self.r2y.at[3 - d], s_2y.at[d - 1], r_2y.at[3 - d], me.at(x=to))

    def finish(self, h):
        mv, me = self.mv, self.mv.me
        got, sem = ((self.r2x, self.sems[5]), (self.r2y, self.sems[7]))[h]
        for d in NEAR:
            mv.arrived(got.at[d - 1], sem.at[d - 1])
        total = (self.s0[0] if h == 0 else self.s1[rows(me.x * 64, 64), :]).astype(F32)
        for d in range(3):
            total = total + got[d].astype(F32)
        return total.astype(BF16)

    @staticmethod
    def scratch(w):
        return [
            vmem(2, 4, 256, w), vmem(4, 3, 64, w), vmem(3, 256, w), vmem(4, 64, w), vmem(256, w), vmem(3, 64, w), vmem(3, 64, w),
            dma(4, 3), dma(4, 3), dma(4), dma(3), dma(4), dma(3), dma(3), dma(3),
        ]


def lanes(column):
    return jnp.broadcast_to(column, (128, 128)).T[0:8, :]


def column(row):
    return jnp.broadcast_to(row, (128, 128)).T[:, 0:1]


class StatsT:
    def __init__(self, mv, tiles, s_t, r_t):
        self.mv, self.tiles, self.s_t, self.r_t = mv, tiles, s_t, r_t

    def start(self, tile):
        me = self.mv.me
        self.tiles[0] = tile
        for d in range(1, 16):
            dx, dy = d % 4, d // 4
            back = (4 - dx) % 4 + 4 * ((4 - dy) % 4)
            to = me.at(x=rem(me.x + dx, 4), y=rem(me.y + dy, 4))
            self.mv.send(self.tiles.at[0], self.tiles.at[back], self.s_t.at[d], self.r_t.at[back], to)

    def total(self):
        for d in range(1, 16):
            self.mv.arrived(self.tiles.at[d], self.r_t.at[d])
        total = self.tiles[0]
        for d in range(1, 16):
            total = total + self.tiles[d]
        return total

    @staticmethod
    def scratch():
        return [pltpu.VMEM((16, 8, 128), F32), dma(16), dma(16)]


def take(refs, count):
    out = refs[:count]
    del refs[:count]
    return out


def features_kernel(
    ctx, resid, wt, wj, early, joined, feats, early_all,
    ca, sb, rx, ry, s0, s1, r2x, r2y, fa, js, jx, j2, jz, ea,
    s_z, r_z, s_c, r_c, s_x, r_x, s_y, r_y, s_2x, r_2x, s_2y, r_2y,
    s_f1, r_f1, s_f2, r_f2, s_jx, r_jx, s_jz, r_jz, s_out,
    s_ez, r_ez, s_ec, r_ec, s_early,
):
    me = Place()
    x, y, z, c = me.x, me.y, me.z, me.c
    sib = me.sibling()
    group = [group_of(rem(z + e, 4)) for e in range(4)]
    half = rows(c * 128, 128)
    mine = rows(x * 64, 64)
    greet(line_partners(me))
    sends = []

    def send(src, dst, ss, rs, device):
        copy = remote(src, dst, ss, rs, device)
        copy.start()
        sends.append(copy)

    def arrived(dst, rs):
        remote(dst, dst, s_c.at[0], rs, sib).wait_recv()

    send(ctx, ca.at[group[0], :, half, :], s_c.at[0], r_c.at[0], sib)
    for d in NEAR:
        send(ctx, ca.at[group[0], :, half, :], s_z.at[d - 1], r_z.at[3 - d], me.to_z(d))
    ca[group[0], :, half, :] = ctx[...]

    def target(e):
        def level(l, carry):
            for j in range(4):
                part = jnp.dot(
                    ca[group[e], l], wt[l, :, j * 256 : (j + 1) * 256], preferred_element_type=F32
                )
                sb[j // 2, e, l, :, (j % 2) * 256 : (j % 2 + 1) * 256] = part.astype(BF16)
            return carry

        lax.fori_loop(0, 3, level, 0)
        for d in NEAR:
            to = rem(x + d, 4)
            send(sb.at[0, e, :, rows(to * 64, 64), :], rx.at[e, 3 - d], s_x.at[e, d - 1], r_x.at[e, 3 - d], me.at(x=to))
        slot = rem(y - group[e] + 4, 4)

        @pl.when(slot != 0)
        def _():
            remote(sb.at[1, e], ry.at[slot - 1], s_y.at[e], r_y.at[slot - 1], me.at(y=group[e])).start()

    def collect_x(e):
        for d in NEAR:
            arrived(rx.at[e, d - 1], r_x.at[e, d - 1])

        def level(l, carry):
            total = sb[0, e, l, mine, :].astype(F32)
            for d in range(3):
                total = total + rx[e, d, l].astype(F32)
            s0[e, l] = total.astype(BF16)
            return carry

        lax.fori_loop(0, 3, level, 0)
        slot = rem(y - group[e] + 4, 4)

        @pl.when(slot != 0)
        def _():
            remote(s0.at[e], r2x.at[slot - 1], s_2x.at[e], r_2x.at[slot - 1], me.at(y=group[e])).start()

    other = rows((1 - c) * 128, 128)
    mv = Mover(me, s_c.at[0])
    begin = GatherG(mv, lambda q, core: ea.at[:, q, rows(core * 128, 128), :], s_ez, r_ez, s_ec, r_ec)

    def context_in(e):
        if e:
            arrived(ca.at[group[e], :, half, :], r_z.at[e - 1])
            send(ca.at[group[e], :, half, :], ca.at[group[e], :, half, :], s_c.at[e], r_c.at[e], sib)
        arrived(ca.at[group[e], :, other, :], r_c.at[e])

    for e in (0, 1, 3):
        context_in(e)
        target(e)
    ea[:, group[0], half, :] = early[...]
    begin.to_sibling(0, early)
    begin.along_z(early)
    collect_x(0)
    context_in(2)
    target(2)
    for e in (1, 3, 2):
        collect_x(e)
    for e in NEAR:
        begin.forward(e)
    own = rem(group_of(y) - z + 4, 4)
    for d in NEAR:
        arrived(ry.at[d - 1], r_y.at[d - 1])

    def fold(i, carry):
        l, part = lax.div(i, jnp.int32(4)), rows(rem(i, 4) * 64, 64)
        total = sb[1, own, l, part, :].astype(F32)
        for d in range(3):
            total = total + ry[d, l, part, :].astype(F32)
        s1[l, part, :] = total.astype(BF16)
        return carry

    lax.fori_loop(0, 12, fold, 0)
    for d in NEAR:
        to = rem(x + d, 4)
        send(s1.at[:, rows(to * 64, 64), :], r2y.at[3 - d], s_2y.at[d - 1], r_2y.at[3 - d], me.at(x=to))
    for d in NEAR:
        arrived(r2x.at[d - 1], r_2x.at[d - 1])

    for e in range(4):
        begin.whole(e)
    early_out = pltpu.make_async_copy(ea, early_all, s_early.at[0])
    early_out.start()

    def finish(h, part, got):
        def level(l, carry):
            total = part(l).astype(F32)
            for d in range(3):
                total = total + got[d, l].astype(F32)
            fa[h, y, l, mine, :] = (resid[l, :, h * 512 : (h + 1) * 512].astype(F32) + total).astype(BF16)
            return carry

        lax.fori_loop(0, 3, level, 0)

    def block(h, q, p):
        return fa.at[h, q, :, rows(p * 64, 64), :]

    def spread_x(h, q, p, ss, rs):
        for d in NEAR:
            send(block(h, q, p), block(h, q, p), ss(d - 1), rs(3 - d), me.to_x(d))

    def spread_y(h, q, p, ss, rs):
        for d in NEAR:
            send(block(h, q, p), block(h, q, p), ss(d - 1), rs(3 - d), me.to_y(d))

    finish(0, lambda l: s0[own, l], r2x)
    spread_x(0, y, x, lambda i: s_f1.at[0, i], lambda i: r_f1.at[0, i])
    spread_y(0, y, x, lambda i: s_f2.at[0, i, 0], lambda i: r_f2.at[0, i, 0])
    for d in NEAR:
        arrived(r2y.at[d - 1], r_2y.at[d - 1])
    finish(1, lambda l: s1[l, mine, :], r2y)
    spread_y(1, y, x, lambda i: s_f1.at[1, i], lambda i: r_f1.at[1, i])
    spread_x(1, y, x, lambda i: s_f2.at[1, i, 0], lambda i: r_f2.at[1, i, 0])
    for e in NEAR:
        p, q = rem(x + e, 4), rem(y + e, 4)
        arrived(block(0, y, p), r_f1.at[0, e - 1])
        spread_y(0, y, p, lambda i: s_f2.at[0, i, e], lambda i: r_f2.at[0, i, e])
        arrived(block(1, q, x), r_f1.at[1, e - 1])
        spread_x(1, q, x, lambda i: s_f2.at[1, i, e], lambda i: r_f2.at[1, i, e])

    def join(e):
        q = rem(y + e, 4)
        if e:
            for p in range(4):
                arrived(block(0, q, rem(x + p, 4)), r_f2.at[0, e - 1, p])
        for p in NEAR:
            arrived(block(1, q, rem(x + p, 4)), r_f2.at[1, p - 1, e])
        for h in range(2):
            pltpu.make_async_copy(fa.at[h, q], feats.at[h, q], s_out.at[h, e]).start()
        for j in range(2):
            columns = slice(j * 256, (j + 1) * 256)
            total = jnp.zeros((256, 256), F32)
            for l in range(3):
                for h in range(2):
                    total = total + jnp.dot(
                        fa[h, q, l], wj[l, h * 512 : (h + 1) * 512, columns], preferred_element_type=F32
                    )
            js[e, :, columns] = total.astype(BF16)
        send(js.at[e, other, :], jx.at[e], s_jx.at[e], r_jx.at[e], sib)

    def pair(e):
        q = rem(y + e, 4)
        arrived(jx.at[e], r_jx.at[e])
        j2[e] = (js[e, half, :].astype(F32) + jx[e].astype(F32)).astype(BF16)
        to = group_of(q)
        slot = rem(z - to + 4, 4)

        @pl.when(slot != 0)
        def _():
            remote(j2.at[e], jz.at[slot - 1], s_jz.at[e], r_jz.at[slot - 1], me.at(z=to)).start()

    join(0)
    join(1)
    pair(0)
    join(3)
    pair(1)
    join(2)
    pair(3)
    pair(2)
    for d in NEAR:
        arrived(jz.at[d - 1], r_jz.at[d - 1])
    kept = rem(group_of(z) - y + 4, 4)
    total = j2[kept].astype(F32)
    for d in range(3):
        total = total + jz[d].astype(F32)
    joined[...] = total

    mv.drain()
    early_out.wait()
    for copy in sends:
        copy.wait_send()
    for e in range(4):

        @pl.when(rem(y - group[e] + 4, 4) != 0)
        def _():
            remote(sb.at[1, e], ry.at[0], s_y.at[e], r_y.at[0], sib).wait_send()
            remote(s0.at[e], r2x.at[0], s_2x.at[e], r_2x.at[0], sib).wait_send()

        @pl.when(group_of(rem(y + e, 4)) != z)
        def _():
            remote(j2.at[e], jz.at[0], s_jz.at[e], r_jz.at[0], sib).wait_send()

        for h in range(2):
            q = rem(y + e, 4)
            pltpu.make_async_copy(fa.at[h, q], feats.at[h, q], s_out.at[h, e]).wait()


def features_call(ctx, resid, wt, wj, early):
    return pl.pallas_call(
        features_kernel,
        name="features",
        out_shape=(
            jax.ShapeDtypeStruct((128, 512), F32),
            jax.ShapeDtypeStruct((2, 4, 3, 256, 512), BF16),
            jax.ShapeDtypeStruct((2, 4, 256, 512), BF16),
        ),
        in_specs=[IN_VMEM] * 5,
        out_specs=(IN_VMEM, ANYWHERE, ANYWHERE),
        scratch_shapes=[
            vmem(4, 3, 256, 512),
            vmem(2, 4, 3, 256, 512),
            vmem(4, 3, 3, 64, 512),
            vmem(3, 3, 256, 512),
            vmem(4, 3, 64, 512),
            vmem(3, 256, 512),
            vmem(3, 3, 64, 512),
            vmem(3, 3, 64, 512),
            vmem(2, 4, 3, 256, 512),
            vmem(4, 256, 512),
            vmem(4, 128, 512),
            vmem(4, 128, 512),
            vmem(3, 128, 512),
            vmem(2, 4, 256, 512),
            dma(3), dma(3), dma(4), dma(4), dma(4, 3), dma(4, 3), dma(4), dma(3),
            dma(4), dma(3), dma(3), dma(3),
            dma(2, 3), dma(2, 3), dma(2, 3, 4), dma(2, 3, 4), dma(4), dma(4), dma(4), dma(3), dma(2, 4),
            dma(3), dma(3), dma(4), dma(4), dma(1),
        ],
        compiler_params=pltpu.CompilerParams(
            collective_id=0, has_side_effects=True, vmem_limit_bytes=VMEM_LIMIT
        ),
        cost_estimate=pl.CostEstimate(flops=6500000000, bytes_accessed=16000000, transcendentals=0),
    )(ctx, resid, wt, wj, early)


def draft_kernel(*refs):
    refs = list(refs)
    joined, early, own_early, wq, wk, wv, wo, gains, mask = take(refs, 9)
    draft, xn_out, gq_out, at_out, jg_out = take(refs, 5)
    xa, xn, rt, qh, gh, kw, vw, kg, kgot, gq, at, jg, pf = take(refs, 13)
    s_loc, s_rt, r_rt, s_kv, r_kv, s_kg, r_kg = take(refs, 7)
    me = Place()
    x, y, z, c, t = me.x, me.y, me.z, me.c, me.t
    mv = Mover(me, s_loc.at[0])
    mine, half = rows(x * 64, 64), rows(c * 128, 128)
    hidden_rows = GatherG(mv, lambda q, core: xa.at[q, rows(core * 128, 128), :], *take(refs, 4))
    grad_rows = GatherG(mv, lambda q, core: jg.at[q, rows(core * 128, 128), :], *take(refs, 4))
    stats = StatsT(mv, *take(refs, 3))
    inner = StatsT(mv, *take(refs, 3))
    back = SumT(mv, *take(refs, 15))
    qkv = SumT(mv, *take(refs, 15))
    hidden = SumG(mv, *take(refs, 8))
    output = SumG(mv, *take(refs, 8))
    ends = GatherT(mv, lambda h, q, p: gq.at[h, q, rows(p * 64, 64), :], *take(refs, 4))
    attends = GatherT(mv, lambda h, q, p: at.at[h, q, rows(p * 64, 64), :], *take(refs, 4))
    assert not refs
    outs = []

    def local_out(src, dst, i):
        copy = pltpu.make_async_copy(src, dst, s_loc.at[1 + i])
        copy.start()
        outs.append(copy)

    plane = [
        me.at(x=rem(x + d % 4, 4), y=rem(y + d // 4, 4)) for d in range(1, 16)
    ]
    line = [me.at(z=rem(z + d % 4, 4), c=rem(c + d // 4, 2)) for d in range(1, 8)]
    greet(plane + line)

    q0 = group_of(z)
    value = joined[...]
    xa[q0, half, :] = value.astype(BF16)
    hidden_rows.to_sibling(0)
    hidden_rows.along_z()
    first = lax.broadcasted_iota(jnp.int32, (8, 128), 0) == 0
    embed_own = own_early[0].astype(F32)
    stats.start(
        jnp.where(
            first,
            lanes(jnp.sum(value * value, -1, keepdims=True)),
            lanes(jnp.sum(embed_own * embed_own, -1, keepdims=True)),
        )
    )

    def back_part(e):
        q = rem(y + e, 4)
        for j in range(4):
            part = nt(early[1, q], wo[j * 256 : (j + 1) * 256, :])
            back.ps[j // 2, e, :, (j % 2) * 256 : (j % 2 + 1) * 256] = part.astype(BF16)
        back.issue(e)

    back_part(2)
    back_part(1)
    for e in NEAR:
        hidden_rows.forward(e)
    sums = stats.total()
    rate = lax.rsqrt(sums / 8192.0 + epsilon)
    rt[2 * q0 + c] = rate
    for d in range(1, 8):
        dz, dc = d % 4, d // 4
        back_at = (4 - dz) % 4 + 4 * dc
        mv.send(rt.at[2 * q0 + c], rt.at[2 * q0 + c], s_rt.at[d], r_rt.at[back_at], line[d - 1])
    back_part(3)
    back_part(0)
    for e in range(4):
        hidden_rows.whole(e)
    for d in range(1, 8):
        there = 2 * group_of(rem(z + d % 4, 4)) + rem(c + d // 4, 2)
        mv.arrived(rt.at[there], r_rt.at[d])
    gain_e = gains[0:1, :].astype(F32)
    gain_j = gains[1:2, :].astype(F32)

    def qkv_part(e):
        q = rem(y + e, 4)
        for i in range(2):
            part = slice(i * 128, (i + 1) * 128)
            rates = rt[2 * q + i]
            xn[0, q, part, :] = (early[0, q, part, :].astype(F32) * column(rates[1:2, :]) * gain_e).astype(BF16)
            xn[1, q, part, :] = (xa[q, part, :].astype(F32) * column(rates[0:1, :]) * gain_j).astype(BF16)

        def both(w, columns):
            return (dot(xn[0, q], w[0, :, columns]) + dot(xn[1, q], w[1, :, columns])).astype(BF16)

        for h, first_column, at_column, width in (
            (0, 0, 0, 256), (0, 256, 256, 256), (0, 512, 512, 128), (1, 640, 0, 128), (1, 768, 128, 256),
        ):
            qkv.ps[h, e, :, at_column : at_column + width] = both(wq, slice(first_column, first_column + width))
        qkv.ps[1, e, :, 384:512] = both(wk, slice(0, 128))
        qkv.ps[1, e, :, 512:640] = both(wv, slice(0, 128))
        qkv.issue(e)
        for i in range(2):
            local_out(xn.at[i, q], xn_out.at[i, q], 2 * e + i)

    for e in (2, 1, 3, 0):
        qkv_part(e)
    for e in (2, 1, 3, 0):
        back.collect_x(e)
    back.fold()
    for e in (2, 1, 3, 0):
        qkv.collect_x(e)
    qkv.fold()
    for h in range(2):
        got = back.finish(h)
        for i in range(4):
            gh[(4 * h + i) * 64 : (4 * h + i + 1) * 64, :] = got[:, i * 128 : (i + 1) * 128]

    got = qkv.finish(1)
    kw[0:64, :] = jnp.zeros((64, 128), BF16)
    vw[0:64, :] = jnp.zeros((64, 128), BF16)
    kw[192:256, :] = got[:, 384:512]
    vw[192:256, :] = got[:, 512:640]
    for i in range(1, 3):
        after = rem(t + i, 16)
        to = me.at(x=rem(after, 4), y=lax.div(after, jnp.int32(4)))
        place = slice(192 - 64 * i, 256 - 64 * i)
        mv.send(kw.at[192:256, :], kw.at[place, :], s_kv.at[0, i - 1], r_kv.at[0, i - 1], to)
        mv.send(vw.at[192:256, :], vw.at[place, :], s_kv.at[1, i - 1], r_kv.at[1, i - 1], to)
    for i in range(3):
        qh[(5 + i) * 64 : (6 + i) * 64, :] = got[:, i * 128 : (i + 1) * 128]
    got = qkv.finish(0)
    for i in range(5):
        qh[i * 64 : (i + 1) * 64, :] = got[:, i * 128 : (i + 1) * 128]
    for i in range(1, 3):
        place = slice(192 - 64 * i, 256 - 64 * i)
        mv.arrived(kw.at[place, :], r_kv.at[0, i - 1])
        mv.arrived(vw.at[place, :], r_kv.at[1, i - 1])

    scale = 128.0**-0.5
    allowed = jnp.concatenate([mask[...]] * 4, axis=0) > 0.5
    for i in range(2):
        part = slice(i * 256, (i + 1) * 256)
        scores = jnp.where(allowed, nt(qh[part, :], kw[...]) * scale, -1e30)
        powers = jnp.exp(scores - jnp.max(scores, -1, keepdims=True))
        probs = powers / jnp.sum(powers, -1, keepdims=True)
        low = probs.astype(BF16)
        attended = dot(low, vw[...]).astype(BF16)
        for j in range(4):
            at[i, y, mine, j * 128 : (j + 1) * 128] = attended[j * 64 : (j + 1) * 64, :]
        value_grad = tn(low, gh[part, :])
        probs_grad = nt(gh[part, :], vw[...])
        score_grad = probs * (probs_grad - jnp.sum(probs_grad * probs, -1, keepdims=True)) * scale
        score_grad = score_grad.astype(BF16)
        query_grad = dot(score_grad, kw[...]).astype(BF16)
        for j in range(4):
            head = 4 * i + j
            h, at_head = (0, head) if head < 5 else (1, head - 5)
            gq[h, y, mine, at_head * 128 : (at_head + 1) * 128] = query_grad[j * 64 : (j + 1) * 64, :]
        key_grad = tn(score_grad, qh[part, :])
        if i == 0:
            kg[0, :, :] = key_grad
            kg[1, :, :] = value_grad
        else:
            kg[0, :, :] = kg[0, :, :] + key_grad
            kg[1, :, :] = kg[1, :, :] + value_grad
    for i in range(1, 3):
        before = rem(t + 16 - i, 16)
        to = me.at(x=rem(before, 4), y=lax.div(before, jnp.int32(4)))
        mv.send(kg.at[:, 192 - 64 * i : 256 - 64 * i, :], kgot.at[i - 1], s_kg.at[i - 1], r_kg.at[i - 1], to)
    ends.start(0)
    for i in range(2):
        mv.arrived(kgot.at[i], r_kg.at[i])
    for i in range(2):
        total = kg[i, 192:256, :] + kgot[0, i] + kgot[1, i]
        gq[1, y, mine, 384 + 128 * i : 512 + 128 * i] = total.astype(BF16)
    ends.start(1)
    ends.forward()
    attends.start(0)
    attends.start(1)

    def hidden_part(e):
        q = ends.group(e)
        for j in range(2):
            columns = slice(j * 256, (j + 1) * 256)
            total = nt(gq[0, q], wq[1, columns, 0:640])
            total = total + nt(gq[1, q, :, 0:384], wq[1, columns, 640:1024])
            total = total + nt(gq[1, q, :, 384:512], wk[1, columns, :])
            total = total + nt(gq[1, q, :, 512:640], wv[1, columns, :])
            hidden.refs[0][e, :, columns] = total.astype(BF16)
        hidden.swap(e)
        for h in range(2):
            local_out(gq.at[h, q], gq_out.at[h, q], 8 + 2 * e + h)

    hidden_part(0)
    hidden_part(1)
    hidden.pair(0)
    attends.forward()
    hidden_part(3)
    hidden.pair(1)
    hidden_part(2)
    hidden.pair(3)
    hidden.pair(2)
    hidden_grad = hidden.total()
    scaled = hidden_grad * gain_j
    value = joined[...]
    inner.start(lanes(jnp.sum(scaled * value, -1, keepdims=True)))
    pf[...] = scaled

    def output_part(e):
        q = attends.group(e)
        for j in range(2):
            columns = slice(j * 256, (j + 1) * 256)
            total = dot(at[0, q], wo[0:512, columns]) + dot(at[1, q], wo[512:1024, columns])
            output.refs[0][e, :, columns] = total.astype(BF16)
        output.swap(e)
        for h in range(2):
            local_out(at.at[h, q], at_out.at[h, q], 16 + 2 * e + h)

    output_part(0)
    output_part(1)
    mean = column((inner.total() / 8192.0)[0:1, :])
    rate = column(rt[2 * q0 + c][0:1, :])
    value = joined[...]
    own_grad = own_early[1].astype(F32) + rate * pf[...] - value * (rate * rate * rate) * mean
    jg[q0, half, :] = own_grad.astype(BF16)
    grad_rows.to_sibling(0)
    grad_rows.along_z()
    output.pair(0)
    output_part(3)
    output.pair(1)
    output_part(2)
    output.pair(3)
    for e in NEAR:
        grad_rows.forward(e)
    output.pair(2)
    draft[...] = (value + output.total()).astype(BF16)
    for e in range(4):
        grad_rows.whole(e)
    local_out(jg, jg_out, 24)
    mv.drain()
    for copy in outs:
        copy.wait()


def draft_call(*args):
    def gather_g():
        return [dma(3), dma(3), dma(4), dma(4)]

    def gather_t():
        return [dma(2, 3), dma(2, 3), dma(2, 3, 4), dma(2, 3, 4)]

    return pl.pallas_call(
        draft_kernel,
        name="draft",
        out_shape=(
            jax.ShapeDtypeStruct((128, 512), BF16),
            jax.ShapeDtypeStruct((2, 4, 256, 512), BF16),
            jax.ShapeDtypeStruct((2, 4, 256, 640), BF16),
            jax.ShapeDtypeStruct((2, 4, 256, 512), BF16),
            jax.ShapeDtypeStruct((4, 256, 512), BF16),
        ),
        in_specs=[IN_VMEM] * 9,
        out_specs=(IN_VMEM, ANYWHERE, ANYWHERE, ANYWHERE, ANYWHERE),
        scratch_shapes=[
            vmem(4, 256, 512),
            vmem(2, 4, 256, 512),
            vmem(8, 8, 128, dtype=F32),
            vmem(512, 128),
            vmem(512, 128),
            vmem(256, 128),
            vmem(256, 128),
            vmem(2, 256, 128, dtype=F32),
            vmem(2, 2, 64, 128, dtype=F32),
            vmem(2, 4, 256, 640),
            vmem(2, 4, 256, 512),
            vmem(4, 256, 512),
            vmem(128, 512, dtype=F32),
            dma(26), dma(8), dma(8), dma(2, 2), dma(2, 2), dma(2), dma(2),
            *gather_g(), *gather_g(), *StatsT.scratch(), *StatsT.scratch(),
            *SumT.scratch(512), *SumT.scratch(640), *SumG.scratch(), *SumG.scratch(),
            *gather_t(), *gather_t(),
        ],
        compiler_params=pltpu.CompilerParams(
            collective_id=1, has_side_effects=True, vmem_limit_bytes=VMEM_LIMIT
        ),
        cost_estimate=pl.CostEstimate(flops=7000000000, bytes_accessed=16000000, transcendentals=0),
    )(*args)


def local(
    context,
    resid_in,
    target_out_w,
    embedded,
    join_w,
    embed_gain,
    joined_gain,
    query_w,
    key_w,
    value_w,
    out_w,
    segment_ids,
    grad_hidden,
):
    early = jnp.stack([embedded, grad_hidden])
    first_query = lax.axis_index("tensor") * 64
    seq_start = first_query // 512 * 512
    segments = jnp.pad(segment_ids.reshape(-1), (192, 0))
    key_segment = lax.dynamic_slice_in_dim(segments, first_query, 256, 0)
    query_segment = lax.dynamic_slice_in_dim(segments, first_query + 192, 64, 0)
    key_pos = first_query - 192 + jnp.arange(256, dtype=jnp.int32)
    query_pos = first_query + jnp.arange(64, dtype=jnp.int32)
    mask = (
        (query_segment[:, None] == key_segment[None, :])
        & (key_pos[None, :] <= query_pos[:, None])
        & (key_pos[None, :] >= seq_start)
    ).astype(F32)
    joined, feats, early_all = features_call(
        context.transpose(1, 0, 2), resid_in.transpose(1, 0, 2), target_out_w, join_w, early
    )
    draft_hidden, inputs, ends, attended, joined_grad = draft_call(
        joined, early_all, early, query_w, key_w, value_w, out_w, jnp.stack([embed_gain, joined_gain]), mask
    )

    def over_tokens(spec, left, right):
        return jnp.einsum(spec, left, right, preferred_element_type=F32).astype(BF16)

    query_grad = jnp.concatenate([ends[0], ends[1, :, :, 0:384]], -1)
    grad_query = over_tokens("hqtk,qtm->hkm", inputs, query_grad)
    grad_key = over_tokens("hqtk,qtm->hkm", inputs, ends[1, :, :, 384:512])
    grad_value = over_tokens("hqtk,qtm->hkm", inputs, ends[1, :, :, 512:640])
    grad_out = over_tokens("hqtk,qtm->hkm", attended, early_all[1]).reshape(out_w.shape)
    grad_join = over_tokens("hqltk,qtm->lhkm", feats, joined_grad).reshape(join_w.shape)
    return (draft_hidden, grad_join, grad_query, grad_key, grad_value, grad_out)


def solution(mesh):
    in_specs = (
        P(("group", "seq"), None, "tensor"),
        P("tensor", None, ("group", "seq")),
        P(None, "tensor", ("group", "seq")),
        P(("group", "seq"), "tensor"),
        P(None, ("group", "seq"), "tensor"),
        P("tensor"),
        P("tensor"),
        P(None, "tensor", ("group", "seq")),
        P(None, "tensor", ("group", "seq")),
        P(None, "tensor", ("group", "seq")),
        P(("group", "seq"), "tensor"),
        P(),
        P(("group", "seq"), "tensor"),
    )
    out_specs = (
        P(("group", "seq"), "tensor"),
        P(None, ("group", "seq"), "tensor"),
        P(None, "tensor", ("group", "seq")),
        P(None, "tensor", ("group", "seq")),
        P(None, "tensor", ("group", "seq")),
        P(("group", "seq"), "tensor"),
    )
    return jax.shard_map(local, mesh=mesh, in_specs=in_specs, out_specs=out_specs, check_vma=False)
```

```python
import jax
import jax.numpy as jnp
from jax import lax
from jax.experimental import pallas as pl
from jax.experimental.pallas import tpu as pltpu
from jax.sharding import PartitionSpec as P

epsilon = 1e-05
F32 = jnp.float32
BF16 = jnp.bfloat16
NEAR = (1, 3, 2)
VMEM_LIMIT = 62 * 2**20


def rem(value, count):
    return lax.rem(value, jnp.int32(count))


def group_of(z):
    return rem(z, 2) * 2 + lax.div(z, jnp.int32(2))


class Place:
    def __init__(self):
        self.t = lax.axis_index("tensor")
        seq = lax.axis_index("seq")
        self.x, self.y = rem(self.t, 4), lax.div(self.t, jnp.int32(4))
        self.z = lax.div(seq, jnp.int32(2)) * 2 + lax.axis_index("group")
        self.c = rem(seq, 2)

    def at(self, x=None, y=None, z=None, c=None):
        x = self.x if x is None else x
        y = self.y if y is None else y
        z = self.z if z is None else z
        c = self.c if c is None else c
        return (rem(z, 2), y * 4 + x, lax.div(z, jnp.int32(2)) * 2 + c)

    def to_x(self, d):
        return self.at(x=rem(self.x + d, 4))

    def to_y(self, d):
        return self.at(y=rem(self.y + d, 4))

    def to_z(self, d):
        return self.at(z=rem(self.z + d, 4))

    def sibling(self):
        return self.at(c=1 - self.c)


def greet(devices):
    barrier = pltpu.get_barrier_semaphore()
    for device in devices:
        pl.semaphore_signal(barrier, inc=1, device_id=device, device_id_type=pl.DeviceIdType.MESH)
    pl.semaphore_wait(barrier, len(devices))


def remote(src, dst, send, recv, device):
    return pltpu.make_async_remote_copy(
        src_ref=src,
        dst_ref=dst,
        send_sem=send,
        recv_sem=recv,
        device_id=device,
        device_id_type=pl.DeviceIdType.MESH,
    )


def rows(first, count):
    return pl.ds(pl.multiple_of(first, count), count)


def vmem(*shape, dtype=BF16):
    return pltpu.VMEM(shape, dtype)


def dma(*shape):
    return pltpu.SemaphoreType.DMA(shape)


IN_VMEM = pl.BlockSpec(memory_space=pltpu.VMEM)
ANYWHERE = pl.BlockSpec(memory_space=pl.ANY)


def nt(a, b):
    return lax.dot_general(a, b, (((1,), (1,)), ((), ())), preferred_element_type=F32)


def tn(a, b):
    return lax.dot_general(a, b, (((0,), (0,)), ((), ())), preferred_element_type=F32)


def dot(a, b):
    return jnp.dot(a, b, preferred_element_type=F32)


class Mover:
    def __init__(self, me, dummy):
        self.me, self.dummy, self.open = me, dummy, {}

    def send(self, src, dst, ss, rs, device, when=None, tag="end"):
        copy = remote(src, dst, ss, rs, device)
        if when is None:
            copy.start()
        else:
            pl.when(when)(copy.start)
        self.open.setdefault(tag, []).append((when, src, ss))

    def arrived(self, dst, rs):
        remote(dst, dst, self.dummy, rs, self.me.sibling()).wait_recv()

    def settle(self, tag):
        for when, src, ss in self.open.pop(tag, []):
            wait = remote(src, src, ss, self.dummy, self.me.sibling()).wait_send
            if when is None:
                wait()
            else:
                pl.when(when)(wait)

    def drain(self):
        for tag in list(self.open):
            self.settle(tag)


class GatherG:
    def __init__(self, mv, tag, block, s_z, r_z, s_c, r_c):
        me = mv.me
        self.mv, self.tag, self.block, self.sems = mv, tag, block, (s_z, r_z, s_c, r_c)
        self.group = [group_of(rem(me.z + e, 4)) for e in range(4)]

    def to_sibling(self, e, src=None):
        me, (_, _, s_c, r_c) = self.mv.me, self.sems
        place = self.block(self.group[e], me.c)
        self.mv.send(place if src is None else src, place, s_c.at[e], r_c.at[e], me.sibling(), tag=self.tag)

    def along_z(self, src=None):
        me, (s_z, r_z, _, _) = self.mv.me, self.sems
        place = self.block(self.group[0], me.c)
        for d in NEAR:
            self.mv.send(place if src is None else src, place, s_z.at[d - 1], r_z.at[3 - d], me.to_z(d), tag=self.tag)

    def forward(self, e):
        me, (_, r_z, _, _) = self.mv.me, self.sems
        self.mv.arrived(self.block(self.group[e], me.c), r_z.at[e - 1])
        self.to_sibling(e)

    def whole(self, e):
        me, (_, _, _, r_c) = self.mv.me, self.sems
        self.mv.arrived(self.block(self.group[e], 1 - me.c), r_c.at[e])


class GatherT:
    def __init__(self, mv, block, s_1, r_1, s_2, r_2):
        self.mv, self.rows_of, self.sems = mv, block, (s_1, r_1, s_2, r_2)

    def block(self, h, a, b, lo=0, count=64):
        me = self.mv.me
        p, q = (a, b) if h == 0 else (b, a)
        return self.rows_of(h, rem(me.y + q, 4), rem(me.x + p, 4), lo, count)

    def move(self, first_axis, h, part, ss, rs, i):
        me, step = self.mv.me, 1 if i % 2 == 0 else 3
        to = me.to_x(step) if first_axis == (h == 0) else me.to_y(step)
        self.mv.send(part, part, ss, rs, to)

    def to_second(self, h, a):
        s_2, r_2 = self.sems[2:]
        for i in range(2):
            self.move(False, h, self.block(h, a, 0), s_2.at[h, a, i], r_2.at[h, a, i], i)

    def start(self, h):
        s_1, r_1 = self.sems[:2]
        for i in range(2):
            self.move(True, h, self.block(h, 0, 0), s_1.at[h, i], r_1.at[h, i], i)
        self.to_second(h, 0)

    def first(self, h):
        s_1, r_1 = self.sems[:2]
        for i, a in ((0, 3), (1, 1)):
            self.mv.arrived(self.block(h, a, 0), r_1.at[h, i])
            self.move(True, h, self.block(h, a, 0, 32 * i, 32), s_1.at[h, 2 + i], r_1.at[h, 2 + i], i)
            self.to_second(h, a)

    def far(self, h):
        for i in range(2):
            self.mv.arrived(self.block(h, 2, 0, 32 * i, 32), self.sems[1].at[h, 2 + i])
        self.to_second(h, 2)

    def relay(self, h, a):
        s_2, r_2 = self.sems[2:]
        for i, b in ((0, 3), (1, 1)):
            self.mv.arrived(self.block(h, a, b), r_2.at[h, a, i])
            self.move(False, h, self.block(h, a, b, 32 * i, 32), s_2.at[h, a, 2 + i], r_2.at[h, a, 2 + i], i)

    def last(self, h, a):
        for i in range(2):
            self.mv.arrived(self.block(h, a, 2, 32 * i, 32), self.sems[3].at[h, a, 2 + i])

    def middle(self):
        for h in range(2):
            self.first(h)
        for h in range(2):
            self.relay(h, 0)
        for h in range(2):
            self.far(h)
        for a in (3, 1):
            for h in range(2):
                self.relay(h, a)

    def end(self):
        for h in range(2):
            self.relay(h, 2)

    def group(self, e):
        if e == 2:
            for a in range(4):
                self.last(0, a)
        self.last(1, e)
        return rem(self.mv.me.y + e, 4)

    @staticmethod
    def scratch():
        return [dma(2, 4), dma(2, 4), dma(2, 4, 4), dma(2, 4, 4)]


class SumG:
    def __init__(self, mv, js, jx, j2, jz, s_x, r_x, s_z, r_z):
        self.mv, self.refs, self.sems = mv, (js, jx, j2, jz), (s_x, r_x, s_z, r_z)

    def swap(self, e):
        (js, jx, _, _), (s_x, r_x, _, _), me = self.refs, self.sems, self.mv.me
        self.mv.send(js.at[e, rows((1 - me.c) * 128, 128), :], jx.at[e], s_x.at[e], r_x.at[e], me.sibling(), tag=self)

    def pair(self, e):
        (js, jx, j2, jz), (_, r_x, s_z, r_z), me = self.refs, self.sems, self.mv.me
        self.mv.arrived(jx.at[e], r_x.at[e])
        j2[e] = (js[e, rows(me.c * 128, 128), :].astype(F32) + jx[e].astype(F32)).astype(BF16)
        to = group_of(rem(me.y + e, 4))
        slot = rem(me.z - to + 4, 4)
        at = jnp.maximum(slot - 1, 0)
        self.mv.send(j2.at[e], jz.at[at], s_z.at[e], r_z.at[at], me.at(z=to), when=slot != 0, tag=self)

    def total(self):
        (_, _, j2, jz), (_, _, _, r_z), me = self.refs, self.sems, self.mv.me
        for d in NEAR:
            self.mv.arrived(jz.at[d - 1], r_z.at[d - 1])
        total = j2[rem(group_of(me.z) - me.y + 4, 4)].astype(F32)
        for d in range(3):
            total = total + jz[d].astype(F32)
        return total

    @staticmethod
    def scratch():
        return [vmem(4, 256, 512), vmem(4, 128, 512), vmem(4, 128, 512), vmem(3, 128, 512), dma(4), dma(4), dma(4), dma(3)]


class SumT:
    def __init__(self, mv, ps, rx, ry, s0, s1, r2x, r2y, *sems):
        self.mv, self.ps, self.rx, self.ry, self.s0, self.s1, self.r2x, self.r2y = mv, ps, rx, ry, s0, s1, r2x, r2y
        self.sems = sems

    def issue(self, e):
        mv, me = self.mv, self.mv.me
        s_x, r_x, s_y, r_y = self.sems[:4]
        for d in NEAR:
            to = rem(me.x + d, 4)
            mv.send(self.ps.at[0, e, rows(to * 64, 64), :], self.rx.at[e, 3 - d], s_x.at[e, d - 1], r_x.at[e, 3 - d], me.at(x=to), tag=self)
        if e:
            mv.send(self.ps.at[1, e], self.ry.at[3 - e], s_y.at[e], r_y.at[3 - e], me.to_y(e), tag=self)

    def collect_x(self, e):
        mv, me = self.mv, self.mv.me
        r_x, s_2x, r_2x = self.sems[1], self.sems[4], self.sems[5]
        for d in NEAR:
            mv.arrived(self.rx.at[e, d - 1], r_x.at[e, d - 1])
        total = self.ps[0, e, rows(me.x * 64, 64), :].astype(F32)
        for d in range(3):
            total = total + self.rx[e, d].astype(F32)
        self.s0[e] = total.astype(BF16)
        if e:
            mv.send(self.s0.at[e], self.r2x.at[3 - e], s_2x.at[e], r_2x.at[3 - e], me.to_y(e))

    def fold(self):
        mv, me = self.mv, self.mv.me
        r_y, s_2y, r_2y = self.sems[3], self.sems[6], self.sems[7]
        for d in NEAR:
            mv.arrived(self.ry.at[d - 1], r_y.at[d - 1])
        for d in (2, 1, 3, 0):
            to = rem(me.x + d, 4)
            part = rows(to * 64, 64)
            total = self.ps[1, 0, part, :].astype(F32)
            for i in range(3):
                total = total + self.ry[i, part, :].astype(F32)
            self.s1[part, :] = total.astype(BF16)
            if d:
                mv.send(self.s1.at[part, :], self.r2y.at[3 - d], s_2y.at[d - 1], r_2y.at[3 - d], me.at(x=to))

    def finish(self, h):
        mv, me = self.mv, self.mv.me
        got, sem = ((self.r2x, self.sems[5]), (self.r2y, self.sems[7]))[h]
        for d in NEAR:
            mv.arrived(got.at[d - 1], sem.at[d - 1])
        total = (self.s0[0] if h == 0 else self.s1[rows(me.x * 64, 64), :]).astype(F32)
        for d in range(3):
            total = total + got[d].astype(F32)
        return total.astype(BF16)

    @staticmethod
    def scratch(w):
        return [
            vmem(4, 3, 64, w), vmem(3, 256, w), vmem(4, 64, w), vmem(256, w), vmem(3, 64, w), vmem(3, 64, w),
            dma(4, 3), dma(4, 3), dma(4), dma(3), dma(4), dma(3), dma(3), dma(3),
        ]


def lanes(column):
    return jnp.broadcast_to(column, (128, 128)).T[0:8, :]


def column(row):
    return jnp.broadcast_to(row, (128, 128)).T[:, 0:1]


class TilesG:
    def __init__(self, mv, line, tiles, s_t, r_t):
        self.mv, self.line, self.tiles, self.s_t, self.r_t = mv, line, tiles, s_t, r_t

    def place(self, e, core):
        me = self.mv.me
        return self.tiles.at[2 * group_of(rem(me.z + e, 4)) + rem(me.c + core, 2)]

    def start(self, tile):
        me = self.mv.me
        self.tiles[2 * group_of(me.z) + me.c] = tile
        for d in range(1, 8):
            back = (4 - d % 4) % 4 + 4 * (d // 4)
            self.mv.send(self.place(0, 0), self.place(0, 0), self.s_t.at[d], self.r_t.at[back], self.line[d - 1])

    def whole(self):
        for d in range(1, 8):
            self.mv.arrived(self.place(d % 4, d // 4), self.r_t.at[d])

    def column(self, q, i):
        return column(self.tiles[2 * q + i][0:1, :])

    @staticmethod
    def scratch():
        return [pltpu.VMEM((8, 8, 128), F32), dma(8), dma(8)]


class StatsT:
    def __init__(self, mv, tiles, s_t, r_t):
        self.mv, self.tiles, self.s_t, self.r_t = mv, tiles, s_t, r_t

    def start(self, tile):
        me = self.mv.me
        self.tiles[0] = tile
        for d in range(1, 16):
            dx, dy = d % 4, d // 4
            back = (4 - dx) % 4 + 4 * ((4 - dy) % 4)
            to = me.at(x=rem(me.x + dx, 4), y=rem(me.y + dy, 4))
            self.mv.send(self.tiles.at[0], self.tiles.at[back], self.s_t.at[d], self.r_t.at[back], to)

    def total(self):
        for d in range(1, 16):
            self.mv.arrived(self.tiles.at[d], self.r_t.at[d])
        total = self.tiles[0]
        for d in range(1, 16):
            total = total + self.tiles[d]
        return total

    @staticmethod
    def scratch():
        return [pltpu.VMEM((16, 8, 128), F32), dma(16), dma(16)]


def take(refs, count):
    out = refs[:count]
    del refs[:count]
    return out


def step_kernel(*refs):
    refs = list(refs)
    ctx, resid, wt, wj, embedded, cotangent, gain_e, gain_j, wq, wk, wv, wo, mask = take(refs, 13)
    draft, join_out, query_out, key_out, value_out, output_out = take(refs, 6)
    ca, sb, rx, ry, s0, s1, r2x, r2y, fa, ea, xa, qh, gh, kw, vw, kg, kgot, gq, at, jg, joined, kvs, qps = take(refs, 23)
    s_loc, s_kv, r_kv, s_kg, r_kg = take(refs, 5)
    s_x, r_x, s_y, r_y, s_2x, r_2x, s_2y, r_2y = take(refs, 8)
    me = Place()
    x, y, z, c, t = me.x, me.y, me.z, me.c, me.t
    mv = Mover(me, s_loc.at[0])
    mine, half = rows(x * 64, 64), rows(c * 128, 128)
    plane = [me.at(x=rem(x + d % 4, 4), y=rem(y + d // 4, 4)) for d in range(1, 16)]
    line = [me.at(z=rem(z + d % 4, 4), c=rem(c + d // 4, 2)) for d in range(1, 8)]
    xn, back_ps, stage = sb.at[:, :, 1], sb.at[:, :, 0], sb.at[:, :, 2]
    context_rows = GatherG(mv, "ctx", lambda q, core: ca.at[q, :, rows(core * 128, 128), :], *take(refs, 4))
    early_rows = GatherG(mv, "end", lambda q, core: ea.at[:, q, rows(core * 128, 128), :], *take(refs, 4))
    hidden_rows = GatherG(mv, "xa", lambda q, core: xa.at[q, rows(core * 128, 128), :], *take(refs, 4))
    grad_rows = GatherG(mv, "end", lambda q, core: jg.at[q, rows(core * 128, 128), :], *take(refs, 4))
    embed_stats, hidden_stats, inner_stats = (StatsT(mv, *take(refs, 3)) for _ in range(3))
    embed_rates, hidden_rates, factors = (TilesG(mv, line, *take(refs, 3)) for _ in range(3))
    back = SumT(mv, back_ps, *take(refs, 14))
    qkv = SumT(mv, qps, *take(refs, 14))
    line_sum = SumG(mv, *take(refs, 8))
    output = SumG(mv, *take(refs, 8))
    feats = GatherT(mv, lambda h, q, p, lo, n: fa.at[h, q, :, pl.ds(pl.multiple_of(p * 64 + lo, 32), n), :], *take(refs, 4))
    ends = GatherT(mv, lambda h, q, p, lo, n: gq.at[h, q, pl.ds(pl.multiple_of(p * 64 + lo, 32), n), :], *take(refs, 4))
    attends = GatherT(mv, lambda h, q, p, lo, n: at.at[h, q, pl.ds(pl.multiple_of(p * 64 + lo, 32), n), :], *take(refs, 4))
    assert not refs
    outs = []

    def local_out(src, dst):
        copy = pltpu.make_async_copy(src, dst, s_loc.at[1 + len(outs)])
        copy.start()
        outs.append(copy)

    greet(plane + line)

    group = context_rows.group
    q0 = group[0]
    context_rows.to_sibling(0, ctx)
    context_rows.along_z(ctx)
    ca[q0, :, half, :] = ctx[...]
    ea[0, q0, half, :] = embedded[...]
    ea[1, q0, half, :] = cotangent[...]
    own_embedded = embedded[...].astype(F32)
    embed_stats.start(lanes(jnp.sum(own_embedded * own_embedded, -1, keepdims=True)))

    def target(e):
        def level(l, carry):
            for j in range(4):
                part = dot(ca[group[e], l], wt[l, :, j * 256 : (j + 1) * 256])
                sb[j // 2, e, l, :, (j % 2) * 256 : (j % 2 + 1) * 256] = part.astype(BF16)
            return carry

        lax.fori_loop(0, 3, level, 0)
        for d in NEAR:
            to = rem(x + d, 4)
            mv.send(
                sb.at[0, e, :, rows(to * 64, 64), :], rx.at[e, 3 - d], s_x.at[e, d - 1], r_x.at[e, 3 - d],
                me.at(x=to), tag="sb",
            )
        slot = rem(y - group[e] + 4, 4)
        to = jnp.maximum(slot - 1, 0)
        mv.send(sb.at[1, e], ry.at[to], s_y.at[e], r_y.at[to], me.at(y=group[e]), when=slot != 0, tag="sb")

    def collect_x(e):
        for d in NEAR:
            mv.arrived(rx.at[e, d - 1], r_x.at[e, d - 1])

        def level(l, carry):
            total = sb[0, e, l, mine, :].astype(F32)
            for d in range(3):
                total = total + rx[e, d, l].astype(F32)
            s0[e, l] = total.astype(BF16)
            return carry

        lax.fori_loop(0, 3, level, 0)
        slot = rem(y - group[e] + 4, 4)
        to = jnp.maximum(slot - 1, 0)
        mv.send(s0.at[e], r2x.at[to], s_2x.at[e], r_2x.at[to], me.at(y=group[e]), when=slot != 0)

    for e in (0, 1, 3):
        if e:
            context_rows.forward(e)
        context_rows.whole(e)
        target(e)
    early_rows.to_sibling(0)
    early_rows.along_z()
    collect_x(0)
    context_rows.forward(2)
    context_rows.whole(2)
    target(2)
    embed_rates.start(lax.rsqrt(embed_stats.total() / 8192.0 + epsilon))
    for e in (1, 3, 2):
        collect_x(e)
    for e in NEAR:
        early_rows.forward(e)
    own = rem(group_of(y) - z + 4, 4)
    for d in NEAR:
        mv.arrived(ry.at[d - 1], r_y.at[d - 1])
    for d in (2, 1, 3, 0):
        to = rem(x + d, 4)
        part = rows(to * 64, 64)

        def fold(l, carry):
            total = sb[1, own, l, part, :].astype(F32)
            for i in range(3):
                total = total + ry[i, l, part, :].astype(F32)
            s1[l, part, :] = total.astype(BF16)
            return carry

        lax.fori_loop(0, 3, fold, 0)
        if d:
            mv.send(s1.at[:, part, :], r2y.at[3 - d], s_2y.at[d - 1], r_2y.at[3 - d], me.at(x=to))

    def finish(h, part, got, sem):
        for d in NEAR:
            mv.arrived(got.at[d - 1], sem.at[d - 1])

        def level(l, carry):
            total = part(l).astype(F32)
            for d in range(3):
                total = total + got[d, l].astype(F32)
            fa[h, y, l, mine, :] = (resid[l, :, h * 512 : (h + 1) * 512].astype(F32) + total).astype(BF16)
            return carry

        lax.fori_loop(0, 3, level, 0)
        feats.start(h)

    finish(0, lambda l: s0[own, l], r2x, r_2x)
    finish(1, lambda l: s1[l, mine, :], r2y, r_2y)

    mv.settle("sb")
    for e in range(4):
        early_rows.whole(e)
    embed_rates.whole()
    scale_e = gain_e[...].astype(F32)
    scale_j = gain_j[...].astype(F32)

    def inputs_part(e, i, source, rates, scales):
        q = rem(y + e, 4)
        for k in range(2):
            part = slice(k * 128, (k + 1) * 128)
            xn[i, q, part, :] = (source(q)[part, :].astype(F32) * rates.column(q, k) * scales).astype(BF16)
        for h, first, there, width in (
            (0, 0, 0, 256), (0, 256, 256, 256), (0, 512, 512, 128), (1, 640, 0, 128), (1, 768, 128, 256), (1, 0, 384, 128), (1, 0, 512, 128),
        ):
            w = (wk if there == 384 else wv) if h == 1 and there >= 384 else wq
            total = dot(xn[i, q], w[i, :, first : first + width])
            if i:
                total = total + qps[h, e, :, there : there + width].astype(F32)
            qps[h, e, :, there : there + width] = total.astype(BF16)

    def embed_part(e):
        inputs_part(e, 0, lambda q: ea[0, q], embed_rates, scale_e)

    def back_part(e):
        q = rem(y + e, 4)
        for j in range(4):
            part = nt(ea[1, q], wo[j * 256 : (j + 1) * 256, :])
            back_ps[j // 2, e, :, (j % 2) * 256 : (j % 2 + 1) * 256] = part.astype(BF16)

    def join(e):
        q = feats.group(e)
        for j in range(2):
            columns = slice(j * 256, (j + 1) * 256)
            total = jnp.zeros((256, 256), F32)
            for l in range(3):
                for h in range(2):
                    total = total + dot(fa[h, q, l], wj[l, h * 512 : (h + 1) * 512, columns])
            line_sum.refs[0][e, :, columns] = total.astype(BF16)
        line_sum.swap(e)

    for h in range(2):
        feats.first(h)
    embed_part(2)
    embed_part(1)
    for h in range(2):
        feats.relay(h, 0)
    for h in range(2):
        feats.far(h)
    embed_part(3)
    embed_part(0)
    for h in range(2):
        feats.relay(h, 3)
    back_part(2)
    back_part(1)
    for h in range(2):
        feats.relay(h, 1)
    back_part(3)
    back_part(0)
    join(0)
    feats.end()
    join(1)
    line_sum.pair(0)
    for e in (2, 1, 3, 0):
        back.issue(e)
    join(3)
    line_sum.pair(1)
    join(2)
    line_sum.pair(3)
    line_sum.pair(2)
    value = line_sum.total()
    joined[...] = value

    xa[q0, half, :] = value.astype(BF16)
    hidden_rows.to_sibling(0)
    hidden_rows.along_z()
    hidden_stats.start(lanes(jnp.sum(value * value, -1, keepdims=True)))
    for e in NEAR:
        hidden_rows.forward(e)
    hidden_rates.start(lax.rsqrt(hidden_stats.total() / 8192.0 + epsilon))
    for e in (2, 1, 3, 0):
        back.collect_x(e)
    for e in range(4):
        hidden_rows.whole(e)
    hidden_rates.whole()
    for e in (2, 1, 3, 0):
        inputs_part(e, 1, lambda q: xa[q], hidden_rates, scale_j)
        qkv.issue(e)
    back.fold()
    for h in range(2):
        got = back.finish(h)
        for i in range(4):
            gh[(4 * h + i) * 64 : (4 * h + i + 1) * 64, :] = got[:, i * 128 : (i + 1) * 128]
    for e in (2, 1, 3, 0):
        qkv.collect_x(e)
    qkv.fold()

    got = qkv.finish(1)
    kw[0:64, :] = jnp.zeros((64, 128), BF16)
    vw[0:64, :] = jnp.zeros((64, 128), BF16)
    kw[192:256, :] = got[:, 384:512]
    vw[192:256, :] = got[:, 512:640]
    for i in range(1, 3):
        after = rem(t + i, 16)
        to = me.at(x=rem(after, 4), y=lax.div(after, jnp.int32(4)))
        place = slice(192 - 64 * i, 256 - 64 * i)
        mv.send(kw.at[192:256, :], kw.at[place, :], s_kv.at[0, i - 1], r_kv.at[0, i - 1], to)
        mv.send(vw.at[192:256, :], vw.at[place, :], s_kv.at[1, i - 1], r_kv.at[1, i - 1], to)
    for i in range(3):
        qh[(5 + i) * 64 : (6 + i) * 64, :] = got[:, i * 128 : (i + 1) * 128]
    got = qkv.finish(0)
    for i in range(5):
        qh[i * 64 : (i + 1) * 64, :] = got[:, i * 128 : (i + 1) * 128]
    for i in range(1, 3):
        place = slice(192 - 64 * i, 256 - 64 * i)
        mv.arrived(kw.at[place, :], r_kv.at[0, i - 1])
        mv.arrived(vw.at[place, :], r_kv.at[1, i - 1])

    scale = 128.0**-0.5
    allowed = jnp.concatenate([mask[...]] * 4, axis=0) > 0.5
    for i in range(2):
        part = slice(i * 256, (i + 1) * 256)
        scores = jnp.where(allowed, nt(qh[part, :], kw[...]) * scale, -1e30)
        powers = jnp.exp(scores - jnp.max(scores, -1, keepdims=True))
        probs = powers / jnp.sum(powers, -1, keepdims=True)
        low = probs.astype(BF16)
        attended = dot(low, vw[...]).astype(BF16)
        for j in range(4):
            at[i, y, mine, j * 128 : (j + 1) * 128] = attended[j * 64 : (j + 1) * 64, :]
        value_grad = tn(low, gh[part, :])
        probs_grad = nt(gh[part, :], vw[...])
        score_grad = probs * (probs_grad - jnp.sum(probs_grad * probs, -1, keepdims=True)) * scale
        score_grad = score_grad.astype(BF16)
        query_grad = dot(score_grad, kw[...]).astype(BF16)
        for j in range(4):
            head = 4 * i + j
            h, at_head = (0, head) if head < 5 else (1, head - 5)
            gq[h, y, mine, at_head * 128 : (at_head + 1) * 128] = query_grad[j * 64 : (j + 1) * 64, :]
        key_grad = tn(score_grad, qh[part, :])
        if i == 0:
            kg[0, :, :] = key_grad
            kg[1, :, :] = value_grad
        else:
            kg[0, :, :] = kg[0, :, :] + key_grad
            kg[1, :, :] = kg[1, :, :] + value_grad
    for i in range(1, 3):
        before = rem(t + 16 - i, 16)
        to = me.at(x=rem(before, 4), y=lax.div(before, jnp.int32(4)))
        mv.send(kg.at[:, 192 - 64 * i : 256 - 64 * i, :], kgot.at[i - 1], s_kg.at[i - 1], r_kg.at[i - 1], to)
    ends.start(0)
    for i in range(2):
        mv.arrived(kgot.at[i], r_kg.at[i])
    for i in range(2):
        total = kg[i, 192:256, :] + kgot[0, i] + kgot[1, i]
        gq[1, y, mine, 384 + 128 * i : 512 + 128 * i] = total.astype(BF16)
    ends.start(1)
    mv.settle(line_sum)
    mv.settle("xa")
    mv.settle("ctx")
    mv.settle(back)
    ends.middle()

    def hidden_part(e):
        q = ends.group(e)
        for j in range(2):
            columns = slice(j * 256, (j + 1) * 256)
            total = nt(gq[0, q], wq[1, columns, 0:640])
            total = total + nt(gq[1, q, :, 0:384], wq[1, columns, 640:1024])
            total = total + nt(gq[1, q, :, 384:512], wk[1, columns, :])
            total = total + nt(gq[1, q, :, 512:640], wv[1, columns, :])
            line_sum.refs[0][e, :, columns] = total.astype(BF16)
        line_sum.swap(e)

    hidden_part(0)
    ends.end()
    attends.start(0)
    attends.start(1)
    hidden_part(1)
    line_sum.pair(0)
    hidden_part(3)
    line_sum.pair(1)
    hidden_part(2)
    line_sum.pair(3)
    line_sum.pair(2)

    def query_weight(h):
        for first in (0, 256, 512, 640, 896):
            width = 128 if first in (512, 896) else 256
            i, there = (0, first) if first < 640 else (1, first - 640)
            total = jnp.zeros((512, width), F32)
            for q in range(4):
                total = total + tn(xn[h, q], gq[i, q, :, there : there + width])
            total = total.astype(BF16)
            place = first % 512
            for k in range(2):
                stage[h, 2 * k + first // 512, :, place : place + width] = total[k * 256 : (k + 1) * 256, :]
        for k in range(4):
            local_out(stage.at[h, k], query_out.at[h, (k // 2) * 256 : (k // 2 + 1) * 256, (k % 2) * 512 : (k % 2 + 1) * 512])

    def key_value_weight(h):
        total = jnp.zeros((512, 256), F32)
        for q in range(4):
            total = total + tn(xn[h, q], gq[1, q, :, 384:640])
        kvs[0, h] = total[:, 0:128].astype(BF16)
        kvs[1, h] = total[:, 128:256].astype(BF16)
        local_out(kvs.at[0, h], key_out.at[h])
        local_out(kvs.at[1, h], value_out.at[h])

    def output_weight(h):
        for j in range(2):
            columns = slice(j * 256, (j + 1) * 256)
            total = jnp.zeros((512, 256), F32)
            for q in range(4):
                total = total + tn(at[h, q], ea[1, q, :, columns])
            total = total.astype(BF16)
            for k in range(2):
                back_ps[h, k, :, columns] = total[k * 256 : (k + 1) * 256, :]
        for k in range(2):
            local_out(back_ps.at[h, k], output_out.at[(2 * h + k) * 256 : (2 * h + k + 1) * 256, :])

    key_value_weight(0)
    key_value_weight(1)
    for h in range(2):
        attends.first(h)
    hidden_grad = line_sum.total()
    scaled = hidden_grad * scale_j
    value = joined[...]
    inner_stats.start(lanes(jnp.sum(scaled * value, -1, keepdims=True)))
    own_rate = hidden_rates.tiles[2 * q0 + c]
    jg[q0, half, :] = (cotangent[...].astype(F32) + column(own_rate[0:1, :]) * scaled).astype(BF16)
    grad_rows.to_sibling(0)
    grad_rows.along_z()
    for h in range(2):
        attends.relay(h, 0)
    for h in range(2):
        attends.far(h)
    query_weight(0)
    mean = inner_stats.total() / 8192.0
    factors.start(own_rate * own_rate * own_rate * mean)
    for a in (3, 1):
        for h in range(2):
            attends.relay(h, a)
    attends.end()

    def output_part(e):
        q = attends.group(e)
        for j in range(2):
            columns = slice(j * 256, (j + 1) * 256)
            total = dot(at[0, q], wo[0:512, columns]) + dot(at[1, q], wo[512:1024, columns])
            output.refs[0][e, :, columns] = total.astype(BF16)
        output.swap(e)

    for e in NEAR:
        grad_rows.forward(e)
    output_part(0)
    output_part(1)
    output.pair(0)
    output_part(3)
    output.pair(1)
    output_part(2)
    output.pair(3)
    output.pair(2)
    query_weight(1)
    for e in range(4):
        grad_rows.whole(e)
    factors.whole()
    for q in range(4):
        for k in range(2):
            part = slice(k * 128, (k + 1) * 128)
            grad = jg[q, part, :].astype(F32) - xa[q, part, :].astype(F32) * factors.column(q, k)
            xa[q, part, :] = grad.astype(BF16)

    def join_weight(l, carry):
        for h in range(2):
            for j in range(2):
                columns = slice(j * 256, (j + 1) * 256)
                total = jnp.zeros((512, 256), F32)
                for q in range(4):
                    total = total + tn(fa[h, q, l], xa[q, :, columns])
                total = total.astype(BF16)
                for k in range(2):
                    ca[2 * h + k, l, :, columns] = total[k * 256 : (k + 1) * 256, :]
        return carry

    lax.fori_loop(0, 3, join_weight, 0)
    for k in range(4):
        local_out(ca.at[k], join_out.at[:, k * 256 : (k + 1) * 256, :])
    output_weight(0)
    output_weight(1)
    draft[...] = (value + output.total()).astype(BF16)
    mv.drain()
    for copy in outs:
        copy.wait()


def step_call(*args):
    def gather_g():
        return [dma(3), dma(3), dma(4), dma(4)]

    shape = jax.ShapeDtypeStruct
    return pl.pallas_call(
        step_kernel,
        name="step",
        out_shape=(
            shape((128, 512), BF16),
            shape((3, 1024, 512), BF16),
            shape((2, 512, 1024), BF16),
            shape((2, 512, 128), BF16),
            shape((2, 512, 128), BF16),
            shape((1024, 512), BF16),
        ),
        in_specs=[IN_VMEM] * 13,
        out_specs=(IN_VMEM, *[ANYWHERE] * 5),
        scratch_shapes=[
            vmem(4, 3, 256, 512),
            vmem(2, 4, 3, 256, 512),
            vmem(4, 3, 3, 64, 512),
            vmem(3, 3, 256, 512),
            vmem(4, 3, 64, 512),
            vmem(3, 256, 512),
            vmem(3, 3, 64, 512),
            vmem(3, 3, 64, 512),
            vmem(2, 4, 3, 256, 512),
            vmem(2, 4, 256, 512),
            vmem(4, 256, 512),
            vmem(512, 128),
            vmem(512, 128),
            vmem(256, 128),
            vmem(256, 128),
            vmem(2, 256, 128, dtype=F32),
            vmem(2, 2, 64, 128, dtype=F32),
            vmem(2, 4, 256, 640),
            vmem(2, 4, 256, 512),
            vmem(4, 256, 512),
            vmem(128, 512, dtype=F32),
            vmem(2, 2, 512, 128),
            vmem(2, 4, 256, 640),
            dma(26), dma(2, 2), dma(2, 2), dma(2), dma(2),
            dma(4, 3), dma(4, 3), dma(4), dma(3), dma(4), dma(3), dma(3), dma(3),
            *gather_g(), *gather_g(), *gather_g(), *gather_g(),
            *StatsT.scratch(), *StatsT.scratch(), *StatsT.scratch(),
            *TilesG.scratch(), *TilesG.scratch(), *TilesG.scratch(),
            *SumT.scratch(512), *SumT.scratch(640), *SumG.scratch(), *SumG.scratch(),
            *GatherT.scratch(), *GatherT.scratch(), *GatherT.scratch(),
        ],
        compiler_params=pltpu.CompilerParams(
            collective_id=0, has_side_effects=True, vmem_limit_bytes=VMEM_LIMIT
        ),
        cost_estimate=pl.CostEstimate(flops=20000000000, bytes_accessed=24000000, transcendentals=0),
    )(*args)


def local(
    context,
    resid_in,
    target_out_w,
    embedded,
    join_w,
    embed_gain,
    joined_gain,
    query_w,
    key_w,
    value_w,
    out_w,
    segment_ids,
    grad_hidden,
):
    first_query = lax.axis_index("tensor") * 64
    seq_start = first_query // 512 * 512
    segments = jnp.pad(segment_ids.reshape(-1), (192, 0))
    key_segment = lax.dynamic_slice_in_dim(segments, first_query, 256, 0)
    query_segment = lax.dynamic_slice_in_dim(segments, first_query + 192, 64, 0)
    key_pos = first_query - 192 + jnp.arange(256, dtype=jnp.int32)
    query_pos = first_query + jnp.arange(64, dtype=jnp.int32)
    mask = (
        (query_segment[:, None] == key_segment[None, :])
        & (key_pos[None, :] <= query_pos[:, None])
        & (key_pos[None, :] >= seq_start)
    ).astype(F32)
    return step_call(
        context.transpose(1, 0, 2),
        resid_in.transpose(1, 0, 2),
        target_out_w,
        join_w,
        embedded,
        grad_hidden,
        embed_gain.reshape(1, -1),
        joined_gain.reshape(1, -1),
        query_w,
        key_w,
        value_w,
        out_w,
        mask,
    )


def solution(mesh):
    in_specs = (
        P(("group", "seq"), None, "tensor"),
        P("tensor", None, ("group", "seq")),
        P(None, "tensor", ("group", "seq")),
        P(("group", "seq"), "tensor"),
        P(None, ("group", "seq"), "tensor"),
        P("tensor"),
        P("tensor"),
        P(None, "tensor", ("group", "seq")),
        P(None, "tensor", ("group", "seq")),
        P(None, "tensor", ("group", "seq")),
        P(("group", "seq"), "tensor"),
        P(),
        P(("group", "seq"), "tensor"),
    )
    out_specs = (
        P(("group", "seq"), "tensor"),
        P(None, ("group", "seq"), "tensor"),
        P(None, "tensor", ("group", "seq")),
        P(None, "tensor", ("group", "seq")),
        P(None, "tensor", ("group", "seq")),
        P(("group", "seq"), "tensor"),
    )
    return jax.shard_map(local, mesh=mesh, in_specs=in_specs, out_specs=out_specs, check_vma=False)
```

```python
import jax
import jax.numpy as jnp
from jax import lax
from jax.experimental import pallas as pl
from jax.experimental.pallas import tpu as pltpu
from jax.sharding import PartitionSpec as P

epsilon = 1e-05
F32 = jnp.float32
BF16 = jnp.bfloat16
NEAR = (1, 3, 2)
VMEM_LIMIT = 62 * 2**20


def rem(value, count):
    return lax.rem(value, jnp.int32(count))


def group_of(z):
    return rem(z, 2) * 2 + lax.div(z, jnp.int32(2))


class Place:
    def __init__(self):
        self.t = lax.axis_index("tensor")
        seq = lax.axis_index("seq")
        self.x, self.y = rem(self.t, 4), lax.div(self.t, jnp.int32(4))
        self.z = lax.div(seq, jnp.int32(2)) * 2 + lax.axis_index("group")
        self.c = rem(seq, 2)

    def at(self, x=None, y=None, z=None, c=None):
        x = self.x if x is None else x
        y = self.y if y is None else y
        z = self.z if z is None else z
        c = self.c if c is None else c
        return (rem(z, 2), y * 4 + x, lax.div(z, jnp.int32(2)) * 2 + c)

    def to_x(self, d):
        return self.at(x=rem(self.x + d, 4))

    def to_y(self, d):
        return self.at(y=rem(self.y + d, 4))

    def to_z(self, d):
        return self.at(z=rem(self.z + d, 4))

    def sibling(self):
        return self.at(c=1 - self.c)


def greet(devices):
    barrier = pltpu.get_barrier_semaphore()
    for device in devices:
        pl.semaphore_signal(barrier, inc=1, device_id=device, device_id_type=pl.DeviceIdType.MESH)
    pl.semaphore_wait(barrier, len(devices))


def remote(src, dst, send, recv, device):
    return pltpu.make_async_remote_copy(
        src_ref=src,
        dst_ref=dst,
        send_sem=send,
        recv_sem=recv,
        device_id=device,
        device_id_type=pl.DeviceIdType.MESH,
    )


def rows(first, count):
    return pl.ds(pl.multiple_of(first, count), count)


def vmem(*shape, dtype=BF16):
    return pltpu.VMEM(shape, dtype)


def dma(*shape):
    return pltpu.SemaphoreType.DMA(shape)


IN_VMEM = pl.BlockSpec(memory_space=pltpu.VMEM)
ANYWHERE = pl.BlockSpec(memory_space=pl.ANY)


def nt(a, b):
    return lax.dot_general(a, b, (((1,), (1,)), ((), ())), preferred_element_type=F32)


def tn(a, b):
    return lax.dot_general(a, b, (((0,), (0,)), ((), ())), preferred_element_type=F32)


def dot(a, b):
    return jnp.dot(a, b, preferred_element_type=F32)


class Mover:
    def __init__(self, me, dummy):
        self.me, self.dummy, self.open = me, dummy, {}

    def send(self, src, dst, ss, rs, device, when=None, tag="end"):
        copy = remote(src, dst, ss, rs, device)
        if when is None:
            copy.start()
        else:
            pl.when(when)(copy.start)
        self.open.setdefault(tag, []).append((when, src, ss))

    def arrived(self, dst, rs):
        remote(dst, dst, self.dummy, rs, self.me.sibling()).wait_recv()

    def settle(self, tag):
        for when, src, ss in self.open.pop(tag, []):
            wait = remote(src, src, ss, self.dummy, self.me.sibling()).wait_send
            if when is None:
                wait()
            else:
                pl.when(when)(wait)

    def drain(self):
        for tag in list(self.open):
            self.settle(tag)


class GatherG:
    def __init__(self, mv, tag, block, s_z, r_z, s_c, r_c):
        me = mv.me
        self.mv, self.tag, self.block, self.sems = mv, tag, block, (s_z, r_z, s_c, r_c)
        self.group = [group_of(rem(me.z + e, 4)) for e in range(4)]

    def to_sibling(self, e, src=None):
        me, (_, _, s_c, r_c) = self.mv.me, self.sems
        place = self.block(self.group[e], me.c)
        self.mv.send(place if src is None else src, place, s_c.at[e], r_c.at[e], me.sibling(), tag=self.tag)

    def along_z(self, src=None):
        me, (s_z, r_z, _, _) = self.mv.me, self.sems
        place = self.block(self.group[0], me.c)
        for d in NEAR:
            self.mv.send(place if src is None else src, place, s_z.at[d - 1], r_z.at[3 - d], me.to_z(d), tag=self.tag)

    def forward(self, e):
        me, (_, r_z, _, _) = self.mv.me, self.sems
        self.mv.arrived(self.block(self.group[e], me.c), r_z.at[e - 1])
        self.to_sibling(e)

    def whole(self, e):
        me, (_, _, _, r_c) = self.mv.me, self.sems
        self.mv.arrived(self.block(self.group[e], 1 - me.c), r_c.at[e])


class GatherT:
    def __init__(self, mv, block, s_1, r_1, s_2, r_2):
        self.mv, self.rows_of, self.sems = mv, block, (s_1, r_1, s_2, r_2)

    def block(self, h, a, b, lo=0, count=64):
        me = self.mv.me
        p, q = (a, b) if h == 0 else (b, a)
        return self.rows_of(h, rem(me.y + q, 4), rem(me.x + p, 4), lo, count)

    def move(self, first_axis, h, part, ss, rs, i):
        me, step = self.mv.me, 1 if i % 2 == 0 else 3
        to = me.to_x(step) if first_axis == (h == 0) else me.to_y(step)
        self.mv.send(part, part, ss, rs, to)

    def to_second(self, h, a):
        s_2, r_2 = self.sems[2:]
        for i in range(2):
            self.move(False, h, self.block(h, a, 0), s_2.at[h, a, i], r_2.at[h, a, i], i)

    def start(self, h):
        s_1, r_1 = self.sems[:2]
        for i in range(2):
            self.move(True, h, self.block(h, 0, 0), s_1.at[h, i], r_1.at[h, i], i)
        self.to_second(h, 0)

    def first(self, h):
        s_1, r_1 = self.sems[:2]
        for i, a in ((0, 3), (1, 1)):
            self.mv.arrived(self.block(h, a, 0), r_1.at[h, i])
            self.move(True, h, self.block(h, a, 0, 32 * i, 32), s_1.at[h, 2 + i], r_1.at[h, 2 + i], i)
            self.to_second(h, a)

    def far(self, h):
        for i in range(2):
            self.mv.arrived(self.block(h, 2, 0, 32 * i, 32), self.sems[1].at[h, 2 + i])
        self.to_second(h, 2)

    def relay(self, h, a):
        s_2, r_2 = self.sems[2:]
        for i, b in ((0, 3), (1, 1)):
            self.mv.arrived(self.block(h, a, b), r_2.at[h, a, i])
            self.move(False, h, self.block(h, a, b, 32 * i, 32), s_2.at[h, a, 2 + i], r_2.at[h, a, 2 + i], i)

    def last(self, h, a):
        for i in range(2):
            self.mv.arrived(self.block(h, a, 2, 32 * i, 32), self.sems[3].at[h, a, 2 + i])

    def middle(self):
        for h in range(2):
            self.first(h)
        for h in range(2):
            self.relay(h, 0)
        for h in range(2):
            self.far(h)
        for a in (3, 1):
            for h in range(2):
                self.relay(h, a)

    def end(self):
        for h in range(2):
            self.relay(h, 2)

    def group(self, e):
        if e == 2:
            for a in range(4):
                self.last(0, a)
        self.last(1, e)
        return rem(self.mv.me.y + e, 4)

    @staticmethod
    def scratch():
        return [dma(2, 4), dma(2, 4), dma(2, 4, 4), dma(2, 4, 4)]


class SumG:
    def __init__(self, mv, js, jx, j2, jz, s_x, r_x, s_z, r_z):
        self.mv, self.refs, self.sems = mv, (js, jx, j2, jz), (s_x, r_x, s_z, r_z)

    def swap(self, e):
        (js, jx, _, _), (s_x, r_x, _, _), me = self.refs, self.sems, self.mv.me
        self.mv.send(js.at[e, rows((1 - me.c) * 128, 128), :], jx.at[e], s_x.at[e], r_x.at[e], me.sibling(), tag=self)

    def pair(self, e):
        (js, jx, j2, jz), (_, r_x, s_z, r_z), me = self.refs, self.sems, self.mv.me
        self.mv.arrived(jx.at[e], r_x.at[e])
        j2[e] = (js[e, rows(me.c * 128, 128), :].astype(F32) + jx[e].astype(F32)).astype(BF16)
        to = group_of(rem(me.y + e, 4))
        slot = rem(me.z - to + 4, 4)
        at = jnp.maximum(slot - 1, 0)
        self.mv.send(j2.at[e], jz.at[at], s_z.at[e], r_z.at[at], me.at(z=to), when=slot != 0, tag=self)

    def total(self):
        (_, _, j2, jz), (_, _, _, r_z), me = self.refs, self.sems, self.mv.me
        for d in NEAR:
            self.mv.arrived(jz.at[d - 1], r_z.at[d - 1])
        total = j2[rem(group_of(me.z) - me.y + 4, 4)].astype(F32)
        for d in range(3):
            total = total + jz[d].astype(F32)
        return total

    @staticmethod
    def scratch():
        return [vmem(4, 256, 512), vmem(4, 128, 512), vmem(4, 128, 512), vmem(3, 128, 512), dma(4), dma(4), dma(4), dma(3)]


class SumT:
    def __init__(self, mv, ps, hx, rx, hy, ry, s0, s1, r2x, r2y, *sems):
        self.mv, self.ps, self.hx, self.rx, self.hy, self.ry = mv, ps, hx, rx, hy, ry
        self.s0, self.s1, self.r2x, self.r2y = s0, s1, r2x, r2y
        self.sems = sems

    def issue(self, e):
        mv, me = self.mv, self.mv.me
        s_hx, r_hx, _, _, s_hy, r_hy = self.sems[:6]
        opposite = rem(me.x + 2, 4) * 64
        for i, step in enumerate((1, 3)):
            part = self.ps.at[0, e, rows(opposite + 32 * i, 32), :]
            mv.send(part, self.hx.at[e, i], s_hx.at[e, i], r_hx.at[e, i], me.to_x(step), tag=self)
            if e == 2:
                part = self.ps.at[1, 2, 128 * i : 128 * i + 128, :]
                mv.send(part, self.hy.at[i], s_hy.at[i], r_hy.at[i], me.to_y(step), tag=self)

    def second(self, e):
        mv, me = self.mv, self.mv.me
        _, r_hx, s_x, r_x, _, r_hy, s_y, r_y = self.sems[:8]
        for i, step in enumerate((1, 3)):
            if e == step:
                mv.arrived(self.hy.at[i], r_hy.at[i])
                part = slice(128 * i, 128 * i + 128)
                self.ps[1, e, part, :] = (self.ps[1, e, part, :].astype(F32) + self.hy[i].astype(F32)).astype(BF16)
                mv.send(self.ps.at[1, e], self.ry.at[i], s_y.at[i], r_y.at[i], me.to_y(step), tag=self)
        for i, step in enumerate((1, 3)):
            to = rem(me.x + step, 4) * 64
            mv.arrived(self.hx.at[e, i], r_hx.at[e, i])
            part = rows(to + 32 * i, 32)
            self.ps[0, e, part, :] = (self.ps[0, e, part, :].astype(F32) + self.hx[e, i].astype(F32)).astype(BF16)
            mv.send(self.ps.at[0, e, rows(to, 64), :], self.rx.at[e, i], s_x.at[e, i], r_x.at[e, i], me.to_x(step), tag=self)

    def collect_x(self, e):
        mv, me = self.mv, self.mv.me
        r_x, s_2x, r_2x = self.sems[3], self.sems[8], self.sems[9]
        total = self.ps[0, e, rows(me.x * 64, 64), :].astype(F32)
        for i in range(2):
            mv.arrived(self.rx.at[e, i], r_x.at[e, i])
            total = total + self.rx[e, i].astype(F32)
        self.s0[e] = total.astype(BF16)
        if e:
            mv.send(self.s0.at[e], self.r2x.at[3 - e], s_2x.at[e], r_2x.at[3 - e], me.to_y(e), tag=self)

    def fold(self):
        mv, me = self.mv, self.mv.me
        r_y, s_2y, r_2y = self.sems[7], self.sems[10], self.sems[11]
        for i in range(2):
            mv.arrived(self.ry.at[i], r_y.at[i])
        for d in (2, 1, 3, 0):
            to = rem(me.x + d, 4)
            part = rows(to * 64, 64)
            total = self.ps[1, 0, part, :].astype(F32)
            for i in range(2):
                total = total + self.ry[i, part, :].astype(F32)
            self.s1[part, :] = total.astype(BF16)
            if d:
                mv.send(self.s1.at[part, :], self.r2y.at[3 - d], s_2y.at[d - 1], r_2y.at[3 - d], me.at(x=to), tag=self)

    def finish(self, h):
        mv, me = self.mv, self.mv.me
        got, sem = ((self.r2x, self.sems[9]), (self.r2y, self.sems[11]))[h]
        for d in NEAR:
            mv.arrived(got.at[d - 1], sem.at[d - 1])
        total = (self.s0[0] if h == 0 else self.s1[rows(me.x * 64, 64), :]).astype(F32)
        for d in range(3):
            total = total + got[d].astype(F32)
        return total

    @staticmethod
    def scratch(w):
        return [
            vmem(4, 2, 32, w), vmem(4, 2, 64, w), vmem(2, 128, w), vmem(2, 256, w),
            vmem(4, 64, w), vmem(256, w), vmem(3, 64, w), vmem(3, 64, w),
            dma(4, 2), dma(4, 2), dma(4, 2), dma(4, 2), dma(2), dma(2), dma(2), dma(2), dma(4), dma(3), dma(3), dma(3),
        ]


def lanes(column):
    return jnp.broadcast_to(column, (128, 128)).T[0:8, :]


def column(row):
    return jnp.broadcast_to(row, (128, 128)).T[:, 0:1]


class TilesG:
    def __init__(self, mv, line, tiles, s_t, r_t):
        self.mv, self.line, self.tiles, self.s_t, self.r_t = mv, line, tiles, s_t, r_t

    def place(self, e, core):
        me = self.mv.me
        return self.tiles.at[2 * group_of(rem(me.z + e, 4)) + rem(me.c + core, 2)]

    def start(self, tile):
        me = self.mv.me
        self.tiles[2 * group_of(me.z) + me.c] = tile
        for d in range(1, 8):
            back = (4 - d % 4) % 4 + 4 * (d // 4)
            self.mv.send(self.place(0, 0), self.place(0, 0), self.s_t.at[d], self.r_t.at[back], self.line[d - 1])

    def whole(self):
        for d in range(1, 8):
            self.mv.arrived(self.place(d % 4, d // 4), self.r_t.at[d])

    def column(self, q, i):
        return column(self.tiles[2 * q + i][0:1, :])

    @staticmethod
    def scratch():
        return [pltpu.VMEM((8, 8, 128), F32), dma(8), dma(8)]


class StatsT:
    def __init__(self, mv, tiles, s_t, r_t):
        self.mv, self.tiles, self.s_t, self.r_t = mv, tiles, s_t, r_t

    def start(self, tile):
        me = self.mv.me
        self.tiles[0] = tile
        for d in range(1, 16):
            dx, dy = d % 4, d // 4
            back = (4 - dx) % 4 + 4 * ((4 - dy) % 4)
            to = me.at(x=rem(me.x + dx, 4), y=rem(me.y + dy, 4))
            self.mv.send(self.tiles.at[0], self.tiles.at[back], self.s_t.at[d], self.r_t.at[back], to)

    def total(self):
        for d in range(1, 16):
            self.mv.arrived(self.tiles.at[d], self.r_t.at[d])
        total = self.tiles[0]
        for d in range(1, 16):
            total = total + self.tiles[d]
        return total

    @staticmethod
    def scratch():
        return [pltpu.VMEM((16, 8, 128), F32), dma(16), dma(16)]


def take(refs, count):
    out = refs[:count]
    del refs[:count]
    return out


def step_kernel(*refs):
    refs = list(refs)
    ctx, resid, embedded, cotangent, gains, mask = take(refs, 6)
    weights = take(refs, 6)
    draft, join_out, query_out, key_out, value_out, output_out = take(refs, 6)
    wt, wj, wq, wk, wv, wo = held = take(refs, 6)
    ca, sb, fa, ea, xa, qh, gh, kw, vw, kg, kgot, gq, at, jg, joined, kvs, qps, sums = take(refs, 18)
    s_loc, s_kv, r_kv, s_kg, r_kg, s_w = take(refs, 6)
    me = Place()
    x, y, z, c, t = me.x, me.y, me.z, me.c, me.t
    mv = Mover(me, s_loc.at[0])
    mine, half = rows(x * 64, 64), rows(c * 128, 128)
    plane = [me.at(x=rem(x + d % 4, 4), y=rem(y + d // 4, 4)) for d in range(1, 16)]
    line = [me.at(z=rem(z + d % 4, 4), c=rem(c + d // 4, 2)) for d in range(1, 8)]
    xn, back_ps, stage = sb.at[:, :, 1], sb.at[:, :, 0], sb.at[:, :, 2]
    context_rows = [
        GatherG(mv, "ctx", lambda q, core, l=l: ca.at[q, l, rows(core * 128, 128), :], *take(refs, 4)) for l in range(3)
    ]
    levels = [SumT(mv, sb.at[:, :, l], *take(refs, 20)) for l in range(3)]
    early_rows = GatherG(mv, "end", lambda q, core: ea.at[:, q, rows(core * 128, 128), :], *take(refs, 4))
    hidden_rows = GatherG(mv, "xa", lambda q, core: xa.at[q, rows(core * 128, 128), :], *take(refs, 4))
    grad_rows = GatherG(mv, "end", lambda q, core: jg.at[q, rows(core * 128, 128), :], *take(refs, 4))
    embed_stats, hidden_stats, inner_stats = (StatsT(mv, *take(refs, 3)) for _ in range(3))
    embed_rates, hidden_rates, factors = (TilesG(mv, line, *take(refs, 3)) for _ in range(3))
    back = SumT(mv, back_ps, *take(refs, 20))
    qkv = SumT(mv, qps, *take(refs, 20))
    line_sum = SumG(mv, *take(refs, 8))
    output = SumG(mv, *take(refs, 8))
    feats = [
        GatherT(mv, lambda h, q, p, lo, n, l=l: fa.at[h, q, l, pl.ds(pl.multiple_of(p * 64 + lo, 32), n), :], *take(refs, 4))
        for l in range(3)
    ]
    ends = GatherT(mv, lambda h, q, p, lo, n: gq.at[h, q, pl.ds(pl.multiple_of(p * 64 + lo, 32), n), :], *take(refs, 4))
    attends = GatherT(mv, lambda h, q, p, lo, n: at.at[h, q, pl.ds(pl.multiple_of(p * 64 + lo, 32), n), :], *take(refs, 4))
    assert not refs
    outs = []

    def local_out(src, dst):
        copy = pltpu.make_async_copy(src, dst, s_loc.at[1 + len(outs)])
        copy.start()
        outs.append(copy)

    loads = [pltpu.make_async_copy(src, dst, s_w.at[i]) for i, (src, dst) in enumerate(zip(weights, held))]
    for load in loads:
        load.start()
    greet(plane + line)

    q0 = group_of(z)

    def context_out(l):
        context_rows[l].to_sibling(0, ctx.at[l])
        context_rows[l].along_z(ctx.at[l])

    context_out(0)
    context_out(1)
    ca[q0, :, half, :] = ctx[...]
    ea[0, q0, half, :] = embedded[...]
    ea[1, q0, half, :] = cotangent[...]
    own_embedded = embedded[...].astype(F32)
    embed_stats.start(lanes(jnp.sum(own_embedded * own_embedded, -1, keepdims=True)))

    def context_in(l):
        for e in NEAR:
            context_rows[l].forward(e)
        for e in range(4):
            context_rows[l].whole(e)

    def target(l):
        for e in (2, 1, 3, 0):
            q = rem(y + e, 4)
            for j in range(4):
                part = dot(ca[q, l], wt[l, :, j * 256 : (j + 1) * 256])
                sb[j // 2, e, l, :, (j % 2) * 256 : (j % 2 + 1) * 256] = part.astype(BF16)
            levels[l].issue(e)

    def second(l):
        for e in (1, 3, 2, 0):
            levels[l].second(e)

    def collect(l):
        for e in (2, 1, 3, 0):
            levels[l].collect_x(e)
        levels[l].fold()

    def finish(l):
        for h in range(2):
            total = levels[l].finish(h)
            fa[h, y, l, mine, :] = (resid[l, :, h * 512 : (h + 1) * 512].astype(F32) + total).astype(BF16)
            feats[l].start(h)

    def both(step, *args):
        for h in range(2):
            step(h, *args)

    loads[0].wait()
    context_in(0)
    context_out(2)
    target(0)
    context_in(1)
    early_rows.to_sibling(0)
    early_rows.along_z()
    target(1)
    second(0)
    context_in(2)
    target(2)
    second(1)
    embed_rates.start(lax.rsqrt(embed_stats.total() / 8192.0 + epsilon))
    collect(0)
    second(2)
    for e in NEAR:
        early_rows.forward(e)
    finish(0)
    collect(1)
    both(feats[0].first)
    finish(1)
    both(feats[0].relay, 0)
    collect(2)
    both(feats[0].far)
    both(feats[1].first)
    finish(2)

    for e in range(4):
        early_rows.whole(e)
    embed_rates.whole()
    scale_e = gains[0:1, :].astype(F32)
    scale_j = gains[1:2, :].astype(F32)
    for l in range(3):
        mv.settle(levels[l])
    for load in loads[1:]:
        load.wait()

    def inputs_part(e, i, source, rates, scales):
        q = rem(y + e, 4)
        for k in range(2):
            part = slice(k * 128, (k + 1) * 128)
            xn[i, q, part, :] = (source(q)[part, :].astype(F32) * rates.column(q, k) * scales).astype(BF16)
        for h, first, there, width in (
            (0, 0, 0, 256), (0, 256, 256, 256), (0, 512, 512, 128), (1, 640, 0, 128), (1, 768, 128, 256), (1, 0, 384, 128), (1, 0, 512, 128),
        ):
            w = (wk if there == 384 else wv) if h == 1 and there >= 384 else wq
            total = dot(xn[i, q], w[i, :, first : first + width])
            if i:
                total = total + qps[h, e, :, there : there + width].astype(F32)
            qps[h, e, :, there : there + width] = total.astype(BF16)

    def embed_part(e):
        inputs_part(e, 0, lambda q: ea[0, q], embed_rates, scale_e)

    def back_part(e):
        q = rem(y + e, 4)
        for j in range(4):
            part = nt(ea[1, q], wo[j * 256 : (j + 1) * 256, :])
            back_ps[j // 2, e, :, (j % 2) * 256 : (j % 2 + 1) * 256] = part.astype(BF16)

    def join(l, e):
        q = feats[l].group(e)
        for j in range(2):
            columns = slice(j * 256, (j + 1) * 256)
            total = dot(fa[0, q, l], wj[l, 0:512, columns]) + dot(fa[1, q, l], wj[l, 512:1024, columns])
            if l:
                total = total + sums[e, :, columns]
            if l < 2:
                sums[e, :, columns] = total
            else:
                line_sum.refs[0][e, :, columns] = total.astype(BF16)
        if l == 2:
            line_sum.swap(e)

    both(feats[0].relay, 3)
    both(feats[0].relay, 1)
    embed_part(2)
    both(feats[1].relay, 0)
    both(feats[0].relay, 2)
    both(feats[1].far)
    both(feats[2].first)
    embed_part(1)
    both(feats[1].relay, 3)
    both(feats[1].relay, 1)
    both(feats[2].relay, 0)
    embed_part(3)
    both(feats[1].relay, 2)
    both(feats[2].far)
    embed_part(0)
    for e in (0, 1, 3, 2):
        join(0, e)
    both(feats[2].relay, 3)
    both(feats[2].relay, 1)
    for e in (2, 1, 3, 0):
        back_part(e)
    join(1, 0)
    join(1, 1)
    both(feats[2].relay, 2)
    join(1, 3)
    join(1, 2)
    join(2, 0)
    for e in (2, 1, 3, 0):
        back.issue(e)
    join(2, 1)
    line_sum.pair(0)
    join(2, 3)
    line_sum.pair(1)
    join(2, 2)
    line_sum.pair(3)
    line_sum.pair(2)
    value = line_sum.total()
    joined[...] = value

    xa[q0, half, :] = value.astype(BF16)
    hidden_rows.to_sibling(0)
    hidden_rows.along_z()
    hidden_stats.start(lanes(jnp.sum(value * value, -1, keepdims=True)))
    for e in (1, 3, 2, 0):
        back.second(e)
    for e in NEAR:
        hidden_rows.forward(e)
    hidden_rates.start(lax.rsqrt(hidden_stats.total() / 8192.0 + epsilon))
    for e in (2, 1, 3, 0):
        back.collect_x(e)
    for e in range(4):
        hidden_rows.whole(e)
    hidden_rates.whole()
    for e in (2, 1, 3, 0):
        inputs_part(e, 1, lambda q: xa[q], hidden_rates, scale_j)
        qkv.issue(e)
    back.fold()
    for e in (1, 3, 2, 0):
        qkv.second(e)
    for h in range(2):
        got = back.finish(h).astype(BF16)
        for i in range(4):
            gh[(4 * h + i) * 64 : (4 * h + i + 1) * 64, :] = got[:, i * 128 : (i + 1) * 128]
    for e in (2, 1, 3, 0):
        qkv.collect_x(e)
    qkv.fold()

    got = qkv.finish(1).astype(BF16)
    kw[0:64, :] = jnp.zeros((64, 128), BF16)
    vw[0:64, :] = jnp.zeros((64, 128), BF16)
    kw[192:256, :] = got[:, 384:512]
    vw[192:256, :] = got[:, 512:640]
    for i in range(1, 3):
        after = rem(t + i, 16)
        to = me.at(x=rem(after, 4), y=lax.div(after, jnp.int32(4)))
        place = slice(192 - 64 * i, 256 - 64 * i)
        mv.send(kw.at[192:256, :], kw.at[place, :], s_kv.at[0, i - 1], r_kv.at[0, i - 1], to)
        mv.send(vw.at[192:256, :], vw.at[place, :], s_kv.at[1, i - 1], r_kv.at[1, i - 1], to)
    for i in range(3):
        qh[(5 + i) * 64 : (6 + i) * 64, :] = got[:, i * 128 : (i + 1) * 128]
    got = qkv.finish(0).astype(BF16)
    for i in range(5):
        qh[i * 64 : (i + 1) * 64, :] = got[:, i * 128 : (i + 1) * 128]
    for i in range(1, 3):
        place = slice(192 - 64 * i, 256 - 64 * i)
        mv.arrived(kw.at[place, :], r_kv.at[0, i - 1])
        mv.arrived(vw.at[place, :], r_kv.at[1, i - 1])

    scale = 128.0**-0.5
    allowed = jnp.concatenate([mask[...]] * 4, axis=0) > 0.5
    for i in range(2):
        part = slice(i * 256, (i + 1) * 256)
        scores = jnp.where(allowed, nt(qh[part, :], kw[...]) * scale, -1e30)
        powers = jnp.exp(scores - jnp.max(scores, -1, keepdims=True))
        probs = powers / jnp.sum(powers, -1, keepdims=True)
        low = probs.astype(BF16)
        attended = dot(low, vw[...]).astype(BF16)
        for j in range(4):
            at[i, y, mine, j * 128 : (j + 1) * 128] = attended[j * 64 : (j + 1) * 64, :]
        value_grad = tn(low, gh[part, :])
        probs_grad = nt(gh[part, :], vw[...])
        score_grad = probs * (probs_grad - jnp.sum(probs_grad * probs, -1, keepdims=True)) * scale
        score_grad = score_grad.astype(BF16)
        query_grad = dot(score_grad, kw[...]).astype(BF16)
        for j in range(4):
            head = 4 * i + j
            h, at_head = (0, head) if head < 5 else (1, head - 5)
            gq[h, y, mine, at_head * 128 : (at_head + 1) * 128] = query_grad[j * 64 : (j + 1) * 64, :]
        key_grad = tn(score_grad, qh[part, :])
        if i == 0:
            kg[0, :, :] = key_grad
            kg[1, :, :] = value_grad
        else:
            kg[0, :, :] = kg[0, :, :] + key_grad
            kg[1, :, :] = kg[1, :, :] + value_grad
    for i in range(1, 3):
        before = rem(t + 16 - i, 16)
        to = me.at(x=rem(before, 4), y=lax.div(before, jnp.int32(4)))
        mv.send(kg.at[:, 192 - 64 * i : 256 - 64 * i, :], kgot.at[i - 1], s_kg.at[i - 1], r_kg.at[i - 1], to)
    ends.start(0)
    for i in range(2):
        mv.arrived(kgot.at[i], r_kg.at[i])
    for i in range(2):
        total = kg[i, 192:256, :] + kgot[0, i] + kgot[1, i]
        gq[1, y, mine, 384 + 128 * i : 512 + 128 * i] = total.astype(BF16)
    ends.start(1)
    mv.settle(line_sum)
    mv.settle("xa")
    mv.settle("ctx")
    mv.settle(back)
    ends.middle()

    def hidden_part(e):
        q = ends.group(e)
        for j in range(2):
            columns = slice(j * 256, (j + 1) * 256)
            total = nt(gq[0, q], wq[1, columns, 0:640])
            total = total + nt(gq[1, q, :, 0:384], wq[1, columns, 640:1024])
            total = total + nt(gq[1, q, :, 384:512], wk[1, columns, :])
            total = total + nt(gq[1, q, :, 512:640], wv[1, columns, :])
            line_sum.refs[0][e, :, columns] = total.astype(BF16)
        line_sum.swap(e)

    hidden_part(0)
    ends.end()
    attends.start(0)
    attends.start(1)
    hidden_part(1)
    line_sum.pair(0)
    hidden_part(3)
    line_sum.pair(1)
    hidden_part(2)
    line_sum.pair(3)
    line_sum.pair(2)

    def query_weight(h):
        for first in (0, 256, 512, 640, 896):
            width = 128 if first in (512, 896) else 256
            i, there = (0, first) if first < 640 else (1, first - 640)
            total = jnp.zeros((512, width), F32)
            for q in range(4):
                total = total + tn(xn[h, q], gq[i, q, :, there : there + width])
            total = total.astype(BF16)
            place = first % 512
            for k in range(2):
                stage[h, 2 * k + first // 512, :, place : place + width] = total[k * 256 : (k + 1) * 256, :]
        for k in range(4):
            local_out(stage.at[h, k], query_out.at[h, (k // 2) * 256 : (k // 2 + 1) * 256, (k % 2) * 512 : (k % 2 + 1) * 512])

    def key_value_weight(h):
        total = jnp.zeros((512, 256), F32)
        for q in range(4):
            total = total + tn(xn[h, q], gq[1, q, :, 384:640])
        kvs[0, h] = total[:, 0:128].astype(BF16)
        kvs[1, h] = total[:, 128:256].astype(BF16)
        local_out(kvs.at[0, h], key_out.at[h])
        local_out(kvs.at[1, h], value_out.at[h])

    def output_weight(h):
        for j in range(2):
            columns = slice(j * 256, (j + 1) * 256)
            total = jnp.zeros((512, 256), F32)
            for q in range(4):
                total = total + tn(at[h, q], ea[1, q, :, columns])
            total = total.astype(BF16)
            for k in range(2):
                back_ps[h, k, :, columns] = total[k * 256 : (k + 1) * 256, :]
        for k in range(2):
            local_out(back_ps.at[h, k], output_out.at[(2 * h + k) * 256 : (2 * h + k + 1) * 256, :])

    key_value_weight(0)
    key_value_weight(1)
    for h in range(2):
        attends.first(h)
    hidden_grad = line_sum.total()
    scaled = hidden_grad * scale_j
    value = joined[...]
    inner_stats.start(lanes(jnp.sum(scaled * value, -1, keepdims=True)))
    own_rate = hidden_rates.tiles[2 * q0 + c]
    jg[q0, half, :] = (cotangent[...].astype(F32) + column(own_rate[0:1, :]) * scaled).astype(BF16)
    grad_rows.to_sibling(0)
    grad_rows.along_z()
    for h in range(2):
        attends.relay(h, 0)
    for h in range(2):
        attends.far(h)
    query_weight(0)
    mean = inner_stats.total() / 8192.0
    factors.start(own_rate * own_rate * own_rate * mean)
    for a in (3, 1):
        for h in range(2):
            attends.relay(h, a)
    attends.end()

    def output_part(e):
        q = attends.group(e)
        for j in range(2):
            columns = slice(j * 256, (j + 1) * 256)
            total = dot(at[0, q], wo[0:512, columns]) + dot(at[1, q], wo[512:1024, columns])
            output.refs[0][e, :, columns] = total.astype(BF16)
        output.swap(e)

    for e in NEAR:
        grad_rows.forward(e)
    output_part(0)
    output_part(1)
    output.pair(0)
    output_part(3)
    output.pair(1)
    output_part(2)
    output.pair(3)
    output.pair(2)
    query_weight(1)
    for e in range(4):
        grad_rows.whole(e)
    factors.whole()
    for q in range(4):
        for k in range(2):
            part = slice(k * 128, (k + 1) * 128)
            grad = jg[q, part, :].astype(F32) - xa[q, part, :].astype(F32) * factors.column(q, k)
            xa[q, part, :] = grad.astype(BF16)

    def join_weight(l, carry):
        for h in range(2):
            for j in range(2):
                columns = slice(j * 256, (j + 1) * 256)
                total = jnp.zeros((512, 256), F32)
                for q in range(4):
                    total = total + tn(fa[h, q, l], xa[q, :, columns])
                total = total.astype(BF16)
                for k in range(2):
                    ca[2 * h + k, l, :, columns] = total[k * 256 : (k + 1) * 256, :]
        return carry

    lax.fori_loop(0, 3, join_weight, 0)
    for k in range(4):
        local_out(ca.at[k], join_out.at[:, k * 256 : (k + 1) * 256, :])
    output_weight(0)
    output_weight(1)
    draft[...] = (value + output.total()).astype(BF16)
    mv.drain()
    for copy in outs:
        copy.wait()


def step_call(*args):
    def gather_g():
        return [dma(3), dma(3), dma(4), dma(4)]

    shape = jax.ShapeDtypeStruct
    return pl.pallas_call(
        step_kernel,
        name="step",
        out_shape=(
            shape((128, 512), BF16),
            shape((3, 1024, 512), BF16),
            shape((2, 512, 1024), BF16),
            shape((2, 512, 128), BF16),
            shape((2, 512, 128), BF16),
            shape((1024, 512), BF16),
        ),
        in_specs=[IN_VMEM] * 6 + [ANYWHERE] * 6,
        out_specs=(IN_VMEM, *[ANYWHERE] * 5),
        scratch_shapes=[
            vmem(3, 512, 1024),
            vmem(3, 1024, 512),
            vmem(2, 512, 1024),
            vmem(2, 512, 128),
            vmem(2, 512, 128),
            vmem(1024, 512),
            vmem(4, 3, 256, 512),
            vmem(2, 4, 3, 256, 512),
            vmem(2, 4, 3, 256, 512),
            vmem(2, 4, 256, 512),
            vmem(4, 256, 512),
            vmem(512, 128),
            vmem(512, 128),
            vmem(256, 128),
            vmem(256, 128),
            vmem(2, 256, 128, dtype=F32),
            vmem(2, 2, 64, 128, dtype=F32),
            vmem(2, 4, 256, 640),
            vmem(2, 4, 256, 512),
            vmem(4, 256, 512),
            vmem(128, 512, dtype=F32),
            vmem(2, 2, 512, 128),
            vmem(2, 4, 256, 640),
            vmem(4, 256, 512, dtype=F32),
            dma(26), dma(2, 2), dma(2, 2), dma(2), dma(2), dma(6),
            *gather_g(), *gather_g(), *gather_g(),
            *SumT.scratch(512), *SumT.scratch(512), *SumT.scratch(512),
            *gather_g(), *gather_g(), *gather_g(),
            *StatsT.scratch(), *StatsT.scratch(), *StatsT.scratch(),
            *TilesG.scratch(), *TilesG.scratch(), *TilesG.scratch(),
            *SumT.scratch(512), *SumT.scratch(640), *SumG.scratch(), *SumG.scratch(),
            *GatherT.scratch(), *GatherT.scratch(), *GatherT.scratch(), *GatherT.scratch(), *GatherT.scratch(),
        ],
        compiler_params=pltpu.CompilerParams(
            collective_id=0, has_side_effects=True, vmem_limit_bytes=VMEM_LIMIT
        ),
        cost_estimate=pl.CostEstimate(flops=20000000000, bytes_accessed=24000000, transcendentals=0),
    )(*args)


def local(
    context,
    resid_in,
    target_out_w,
    embedded,
    join_w,
    embed_gain,
    joined_gain,
    query_w,
    key_w,
    value_w,
    out_w,
    segment_ids,
    grad_hidden,
):
    first_query = lax.axis_index("tensor") * 64
    seq_start = first_query // 512 * 512
    segments = jnp.pad(segment_ids.reshape(-1), (192, 0))
    key_segment = lax.dynamic_slice_in_dim(segments, first_query, 256, 0)
    query_segment = lax.dynamic_slice_in_dim(segments, first_query + 192, 64, 0)
    key_pos = first_query - 192 + jnp.arange(256, dtype=jnp.int32)
    query_pos = first_query + jnp.arange(64, dtype=jnp.int32)
    mask = (
        (query_segment[:, None] == key_segment[None, :])
        & (key_pos[None, :] <= query_pos[:, None])
        & (key_pos[None, :] >= seq_start)
    ).astype(F32)
    return step_call(
        context.transpose(1, 0, 2),
        resid_in.transpose(1, 0, 2),
        embedded,
        grad_hidden,
        jnp.stack([embed_gain, joined_gain]),
        mask,
        target_out_w,
        join_w,
        query_w,
        key_w,
        value_w,
        out_w,
    )


def solution(mesh):
    in_specs = (
        P(("group", "seq"), None, "tensor"),
        P("tensor", None, ("group", "seq")),
        P(None, "tensor", ("group", "seq")),
        P(("group", "seq"), "tensor"),
        P(None, ("group", "seq"), "tensor"),
        P("tensor"),
        P("tensor"),
        P(None, "tensor", ("group", "seq")),
        P(None, "tensor", ("group", "seq")),
        P(None, "tensor", ("group", "seq")),
        P(("group", "seq"), "tensor"),
        P(),
        P(("group", "seq"), "tensor"),
    )
    out_specs = (
        P(("group", "seq"), "tensor"),
        P(None, ("group", "seq"), "tensor"),
        P(None, "tensor", ("group", "seq")),
        P(None, "tensor", ("group", "seq")),
        P(None, "tensor", ("group", "seq")),
        P(("group", "seq"), "tensor"),
    )
    return jax.shard_map(local, mesh=mesh, in_specs=in_specs, out_specs=out_specs, check_vma=False)
```

```python
import jax
import jax.numpy as jnp
from jax import lax
from jax.experimental import pallas as pl
from jax.experimental.pallas import tpu as pltpu
from jax.sharding import PartitionSpec as P

epsilon = 1e-05
F32 = jnp.float32
BF16 = jnp.bfloat16
NEAR = (1, 3, 2)
VMEM_LIMIT = 62 * 2**20


def rem(value, count):
    return lax.rem(value, jnp.int32(count))


def group_of(z):
    return rem(z, 2) * 2 + lax.div(z, jnp.int32(2))


class Place:
    def __init__(self):
        self.t = lax.axis_index("tensor")
        seq = lax.axis_index("seq")
        self.x, self.y = rem(self.t, 4), lax.div(self.t, jnp.int32(4))
        self.z = lax.div(seq, jnp.int32(2)) * 2 + lax.axis_index("group")
        self.c = rem(seq, 2)

    def at(self, x=None, y=None, z=None, c=None):
        x = self.x if x is None else x
        y = self.y if y is None else y
        z = self.z if z is None else z
        c = self.c if c is None else c
        return (rem(z, 2), y * 4 + x, lax.div(z, jnp.int32(2)) * 2 + c)

    def to_x(self, d):
        return self.at(x=rem(self.x + d, 4))

    def to_y(self, d):
        return self.at(y=rem(self.y + d, 4))

    def to_z(self, d):
        return self.at(z=rem(self.z + d, 4))

    def sibling(self):
        return self.at(c=1 - self.c)


def greet(devices):
    barrier = pltpu.get_barrier_semaphore()
    for device in devices:
        pl.semaphore_signal(barrier, inc=1, device_id=device, device_id_type=pl.DeviceIdType.MESH)
    pl.semaphore_wait(barrier, len(devices))


def remote(src, dst, send, recv, device):
    return pltpu.make_async_remote_copy(
        src_ref=src,
        dst_ref=dst,
        send_sem=send,
        recv_sem=recv,
        device_id=device,
        device_id_type=pl.DeviceIdType.MESH,
    )


def rows(first, count):
    return pl.ds(pl.multiple_of(first, count), count)


def vmem(*shape, dtype=BF16):
    return pltpu.VMEM(shape, dtype)


def dma(*shape):
    return pltpu.SemaphoreType.DMA(shape)


IN_VMEM = pl.BlockSpec(memory_space=pltpu.VMEM)
ANYWHERE = pl.BlockSpec(memory_space=pl.ANY)


def nt(a, b):
    return lax.dot_general(a, b, (((1,), (1,)), ((), ())), preferred_element_type=F32)


def tn(a, b):
    return lax.dot_general(a, b, (((0,), (0,)), ((), ())), preferred_element_type=F32)


def dot(a, b):
    return jnp.dot(a, b, preferred_element_type=F32)


class Mover:
    def __init__(self, me, dummy):
        self.me, self.dummy, self.open = me, dummy, {}

    def send(self, src, dst, ss, rs, device, when=None, tag="end"):
        copy = remote(src, dst, ss, rs, device)
        if when is None:
            copy.start()
        else:
            pl.when(when)(copy.start)
        self.open.setdefault(tag, []).append((when, src, ss))

    def arrived(self, dst, rs):
        remote(dst, dst, self.dummy, rs, self.me.sibling()).wait_recv()

    def settle(self, tag):
        for when, src, ss in self.open.pop(tag, []):
            wait = remote(src, src, ss, self.dummy, self.me.sibling()).wait_send
            if when is None:
                wait()
            else:
                pl.when(when)(wait)

    def drain(self):
        for tag in list(self.open):
            self.settle(tag)


class GatherG:
    def __init__(self, mv, tag, block, s_z, r_z, s_c, r_c):
        me = mv.me
        self.mv, self.tag, self.block, self.sems = mv, tag, block, (s_z, r_z, s_c, r_c)
        self.group = [group_of(rem(me.z + e, 4)) for e in range(4)]

    def to_sibling(self, e, src=None):
        me, (_, _, s_c, r_c) = self.mv.me, self.sems
        place = self.block(self.group[e], me.c)
        self.mv.send(place if src is None else src, place, s_c.at[e], r_c.at[e], me.sibling(), tag=self.tag)

    def along_z(self, src=None):
        me, (s_z, r_z, _, _) = self.mv.me, self.sems
        place = self.block(self.group[0], me.c)
        for d in NEAR:
            self.mv.send(place if src is None else src, place, s_z.at[d - 1], r_z.at[3 - d], me.to_z(d), tag=self.tag)

    def forward(self, e):
        me, (_, r_z, _, _) = self.mv.me, self.sems
        self.mv.arrived(self.block(self.group[e], me.c), r_z.at[e - 1])
        self.to_sibling(e)

    def whole(self, e):
        me, (_, _, _, r_c) = self.mv.me, self.sems
        self.mv.arrived(self.block(self.group[e], 1 - me.c), r_c.at[e])


class GatherT:
    def __init__(self, mv, block, s_1, r_1, s_2, r_2):
        self.mv, self.rows_of, self.sems = mv, block, (s_1, r_1, s_2, r_2)

    def block(self, h, a, b, lo=0, count=64):
        me = self.mv.me
        p, q = (a, b) if h == 0 else (b, a)
        return self.rows_of(h, rem(me.y + q, 4), rem(me.x + p, 4), lo, count)

    def move(self, first_axis, h, part, ss, rs, i):
        me, step = self.mv.me, 1 if i % 2 == 0 else 3
        to = me.to_x(step) if first_axis == (h == 0) else me.to_y(step)
        self.mv.send(part, part, ss, rs, to)

    def to_second(self, h, a):
        s_2, r_2 = self.sems[2:]
        for i in range(2):
            self.move(False, h, self.block(h, a, 0), s_2.at[h, a, i], r_2.at[h, a, i], i)

    def start(self, h):
        s_1, r_1 = self.sems[:2]
        for i in range(2):
            self.move(True, h, self.block(h, 0, 0), s_1.at[h, i], r_1.at[h, i], i)
        self.to_second(h, 0)

    def first(self, h):
        s_1, r_1 = self.sems[:2]
        for i, a in ((0, 3), (1, 1)):
            self.mv.arrived(self.block(h, a, 0), r_1.at[h, i])
            self.move(True, h, self.block(h, a, 0, 32 * i, 32), s_1.at[h, 2 + i], r_1.at[h, 2 + i], i)
            self.to_second(h, a)

    def far(self, h):
        for i in range(2):
            self.mv.arrived(self.block(h, 2, 0, 32 * i, 32), self.sems[1].at[h, 2 + i])
        self.to_second(h, 2)

    def relay(self, h, a):
        s_2, r_2 = self.sems[2:]
        for i, b in ((0, 3), (1, 1)):
            self.mv.arrived(self.block(h, a, b), r_2.at[h, a, i])
            self.move(False, h, self.block(h, a, b, 32 * i, 32), s_2.at[h, a, 2 + i], r_2.at[h, a, 2 + i], i)

    def last(self, h, a):
        for i in range(2):
            self.mv.arrived(self.block(h, a, 2, 32 * i, 32), self.sems[3].at[h, a, 2 + i])

    def middle(self):
        for h in range(2):
            self.first(h)
        for h in range(2):
            self.relay(h, 0)
        for h in range(2):
            self.far(h)
        for a in (3, 1):
            for h in range(2):
                self.relay(h, a)

    def end(self):
        for h in range(2):
            self.relay(h, 2)

    def group(self, e):
        if e == 2:
            for a in range(4):
                self.last(0, a)
        self.last(1, e)
        return rem(self.mv.me.y + e, 4)

    @staticmethod
    def scratch():
        return [dma(2, 4), dma(2, 4), dma(2, 4, 4), dma(2, 4, 4)]


class SumG:
    def __init__(self, mv, js, jx, j2, jz, s_x, r_x, s_z, r_z):
        self.mv, self.refs, self.sems = mv, (js, jx, j2, jz), (s_x, r_x, s_z, r_z)

    def swap(self, e):
        (js, jx, _, _), (s_x, r_x, _, _), me = self.refs, self.sems, self.mv.me
        self.mv.send(js.at[e, rows((1 - me.c) * 128, 128), :], jx.at[e], s_x.at[e], r_x.at[e], me.sibling(), tag=self)

    def pair(self, e):
        (js, jx, j2, jz), (_, r_x, s_z, r_z), me = self.refs, self.sems, self.mv.me
        self.mv.arrived(jx.at[e], r_x.at[e])
        j2[e] = (js[e, rows(me.c * 128, 128), :].astype(F32) + jx[e].astype(F32)).astype(BF16)
        to = group_of(rem(me.y + e, 4))
        slot = rem(me.z - to + 4, 4)
        at = jnp.maximum(slot - 1, 0)
        self.mv.send(j2.at[e], jz.at[at], s_z.at[e], r_z.at[at], me.at(z=to), when=slot != 0, tag=self)

    def total(self):
        (_, _, j2, jz), (_, _, _, r_z), me = self.refs, self.sems, self.mv.me
        for d in NEAR:
            self.mv.arrived(jz.at[d - 1], r_z.at[d - 1])
        total = j2[rem(group_of(me.z) - me.y + 4, 4)].astype(F32)
        for d in range(3):
            total = total + jz[d].astype(F32)
        return total

    @staticmethod
    def scratch():
        return [vmem(4, 256, 512), vmem(4, 128, 512), vmem(4, 128, 512), vmem(3, 128, 512), dma(4), dma(4), dma(4), dma(3)]


class SumT:
    def __init__(self, mv, ps, hx, rx, hy, ry, s0, s1, r2x, r2y, *sems):
        self.mv, self.ps, self.hx, self.rx, self.hy, self.ry = mv, ps, hx, rx, hy, ry
        self.s0, self.s1, self.r2x, self.r2y = s0, s1, r2x, r2y
        self.sems = sems

    def issue(self, e):
        mv, me = self.mv, self.mv.me
        s_hx, r_hx, _, _, s_hy, r_hy = self.sems[:6]
        opposite = rem(me.x + 2, 4) * 64
        for i, step in enumerate((1, 3)):
            part = self.ps.at[0, e, rows(opposite + 32 * i, 32), :]
            mv.send(part, self.hx.at[e, i], s_hx.at[e, i], r_hx.at[e, i], me.to_x(step), tag=self)
            if e == 2:
                part = self.ps.at[1, 2, 128 * i : 128 * i + 128, :]
                mv.send(part, self.hy.at[i], s_hy.at[i], r_hy.at[i], me.to_y(step), tag=self)

    def second(self, e):
        mv, me = self.mv, self.mv.me
        _, r_hx, s_x, r_x, _, r_hy, s_y, r_y = self.sems[:8]
        for i, step in enumerate((1, 3)):
            if e == step:
                mv.arrived(self.hy.at[i], r_hy.at[i])
                part = slice(128 * i, 128 * i + 128)
                self.ps[1, e, part, :] = (self.ps[1, e, part, :].astype(F32) + self.hy[i].astype(F32)).astype(BF16)
                mv.send(self.ps.at[1, e], self.ry.at[i], s_y.at[i], r_y.at[i], me.to_y(step), tag=self)
        for i, step in enumerate((1, 3)):
            to = rem(me.x + step, 4) * 64
            mv.arrived(self.hx.at[e, i], r_hx.at[e, i])
            part = rows(to + 32 * i, 32)
            self.ps[0, e, part, :] = (self.ps[0, e, part, :].astype(F32) + self.hx[e, i].astype(F32)).astype(BF16)
            mv.send(self.ps.at[0, e, rows(to, 64), :], self.rx.at[e, i], s_x.at[e, i], r_x.at[e, i], me.to_x(step), tag=self)

    def collect_x(self, e):
        mv, me = self.mv, self.mv.me
        r_x, s_2x, r_2x = self.sems[3], self.sems[8], self.sems[9]
        total = self.ps[0, e, rows(me.x * 64, 64), :].astype(F32)
        for i in range(2):
            mv.arrived(self.rx.at[e, i], r_x.at[e, i])
            total = total + self.rx[e, i].astype(F32)
        self.s0[e] = total.astype(BF16)
        if e:
            mv.send(self.s0.at[e], self.r2x.at[3 - e], s_2x.at[e], r_2x.at[3 - e], me.to_y(e), tag=self)

    def fold(self):
        mv, me = self.mv, self.mv.me
        r_y, s_2y, r_2y = self.sems[7], self.sems[10], self.sems[11]
        for i in range(2):
            mv.arrived(self.ry.at[i], r_y.at[i])
        for d in (2, 1, 3, 0):
            to = rem(me.x + d, 4)
            part = rows(to * 64, 64)
            total = self.ps[1, 0, part, :].astype(F32)
            for i in range(2):
                total = total + self.ry[i, part, :].astype(F32)
            self.s1[part, :] = total.astype(BF16)
            if d:
                mv.send(self.s1.at[part, :], self.r2y.at[3 - d], s_2y.at[d - 1], r_2y.at[3 - d], me.at(x=to), tag=self)

    def finish(self, h):
        mv, me = self.mv, self.mv.me
        got, sem = ((self.r2x, self.sems[9]), (self.r2y, self.sems[11]))[h]
        for d in NEAR:
            mv.arrived(got.at[d - 1], sem.at[d - 1])
        total = (self.s0[0] if h == 0 else self.s1[rows(me.x * 64, 64), :]).astype(F32)
        for d in range(3):
            total = total + got[d].astype(F32)
        return total

    @staticmethod
    def scratch(w):
        return [
            vmem(4, 2, 32, w), vmem(4, 2, 64, w), vmem(2, 128, w), vmem(2, 256, w),
            vmem(4, 64, w), vmem(256, w), vmem(3, 64, w), vmem(3, 64, w),
            dma(4, 2), dma(4, 2), dma(4, 2), dma(4, 2), dma(2), dma(2), dma(2), dma(2), dma(4), dma(3), dma(3), dma(3),
        ]


def lanes(column):
    return jnp.broadcast_to(column, (128, 128)).T[0:8, :]


def column(row):
    return jnp.broadcast_to(row, (128, 128)).T[:, 0:1]


class TilesG:
    def __init__(self, mv, line, tiles, s_t, r_t):
        self.mv, self.line, self.tiles, self.s_t, self.r_t = mv, line, tiles, s_t, r_t

    def place(self, e, core):
        me = self.mv.me
        return self.tiles.at[2 * group_of(rem(me.z + e, 4)) + rem(me.c + core, 2)]

    def start(self, tile):
        me = self.mv.me
        self.tiles[2 * group_of(me.z) + me.c] = tile
        for d in range(1, 8):
            back = (4 - d % 4) % 4 + 4 * (d // 4)
            self.mv.send(self.place(0, 0), self.place(0, 0), self.s_t.at[d], self.r_t.at[back], self.line[d - 1])

    def whole(self):
        for d in range(1, 8):
            self.mv.arrived(self.place(d % 4, d // 4), self.r_t.at[d])

    def column(self, q, i):
        return column(self.tiles[2 * q + i][0:1, :])

    @staticmethod
    def scratch():
        return [pltpu.VMEM((8, 8, 128), F32), dma(8), dma(8)]


class StatsT:
    def __init__(self, mv, tiles, s_t, r_t):
        self.mv, self.tiles, self.s_t, self.r_t = mv, tiles, s_t, r_t

    def start(self, tile):
        me = self.mv.me
        self.tiles[0] = tile
        for d in range(1, 16):
            dx, dy = d % 4, d // 4
            back = (4 - dx) % 4 + 4 * ((4 - dy) % 4)
            to = me.at(x=rem(me.x + dx, 4), y=rem(me.y + dy, 4))
            self.mv.send(self.tiles.at[0], self.tiles.at[back], self.s_t.at[d], self.r_t.at[back], to)

    def total(self):
        for d in range(1, 16):
            self.mv.arrived(self.tiles.at[d], self.r_t.at[d])
        total = self.tiles[0]
        for d in range(1, 16):
            total = total + self.tiles[d]
        return total

    @staticmethod
    def scratch():
        return [pltpu.VMEM((16, 8, 128), F32), dma(16), dma(16)]


def take(refs, count):
    out = refs[:count]
    del refs[:count]
    return out


def attention_mask(segments, t):
    ids = segments[...].astype(F32)
    own = jnp.where(t < 8, ids[0:1, :], ids[1:2, :])
    padded = jnp.concatenate([jnp.full((1, 256), -1.0, F32), own], axis=1)
    window = padded[:, 64:320]
    for i in range(1, 8):
        window = jnp.where(rem(t, 8) == i, padded[:, 64 * i + 64 : 64 * i + 320], window)
    query = column(window[:, 128:256])[64:128, :]
    key_at = lax.broadcasted_iota(jnp.int32, (64, 256), 1)
    query_at = lax.broadcasted_iota(jnp.int32, (64, 256), 0) + 192
    return jnp.where((query == window) & (key_at <= query_at), 1.0, 0.0)


def step_kernel(*refs):
    refs = list(refs)
    ctx, resid, embedded, cotangent, gain_e, gain_j, segments = take(refs, 7)
    weights = take(refs, 6)
    draft, feats_out, grads_out, query_out, key_out, value_out, output_out = take(refs, 7)
    wt, wj, wq, wk, wv, wo = held = take(refs, 6)
    ca, sb, fa, ea, xa, qh, gh, kw, vw, kg, kgot, gq, at, jg, joined, kvs, qps, sums = take(refs, 18)
    s_loc, s_kv, r_kv, s_kg, r_kg, s_w = take(refs, 6)
    me = Place()
    x, y, z, c, t = me.x, me.y, me.z, me.c, me.t
    mv = Mover(me, s_loc.at[0])
    mine, half = rows(x * 64, 64), rows(c * 128, 128)
    plane = [me.at(x=rem(x + d % 4, 4), y=rem(y + d // 4, 4)) for d in range(1, 16)]
    line = [me.at(z=rem(z + d % 4, 4), c=rem(c + d // 4, 2)) for d in range(1, 8)]
    xn, back_ps, stage = sb.at[:, :, 1], sb.at[:, :, 0], sb.at[:, :, 2]
    context_rows = [
        GatherG(mv, "ctx", lambda q, core, l=l: ca.at[q, l, rows(core * 128, 128), :], *take(refs, 4)) for l in range(3)
    ]
    levels = [SumT(mv, sb.at[:, :, l], *take(refs, 20)) for l in range(3)]
    early_rows = GatherG(mv, "end", lambda q, core: ea.at[:, q, rows(core * 128, 128), :], *take(refs, 4))
    hidden_rows = GatherG(mv, "xa", lambda q, core: xa.at[q, rows(core * 128, 128), :], *take(refs, 4))
    grad_rows = GatherG(mv, "end", lambda q, core: jg.at[q, rows(core * 128, 128), :], *take(refs, 4))
    embed_stats, hidden_stats, inner_stats = (StatsT(mv, *take(refs, 3)) for _ in range(3))
    embed_rates, hidden_rates, factors = (TilesG(mv, line, *take(refs, 3)) for _ in range(3))
    back = SumT(mv, back_ps, *take(refs, 20))
    qkv = SumT(mv, qps, *take(refs, 20))
    line_sum = SumG(mv, *take(refs, 8))
    output = SumG(mv, *take(refs, 8))
    feats = [
        GatherT(mv, lambda h, q, p, lo, n, l=l: fa.at[h, q, l, pl.ds(pl.multiple_of(p * 64 + lo, 32), n), :], *take(refs, 4))
        for l in range(3)
    ]
    ends = GatherT(mv, lambda h, q, p, lo, n: gq.at[h, q, pl.ds(pl.multiple_of(p * 64 + lo, 32), n), :], *take(refs, 4))
    attends = GatherT(mv, lambda h, q, p, lo, n: at.at[h, q, pl.ds(pl.multiple_of(p * 64 + lo, 32), n), :], *take(refs, 4))
    assert not refs
    outs = []

    def local_out(src, dst):
        copy = pltpu.make_async_copy(src, dst, s_loc.at[1 + len(outs)])
        copy.start()
        outs.append(copy)

    loads = [pltpu.make_async_copy(src, dst, s_w.at[i]) for i, (src, dst) in enumerate(zip(weights, held))]
    for load in loads:
        load.start()
    greet(plane + line)

    q0 = group_of(z)

    def context_out(l):
        context_rows[l].to_sibling(0, ctx.at[l])
        context_rows[l].along_z(ctx.at[l])

    context_out(0)
    context_out(1)
    ca[q0, :, half, :] = ctx[...]
    ea[0, q0, half, :] = embedded[...]
    ea[1, q0, half, :] = cotangent[...]
    own_embedded = embedded[...].astype(F32)
    embed_stats.start(lanes(jnp.sum(own_embedded * own_embedded, -1, keepdims=True)))

    def context_in(l):
        for e in NEAR:
            context_rows[l].forward(e)
        for e in range(4):
            context_rows[l].whole(e)

    def target(l):
        for e in (2, 1, 3, 0):
            q = rem(y + e, 4)
            for j in range(4):
                part = dot(ca[q, l], wt[l, :, j * 256 : (j + 1) * 256])
                sb[j // 2, e, l, :, (j % 2) * 256 : (j % 2 + 1) * 256] = part.astype(BF16)
            levels[l].issue(e)

    def second(l):
        for e in (1, 3, 2, 0):
            levels[l].second(e)

    def collect(l):
        for e in (2, 1, 3, 0):
            levels[l].collect_x(e)
        levels[l].fold()

    def finish(l):
        for h in range(2):
            total = levels[l].finish(h)
            fa[h, y, l, mine, :] = (resid[l, :, h * 512 : (h + 1) * 512].astype(F32) + total).astype(BF16)
            feats[l].start(h)

    def both(step, *args):
        for h in range(2):
            step(h, *args)

    loads[0].wait()
    context_in(0)
    context_out(2)
    target(0)
    context_in(1)
    early_rows.to_sibling(0)
    early_rows.along_z()
    target(1)
    second(0)
    context_in(2)
    target(2)
    second(1)
    embed_rates.start(lax.rsqrt(embed_stats.total() / 8192.0 + epsilon))
    collect(0)
    second(2)
    for e in NEAR:
        early_rows.forward(e)
    finish(0)
    collect(1)
    both(feats[0].first)
    finish(1)
    both(feats[0].relay, 0)
    collect(2)
    both(feats[0].far)
    both(feats[1].first)
    finish(2)

    for e in range(4):
        early_rows.whole(e)
    embed_rates.whole()
    scale_e = gain_e[...].astype(F32)[None, :]
    scale_j = gain_j[...].astype(F32)[None, :]
    for l in range(3):
        mv.settle(levels[l])
    for load in loads[1:]:
        load.wait()

    def inputs_part(e, i, source, rates, scales):
        q = rem(y + e, 4)
        for k in range(2):
            part = slice(k * 128, (k + 1) * 128)
            xn[i, q, part, :] = (source(q)[part, :].astype(F32) * rates.column(q, k) * scales).astype(BF16)
        for h, first, there, width in (
            (0, 0, 0, 256), (0, 256, 256, 256), (0, 512, 512, 128), (1, 640, 0, 128), (1, 768, 128, 256), (1, 0, 384, 128), (1, 0, 512, 128),
        ):
            w = (wk if there == 384 else wv) if h == 1 and there >= 384 else wq
            total = dot(xn[i, q], w[i, :, first : first + width])
            if i:
                total = total + qps[h, e, :, there : there + width].astype(F32)
            qps[h, e, :, there : there + width] = total.astype(BF16)

    def embed_part(e):
        inputs_part(e, 0, lambda q: ea[0, q], embed_rates, scale_e)

    def back_part(e):
        q = rem(y + e, 4)
        for j in range(4):
            part = nt(ea[1, q], wo[j * 256 : (j + 1) * 256, :])
            back_ps[j // 2, e, :, (j % 2) * 256 : (j % 2 + 1) * 256] = part.astype(BF16)

    def join(l, e):
        q = feats[l].group(e)
        for j in range(2):
            columns = slice(j * 256, (j + 1) * 256)
            total = dot(fa[0, q, l], wj[l, 0:512, columns]) + dot(fa[1, q, l], wj[l, 512:1024, columns])
            if l:
                total = total + sums[e, :, columns]
            if l < 2:
                sums[e, :, columns] = total
            else:
                line_sum.refs[0][e, :, columns] = total.astype(BF16)
        if l == 2:
            line_sum.swap(e)

    both(feats[0].relay, 3)
    both(feats[0].relay, 1)
    embed_part(2)
    both(feats[1].relay, 0)
    both(feats[0].relay, 2)
    both(feats[1].far)
    both(feats[2].first)
    embed_part(1)
    both(feats[1].relay, 3)
    both(feats[1].relay, 1)
    both(feats[2].relay, 0)
    embed_part(3)
    both(feats[1].relay, 2)
    both(feats[2].far)
    embed_part(0)
    for e in (0, 1, 3, 2):
        join(0, e)
    both(feats[2].relay, 3)
    both(feats[2].relay, 1)
    for e in (2, 1, 3, 0):
        back_part(e)
    join(1, 0)
    join(1, 1)
    both(feats[2].relay, 2)
    join(1, 3)
    join(1, 2)
    join(2, 0)
    for e in (2, 1, 3, 0):
        back.issue(e)
    join(2, 1)
    line_sum.pair(0)
    join(2, 3)
    line_sum.pair(1)
    join(2, 2)
    line_sum.pair(3)
    line_sum.pair(2)
    local_out(fa, feats_out)
    value = line_sum.total()
    joined[...] = value

    xa[q0, half, :] = value.astype(BF16)
    hidden_rows.to_sibling(0)
    hidden_rows.along_z()
    hidden_stats.start(lanes(jnp.sum(value * value, -1, keepdims=True)))
    for e in (1, 3, 2, 0):
        back.second(e)
    for e in NEAR:
        hidden_rows.forward(e)
    hidden_rates.start(lax.rsqrt(hidden_stats.total() / 8192.0 + epsilon))
    for e in (2, 1, 3, 0):
        back.collect_x(e)
    for e in range(4):
        hidden_rows.whole(e)
    hidden_rates.whole()
    for e in (2, 1, 3, 0):
        inputs_part(e, 1, lambda q: xa[q], hidden_rates, scale_j)
        qkv.issue(e)
    back.fold()
    for e in (1, 3, 2, 0):
        qkv.second(e)
    for h in range(2):
        got = back.finish(h).astype(BF16)
        for i in range(4):
            gh[(4 * h + i) * 64 : (4 * h + i + 1) * 64, :] = got[:, i * 128 : (i + 1) * 128]
    for e in (2, 1, 3, 0):
        qkv.collect_x(e)
    qkv.fold()

    got = qkv.finish(1).astype(BF16)
    kw[0:64, :] = jnp.zeros((64, 128), BF16)
    vw[0:64, :] = jnp.zeros((64, 128), BF16)
    kw[192:256, :] = got[:, 384:512]
    vw[192:256, :] = got[:, 512:640]
    for i in range(1, 3):
        after = rem(t + i, 16)
        to = me.at(x=rem(after, 4), y=lax.div(after, jnp.int32(4)))
        place = slice(192 - 64 * i, 256 - 64 * i)
        mv.send(kw.at[192:256, :], kw.at[place, :], s_kv.at[0, i - 1], r_kv.at[0, i - 1], to)
        mv.send(vw.at[192:256, :], vw.at[place, :], s_kv.at[1, i - 1], r_kv.at[1, i - 1], to)
    for i in range(3):
        qh[(5 + i) * 64 : (6 + i) * 64, :] = got[:, i * 128 : (i + 1) * 128]
    got = qkv.finish(0).astype(BF16)
    for i in range(5):
        qh[i * 64 : (i + 1) * 64, :] = got[:, i * 128 : (i + 1) * 128]
    for i in range(1, 3):
        place = slice(192 - 64 * i, 256 - 64 * i)
        mv.arrived(kw.at[place, :], r_kv.at[0, i - 1])
        mv.arrived(vw.at[place, :], r_kv.at[1, i - 1])

    scale = 128.0**-0.5
    allowed = jnp.concatenate([attention_mask(segments, t)] * 4, axis=0) > 0.5
    for i in range(2):
        part = slice(i * 256, (i + 1) * 256)
        scores = jnp.where(allowed, nt(qh[part, :], kw[...]) * scale, -1e30)
        powers = jnp.exp(scores - jnp.max(scores, -1, keepdims=True))
        probs = powers / jnp.sum(powers, -1, keepdims=True)
        low = probs.astype(BF16)
        attended = dot(low, vw[...]).astype(BF16)
        for j in range(4):
            at[i, y, mine, j * 128 : (j + 1) * 128] = attended[j * 64 : (j + 1) * 64, :]
        value_grad = tn(low, gh[part, :])
        probs_grad = nt(gh[part, :], vw[...])
        score_grad = probs * (probs_grad - jnp.sum(probs_grad * probs, -1, keepdims=True)) * scale
        score_grad = score_grad.astype(BF16)
        query_grad = dot(score_grad, kw[...]).astype(BF16)
        for j in range(4):
            head = 4 * i + j
            h, at_head = (0, head) if head < 5 else (1, head - 5)
            gq[h, y, mine, at_head * 128 : (at_head + 1) * 128] = query_grad[j * 64 : (j + 1) * 64, :]
        key_grad = tn(score_grad, qh[part, :])
        if i == 0:
            kg[0, :, :] = key_grad
            kg[1, :, :] = value_grad
        else:
            kg[0, :, :] = kg[0, :, :] + key_grad
            kg[1, :, :] = kg[1, :, :] + value_grad
    for i in range(1, 3):
        before = rem(t + 16 - i, 16)
        to = me.at(x=rem(before, 4), y=lax.div(before, jnp.int32(4)))
        mv.send(kg.at[:, 192 - 64 * i : 256 - 64 * i, :], kgot.at[i - 1], s_kg.at[i - 1], r_kg.at[i - 1], to)
    ends.start(0)
    for i in range(2):
        mv.arrived(kgot.at[i], r_kg.at[i])
    for i in range(2):
        total = kg[i, 192:256, :] + kgot[0, i] + kgot[1, i]
        gq[1, y, mine, 384 + 128 * i : 512 + 128 * i] = total.astype(BF16)
    ends.start(1)
    mv.settle(line_sum)
    mv.settle("xa")
    mv.settle("ctx")
    mv.settle(back)
    ends.middle()

    def hidden_part(e):
        q = ends.group(e)
        for j in range(2):
            columns = slice(j * 256, (j + 1) * 256)
            total = nt(gq[0, q], wq[1, columns, 0:640])
            total = total + nt(gq[1, q, :, 0:384], wq[1, columns, 640:1024])
            total = total + nt(gq[1, q, :, 384:512], wk[1, columns, :])
            total = total + nt(gq[1, q, :, 512:640], wv[1, columns, :])
            line_sum.refs[0][e, :, columns] = total.astype(BF16)
        line_sum.swap(e)

    hidden_part(0)
    ends.end()
    attends.start(0)
    attends.start(1)
    hidden_part(1)
    line_sum.pair(0)
    hidden_part(3)
    line_sum.pair(1)
    hidden_part(2)
    line_sum.pair(3)
    line_sum.pair(2)

    def query_weight(h):
        for first in (0, 256, 512, 640, 896):
            width = 128 if first in (512, 896) else 256
            i, there = (0, first) if first < 640 else (1, first - 640)
            total = jnp.zeros((512, width), F32)
            for q in range(4):
                total = total + tn(xn[h, q], gq[i, q, :, there : there + width])
            total = total.astype(BF16)
            place = first % 512
            for k in range(2):
                stage[h, 2 * k + first // 512, :, place : place + width] = total[k * 256 : (k + 1) * 256, :]
        for k in range(4):
            local_out(stage.at[h, k], query_out.at[h, (k // 2) * 256 : (k // 2 + 1) * 256, (k % 2) * 512 : (k % 2 + 1) * 512])

    def key_value_weight(h):
        total = jnp.zeros((512, 256), F32)
        for q in range(4):
            total = total + tn(xn[h, q], gq[1, q, :, 384:640])
        kvs[0, h] = total[:, 0:128].astype(BF16)
        kvs[1, h] = total[:, 128:256].astype(BF16)
        local_out(kvs.at[0, h], key_out.at[h])
        local_out(kvs.at[1, h], value_out.at[h])

    def output_weight(h):
        for j in range(2):
            columns = slice(j * 256, (j + 1) * 256)
            total = jnp.zeros((512, 256), F32)
            for q in range(4):
                total = total + tn(at[h, q], ea[1, q, :, columns])
            total = total.astype(BF16)
            for k in range(2):
                back_ps[h, k, :, columns] = total[k * 256 : (k + 1) * 256, :]
        for k in range(2):
            local_out(back_ps.at[h, k], output_out.at[(2 * h + k) * 256 : (2 * h + k + 1) * 256, :])

    key_value_weight(0)
    key_value_weight(1)
    for h in range(2):
        attends.first(h)
    hidden_grad = line_sum.total()
    scaled = hidden_grad * scale_j
    value = joined[...]
    inner_stats.start(lanes(jnp.sum(scaled * value, -1, keepdims=True)))
    own_rate = hidden_rates.tiles[2 * q0 + c]
    jg[q0, half, :] = (cotangent[...].astype(F32) + column(own_rate[0:1, :]) * scaled).astype(BF16)
    grad_rows.to_sibling(0)
    grad_rows.along_z()
    for h in range(2):
        attends.relay(h, 0)
    for h in range(2):
        attends.far(h)
    query_weight(0)
    mean = inner_stats.total() / 8192.0
    factors.start(own_rate * own_rate * own_rate * mean)
    for a in (3, 1):
        for h in range(2):
            attends.relay(h, a)
    attends.end()

    def output_part(e):
        q = attends.group(e)
        for j in range(2):
            columns = slice(j * 256, (j + 1) * 256)
            total = dot(at[0, q], wo[0:512, columns]) + dot(at[1, q], wo[512:1024, columns])
            output.refs[0][e, :, columns] = total.astype(BF16)
        output.swap(e)

    for e in NEAR:
        grad_rows.forward(e)
    output_part(0)
    output_part(1)
    output.pair(0)
    output_part(3)
    output.pair(1)
    output_part(2)
    output.pair(3)
    output.pair(2)
    query_weight(1)
    output_weight(0)
    output_weight(1)
    for e in range(4):
        grad_rows.whole(e)
    factors.whole()
    for q in range(4):
        for k in range(2):
            part = slice(k * 128, (k + 1) * 128)
            grad = jg[q, part, :].astype(F32) - xa[q, part, :].astype(F32) * factors.column(q, k)
            xa[q, part, :] = grad.astype(BF16)

    local_out(xa, grads_out)
    draft[...] = (value + output.total()).astype(BF16)
    mv.drain()
    for copy in outs:
        copy.wait()


def step_call(*args):
    def gather_g():
        return [dma(3), dma(3), dma(4), dma(4)]

    shape = jax.ShapeDtypeStruct
    return pl.pallas_call(
        step_kernel,
        name="step",
        out_shape=(
            shape((128, 512), BF16),
            shape((2, 4, 3, 256, 512), BF16),
            shape((4, 256, 512), BF16),
            shape((2, 512, 1024), BF16),
            shape((2, 512, 128), BF16),
            shape((2, 512, 128), BF16),
            shape((1024, 512), BF16),
        ),
        in_specs=[IN_VMEM] * 7 + [ANYWHERE] * 6,
        out_specs=(IN_VMEM, *[ANYWHERE] * 6),
        scratch_shapes=[
            vmem(3, 512, 1024),
            vmem(3, 1024, 512),
            vmem(2, 512, 1024),
            vmem(2, 512, 128),
            vmem(2, 512, 128),
            vmem(1024, 512),
            vmem(4, 3, 256, 512),
            vmem(2, 4, 3, 256, 512),
            vmem(2, 4, 3, 256, 512),
            vmem(2, 4, 256, 512),
            vmem(4, 256, 512),
            vmem(512, 128),
            vmem(512, 128),
            vmem(256, 128),
            vmem(256, 128),
            vmem(2, 256, 128, dtype=F32),
            vmem(2, 2, 64, 128, dtype=F32),
            vmem(2, 4, 256, 640),
            vmem(2, 4, 256, 512),
            vmem(4, 256, 512),
            vmem(128, 512, dtype=F32),
            vmem(2, 2, 512, 128),
            vmem(2, 4, 256, 640),
            vmem(4, 256, 512, dtype=F32),
            dma(26), dma(2, 2), dma(2, 2), dma(2), dma(2), dma(6),
            *gather_g(), *gather_g(), *gather_g(),
            *SumT.scratch(512), *SumT.scratch(512), *SumT.scratch(512),
            *gather_g(), *gather_g(), *gather_g(),
            *StatsT.scratch(), *StatsT.scratch(), *StatsT.scratch(),
            *TilesG.scratch(), *TilesG.scratch(), *TilesG.scratch(),
            *SumT.scratch(512), *SumT.scratch(640), *SumG.scratch(), *SumG.scratch(),
            *GatherT.scratch(), *GatherT.scratch(), *GatherT.scratch(), *GatherT.scratch(), *GatherT.scratch(),
        ],
        compiler_params=pltpu.CompilerParams(
            collective_id=0, has_side_effects=True, vmem_limit_bytes=VMEM_LIMIT
        ),
        cost_estimate=pl.CostEstimate(flops=20000000000, bytes_accessed=24000000, transcendentals=0),
    )(*args)


def join_weight_kernel(feats, grads, *refs):
    given, join_out, results = refs[:5], refs[5], refs[6:11]
    fa, jg, stage, s_in, s_out, s_on = refs[11:17]
    held = refs[17:]
    taken = [pltpu.make_async_copy(src, dst, s_on.at[i]) for i, (src, dst) in enumerate(zip(given, held))]
    handed = [pltpu.make_async_copy(src, dst, s_on.at[5 + i]) for i, (src, dst) in enumerate(zip(held, results))]
    loads = [pltpu.make_async_copy(grads, jg, s_in.at[3])]
    loads += [pltpu.make_async_copy(feats.at[:, :, l], fa.at[:, :, l], s_in.at[l]) for l in range(3)]
    for copy in loads + taken:
        copy.start()
    loads[0].wait()
    outs = []
    for l in range(3):
        loads[1 + l].wait()
        if l == 1:
            for there, back in zip(taken, handed):
                there.wait()
                back.start()
        for h in range(2):
            for j in range(2):
                columns = slice(j * 256, (j + 1) * 256)
                total = jnp.zeros((512, 256), F32)
                for q in range(4):
                    total = total + tn(fa[h, q, l], jg[q, :, columns])
                stage[l, h, :, columns] = total.astype(BF16)
            copy = pltpu.make_async_copy(stage.at[l, h], join_out.at[l, h * 512 : (h + 1) * 512, :], s_out.at[2 * l + h])
            copy.start()
            outs.append(copy)
    for copy in outs + handed:
        copy.wait()


def join_weight_call(feats, grads, *given):
    return pl.pallas_call(
        join_weight_kernel,
        name="join_weight",
        out_shape=(
            jax.ShapeDtypeStruct((3, 1024, 512), BF16),
            *[jax.ShapeDtypeStruct(array.shape, array.dtype) for array in given],
        ),
        in_specs=[ANYWHERE] * (2 + len(given)),
        out_specs=tuple([ANYWHERE] * (1 + len(given))),
        scratch_shapes=[
            vmem(2, 4, 3, 256, 512), vmem(4, 256, 512), vmem(3, 2, 512, 512), dma(4), dma(6), dma(10),
            *[pltpu.VMEM(array.shape, array.dtype) for array in given],
        ],
        compiler_params=pltpu.CompilerParams(vmem_limit_bytes=VMEM_LIMIT),
        cost_estimate=pl.CostEstimate(flops=3300000000, bytes_accessed=20000000, transcendentals=0),
    )(feats, grads, *given)


def local(
    context,
    resid_in,
    target_out_w,
    embedded,
    join_w,
    embed_gain,
    joined_gain,
    query_w,
    key_w,
    value_w,
    out_w,
    segment_ids,
    grad_hidden,
):
    draft_hidden, feats, grads, *weights = step_call(
        context.transpose(1, 0, 2),
        resid_in.transpose(1, 0, 2),
        embedded,
        grad_hidden,
        embed_gain,
        joined_gain,
        segment_ids,
        target_out_w,
        join_w,
        query_w,
        key_w,
        value_w,
        out_w,
    )
    grad_join, draft_hidden, *weights = join_weight_call(feats, grads, draft_hidden, *weights)
    return (draft_hidden, grad_join, *weights)


def solution(mesh):
    in_specs = (
        P(("group", "seq"), None, "tensor"),
        P("tensor", None, ("group", "seq")),
        P(None, "tensor", ("group", "seq")),
        P(("group", "seq"), "tensor"),
        P(None, ("group", "seq"), "tensor"),
        P("tensor"),
        P("tensor"),
        P(None, "tensor", ("group", "seq")),
        P(None, "tensor", ("group", "seq")),
        P(None, "tensor", ("group", "seq")),
        P(("group", "seq"), "tensor"),
        P(),
        P(("group", "seq"), "tensor"),
    )
    out_specs = (
        P(("group", "seq"), "tensor"),
        P(None, ("group", "seq"), "tensor"),
        P(None, "tensor", ("group", "seq")),
        P(None, "tensor", ("group", "seq")),
        P(None, "tensor", ("group", "seq")),
        P(("group", "seq"), "tensor"),
    )
    return jax.shard_map(local, mesh=mesh, in_specs=in_specs, out_specs=out_specs, check_vma=False)
```

```python
import jax
import jax.numpy as jnp
from jax import lax
from jax.experimental import pallas as pl
from jax.experimental.pallas import tpu as pltpu
from jax.sharding import PartitionSpec as P

epsilon = 1e-05
F32 = jnp.float32
BF16 = jnp.bfloat16
NEAR = (1, 3, 2)
VMEM_LIMIT = 62 * 2**20


def rem(value, count):
    return lax.rem(value, jnp.int32(count))


def group_of(z):
    return rem(z, 2) * 2 + lax.div(z, jnp.int32(2))


class Place:
    def __init__(self):
        self.t = lax.axis_index("tensor")
        seq = lax.axis_index("seq")
        self.x, self.y = rem(self.t, 4), lax.div(self.t, jnp.int32(4))
        self.z = lax.div(seq, jnp.int32(2)) * 2 + lax.axis_index("group")
        self.c = rem(seq, 2)

    def at(self, x=None, y=None, z=None, c=None):
        x = self.x if x is None else x
        y = self.y if y is None else y
        z = self.z if z is None else z
        c = self.c if c is None else c
        return (rem(z, 2), y * 4 + x, lax.div(z, jnp.int32(2)) * 2 + c)

    def to_x(self, d):
        return self.at(x=rem(self.x + d, 4))

    def to_y(self, d):
        return self.at(y=rem(self.y + d, 4))

    def to_z(self, d):
        return self.at(z=rem(self.z + d, 4))

    def sibling(self):
        return self.at(c=1 - self.c)


def greet(devices):
    barrier = pltpu.get_barrier_semaphore()
    for device in devices:
        pl.semaphore_signal(barrier, inc=1, device_id=device, device_id_type=pl.DeviceIdType.MESH)
    pl.semaphore_wait(barrier, len(devices))


def remote(src, dst, send, recv, device):
    return pltpu.make_async_remote_copy(
        src_ref=src,
        dst_ref=dst,
        send_sem=send,
        recv_sem=recv,
        device_id=device,
        device_id_type=pl.DeviceIdType.MESH,
    )


def rows(first, count):
    return pl.ds(pl.multiple_of(first, count), count)


def vmem(*shape, dtype=BF16):
    return pltpu.VMEM(shape, dtype)


def dma(*shape):
    return pltpu.SemaphoreType.DMA(shape)


IN_VMEM = pl.BlockSpec(memory_space=pltpu.VMEM)
ANYWHERE = pl.BlockSpec(memory_space=pl.ANY)


def nt(a, b):
    return lax.dot_general(a, b, (((1,), (1,)), ((), ())), preferred_element_type=F32)


def tn(a, b):
    return lax.dot_general(a, b, (((0,), (0,)), ((), ())), preferred_element_type=F32)


def dot(a, b):
    return jnp.dot(a, b, preferred_element_type=F32)


class Mover:
    def __init__(self, me, dummy):
        self.me, self.dummy, self.open = me, dummy, {}

    def send(self, src, dst, ss, rs, device, when=None, tag="end"):
        copy = remote(src, dst, ss, rs, device)
        if when is None:
            copy.start()
        else:
            pl.when(when)(copy.start)
        self.open.setdefault(tag, []).append((when, src, ss))

    def arrived(self, dst, rs):
        remote(dst, dst, self.dummy, rs, self.me.sibling()).wait_recv()

    def settle(self, tag):
        for when, src, ss in self.open.pop(tag, []):
            wait = remote(src, src, ss, self.dummy, self.me.sibling()).wait_send
            if when is None:
                wait()
            else:
                pl.when(when)(wait)

    def drain(self):
        for tag in list(self.open):
            self.settle(tag)


class GatherG:
    def __init__(self, mv, tag, block, s_z, r_z, s_c, r_c):
        me = mv.me
        self.mv, self.tag, self.block, self.sems = mv, tag, block, (s_z, r_z, s_c, r_c)
        self.group = [group_of(rem(me.z + e, 4)) for e in range(4)]

    def to_sibling(self, e, src=None):
        me, (_, _, s_c, r_c) = self.mv.me, self.sems
        place = self.block(self.group[e], me.c)
        self.mv.send(place if src is None else src, place, s_c.at[e], r_c.at[e], me.sibling(), tag=self.tag)

    def along_z(self, src=None):
        me, (s_z, r_z, _, _) = self.mv.me, self.sems
        place = self.block(self.group[0], me.c)
        for d in NEAR:
            self.mv.send(place if src is None else src, place, s_z.at[d - 1], r_z.at[3 - d], me.to_z(d), tag=self.tag)

    def forward(self, e):
        me, (_, r_z, _, _) = self.mv.me, self.sems
        self.mv.arrived(self.block(self.group[e], me.c), r_z.at[e - 1])
        self.to_sibling(e)

    def whole(self, e):
        me, (_, _, _, r_c) = self.mv.me, self.sems
        self.mv.arrived(self.block(self.group[e], 1 - me.c), r_c.at[e])


class GatherT:
    def __init__(self, mv, block, s_1, r_1, s_2, r_2):
        self.mv, self.rows_of, self.sems = mv, block, (s_1, r_1, s_2, r_2)

    def block(self, h, a, b, lo=0, count=64):
        me = self.mv.me
        p, q = (a, b) if h == 0 else (b, a)
        return self.rows_of(h, rem(me.y + q, 4), rem(me.x + p, 4), lo, count)

    def move(self, first_axis, h, part, ss, rs, i):
        me, step = self.mv.me, 1 if i % 2 == 0 else 3
        to = me.to_x(step) if first_axis == (h == 0) else me.to_y(step)
        self.mv.send(part, part, ss, rs, to)

    def to_second(self, h, a):
        s_2, r_2 = self.sems[2:]
        for i in range(2):
            self.move(False, h, self.block(h, a, 0), s_2.at[h, a, i], r_2.at[h, a, i], i)

    def start(self, h):
        s_1, r_1 = self.sems[:2]
        for i in range(2):
            self.move(True, h, self.block(h, 0, 0), s_1.at[h, i], r_1.at[h, i], i)
        self.to_second(h, 0)

    def first(self, h):
        s_1, r_1 = self.sems[:2]
        for i, a in ((0, 3), (1, 1)):
            self.mv.arrived(self.block(h, a, 0), r_1.at[h, i])
            self.move(True, h, self.block(h, a, 0, 32 * i, 32), s_1.at[h, 2 + i], r_1.at[h, 2 + i], i)
            self.to_second(h, a)

    def far(self, h):
        for i in range(2):
            self.mv.arrived(self.block(h, 2, 0, 32 * i, 32), self.sems[1].at[h, 2 + i])
        self.to_second(h, 2)

    def relay(self, h, a):
        s_2, r_2 = self.sems[2:]
        for i, b in ((0, 3), (1, 1)):
            self.mv.arrived(self.block(h, a, b), r_2.at[h, a, i])
            self.move(False, h, self.block(h, a, b, 32 * i, 32), s_2.at[h, a, 2 + i], r_2.at[h, a, 2 + i], i)

    def last(self, h, a):
        for i in range(2):
            self.mv.arrived(self.block(h, a, 2, 32 * i, 32), self.sems[3].at[h, a, 2 + i])

    def middle(self):
        for h in range(2):
            self.first(h)
        for h in range(2):
            self.relay(h, 0)
        for h in range(2):
            self.far(h)
        for a in (3, 1):
            for h in range(2):
                self.relay(h, a)

    def end(self):
        for h in range(2):
            self.relay(h, 2)

    def group(self, e):
        if e == 2:
            for a in range(4):
                self.last(0, a)
        self.last(1, e)
        return rem(self.mv.me.y + e, 4)

    @staticmethod
    def scratch():
        return [dma(2, 4), dma(2, 4), dma(2, 4, 4), dma(2, 4, 4)]


class DirectT(GatherT):
    def to_second(self, h, a):
        me, (s_2, r_2) = self.mv.me, self.sems[2:]
        for d in NEAR:
            to = me.to_y(d) if h == 0 else me.to_x(d)
            self.mv.send(self.block(h, a, 0), self.block(h, a, 0), s_2.at[h, a, d], r_2.at[h, a, 4 - d], to)

    def start(self, h):
        me, (s_1, r_1) = self.mv.me, self.sems[:2]
        for d in NEAR:
            to = me.to_x(d) if h == 0 else me.to_y(d)
            self.mv.send(self.block(h, 0, 0), self.block(h, 0, 0), s_1.at[h, d], r_1.at[h, 4 - d], to)
        self.to_second(h, 0)

    def first(self, h):
        for a in (1, 3):
            self.mv.arrived(self.block(h, a, 0), self.sems[1].at[h, a])
            self.to_second(h, a)

    def far(self, h):
        self.mv.arrived(self.block(h, 2, 0), self.sems[1].at[h, 2])
        self.to_second(h, 2)

    def relay(self, h, a):
        pass

    def group(self, e):
        if e:
            for a in range(4):
                self.mv.arrived(self.block(0, a, e), self.sems[3].at[0, a, e])
        for b in NEAR:
            self.mv.arrived(self.block(1, e, b), self.sems[3].at[1, e, b])
        return rem(self.mv.me.y + e, 4)


class SumG:
    def __init__(self, mv, js, jx, j2, jz, s_x, r_x, s_z, r_z):
        self.mv, self.refs, self.sems = mv, (js, jx, j2, jz), (s_x, r_x, s_z, r_z)

    def swap(self, e):
        (js, jx, _, _), (s_x, r_x, _, _), me = self.refs, self.sems, self.mv.me
        self.mv.send(js.at[e, rows((1 - me.c) * 128, 128), :], jx.at[e], s_x.at[e], r_x.at[e], me.sibling(), tag=self)

    def pair(self, e):
        (js, jx, j2, jz), (_, r_x, s_z, r_z), me = self.refs, self.sems, self.mv.me
        self.mv.arrived(jx.at[e], r_x.at[e])
        j2[e] = (js[e, rows(me.c * 128, 128), :].astype(F32) + jx[e].astype(F32)).astype(BF16)
        to = group_of(rem(me.y + e, 4))
        slot = rem(me.z - to + 4, 4)
        at = jnp.maximum(slot - 1, 0)
        self.mv.send(j2.at[e], jz.at[at], s_z.at[e], r_z.at[at], me.at(z=to), when=slot != 0, tag=self)

    def total(self):
        (_, _, j2, jz), (_, _, _, r_z), me = self.refs, self.sems, self.mv.me
        for d in NEAR:
            self.mv.arrived(jz.at[d - 1], r_z.at[d - 1])
        total = j2[rem(group_of(me.z) - me.y + 4, 4)].astype(F32)
        for d in range(3):
            total = total + jz[d].astype(F32)
        return total

    @staticmethod
    def scratch():
        return [vmem(4, 256, 512), vmem(4, 128, 512), vmem(4, 128, 512), vmem(3, 128, 512), dma(4), dma(4), dma(4), dma(3)]


class SumT:
    def __init__(self, mv, ps, hx, rx, hy, ry, s0, s1, r2x, r2y, *sems):
        self.mv, self.ps, self.hx, self.rx, self.hy, self.ry = mv, ps, hx, rx, hy, ry
        self.s0, self.s1, self.r2x, self.r2y = s0, s1, r2x, r2y
        self.sems = sems

    def issue(self, e):
        mv, me = self.mv, self.mv.me
        s_hx, r_hx, _, _, s_hy, r_hy = self.sems[:6]
        opposite = rem(me.x + 2, 4) * 64
        for i, step in enumerate((1, 3)):
            part = self.ps.at[0, e, rows(opposite + 32 * i, 32), :]
            mv.send(part, self.hx.at[e, i], s_hx.at[e, i], r_hx.at[e, i], me.to_x(step), tag=self)
            if e == 2:
                part = self.ps.at[1, 2, 128 * i : 128 * i + 128, :]
                mv.send(part, self.hy.at[i], s_hy.at[i], r_hy.at[i], me.to_y(step), tag=self)

    def second(self, e):
        mv, me = self.mv, self.mv.me
        _, r_hx, s_x, r_x, _, r_hy, s_y, r_y = self.sems[:8]
        for i, step in enumerate((1, 3)):
            if e == step:
                mv.arrived(self.hy.at[i], r_hy.at[i])
                part = slice(128 * i, 128 * i + 128)
                self.ps[1, e, part, :] = (self.ps[1, e, part, :].astype(F32) + self.hy[i].astype(F32)).astype(BF16)
                mv.send(self.ps.at[1, e], self.ry.at[i], s_y.at[i], r_y.at[i], me.to_y(step), tag=self)
        for i, step in enumerate((1, 3)):
            to = rem(me.x + step, 4) * 64
            mv.arrived(self.hx.at[e, i], r_hx.at[e, i])
            part = rows(to + 32 * i, 32)
            self.ps[0, e, part, :] = (self.ps[0, e, part, :].astype(F32) + self.hx[e, i].astype(F32)).astype(BF16)
            mv.send(self.ps.at[0, e, rows(to, 64), :], self.rx.at[e, i], s_x.at[e, i], r_x.at[e, i], me.to_x(step), tag=self)

    def collect_x(self, e):
        mv, me = self.mv, self.mv.me
        r_x, s_2x, r_2x = self.sems[3], self.sems[8], self.sems[9]
        total = self.ps[0, e, rows(me.x * 64, 64), :].astype(F32)
        for i in range(2):
            mv.arrived(self.rx.at[e, i], r_x.at[e, i])
            total = total + self.rx[e, i].astype(F32)
        self.s0[e] = total.astype(BF16)
        if e:
            mv.send(self.s0.at[e], self.r2x.at[3 - e], s_2x.at[e], r_2x.at[3 - e], me.to_y(e), tag=self)

    def fold(self):
        mv, me = self.mv, self.mv.me
        r_y, s_2y, r_2y = self.sems[7], self.sems[10], self.sems[11]
        for i in range(2):
            mv.arrived(self.ry.at[i], r_y.at[i])
        for d in (2, 1, 3, 0):
            to = rem(me.x + d, 4)
            part = rows(to * 64, 64)
            total = self.ps[1, 0, part, :].astype(F32)
            for i in range(2):
                total = total + self.ry[i, part, :].astype(F32)
            self.s1[part, :] = total.astype(BF16)
            if d:
                mv.send(self.s1.at[part, :], self.r2y.at[3 - d], s_2y.at[d - 1], r_2y.at[3 - d], me.at(x=to), tag=self)

    def finish(self, h):
        mv, me = self.mv, self.mv.me
        got, sem = ((self.r2x, self.sems[9]), (self.r2y, self.sems[11]))[h]
        for d in NEAR:
            mv.arrived(got.at[d - 1], sem.at[d - 1])
        total = (self.s0[0] if h == 0 else self.s1[rows(me.x * 64, 64), :]).astype(F32)
        for d in range(3):
            total = total + got[d].astype(F32)
        return total

    @staticmethod
    def scratch(w):
        return [
            vmem(4, 2, 32, w), vmem(4, 2, 64, w), vmem(2, 128, w), vmem(2, 256, w),
            vmem(4, 64, w), vmem(256, w), vmem(3, 64, w), vmem(3, 64, w),
            dma(4, 2), dma(4, 2), dma(4, 2), dma(4, 2), dma(2), dma(2), dma(2), dma(2), dma(4), dma(3), dma(3), dma(3),
        ]


def lanes(column):
    return jnp.broadcast_to(column, (128, 128)).T[0:8, :]


def column(row):
    return jnp.broadcast_to(row, (128, 128)).T[:, 0:1]


class TilesG:
    def __init__(self, mv, line, tiles, s_t, r_t):
        self.mv, self.line, self.tiles, self.s_t, self.r_t = mv, line, tiles, s_t, r_t

    def place(self, e, core):
        me = self.mv.me
        return self.tiles.at[2 * group_of(rem(me.z + e, 4)) + rem(me.c + core, 2)]

    def start(self, tile):
        me = self.mv.me
        self.tiles[2 * group_of(me.z) + me.c] = tile
        for d in range(1, 8):
            back = (4 - d % 4) % 4 + 4 * (d // 4)
            self.mv.send(self.place(0, 0), self.place(0, 0), self.s_t.at[d], self.r_t.at[back], self.line[d - 1])

    def whole(self):
        for d in range(1, 8):
            self.mv.arrived(self.place(d % 4, d // 4), self.r_t.at[d])

    def column(self, q, i):
        return column(self.tiles[2 * q + i][0:1, :])

    @staticmethod
    def scratch():
        return [pltpu.VMEM((8, 8, 128), F32), dma(8), dma(8)]


class StatsT:
    def __init__(self, mv, tiles, s_t, r_t):
        self.mv, self.tiles, self.s_t, self.r_t = mv, tiles, s_t, r_t

    def start(self, tile):
        me = self.mv.me
        self.tiles[0] = tile
        for d in range(1, 16):
            dx, dy = d % 4, d // 4
            back = (4 - dx) % 4 + 4 * ((4 - dy) % 4)
            to = me.at(x=rem(me.x + dx, 4), y=rem(me.y + dy, 4))
            self.mv.send(self.tiles.at[0], self.tiles.at[back], self.s_t.at[d], self.r_t.at[back], to)

    def total(self):
        for d in range(1, 16):
            self.mv.arrived(self.tiles.at[d], self.r_t.at[d])
        total = self.tiles[0]
        for d in range(1, 16):
            total = total + self.tiles[d]
        return total

    @staticmethod
    def scratch():
        return [pltpu.VMEM((16, 8, 128), F32), dma(16), dma(16)]


def take(refs, count):
    out = refs[:count]
    del refs[:count]
    return out


def attention_mask(segments, t):
    ids = segments[...].astype(F32)
    own = jnp.where(t < 8, ids[0:1, :], ids[1:2, :])
    padded = jnp.concatenate([jnp.full((1, 256), -1.0, F32), own], axis=1)
    window = padded[:, 64:320]
    for i in range(1, 8):
        window = jnp.where(rem(t, 8) == i, padded[:, 64 * i + 64 : 64 * i + 320], window)
    query = column(window[:, 128:256])[64:128, :]
    key_at = lax.broadcasted_iota(jnp.int32, (64, 256), 1)
    query_at = lax.broadcasted_iota(jnp.int32, (64, 256), 0) + 192
    return jnp.where((query == window) & (key_at <= query_at), 1.0, 0.0)


def step_kernel(*refs):
    refs = list(refs)
    ctx, resid, embedded, cotangent, gain_e, gain_j, segments = take(refs, 7)
    weights = take(refs, 6)
    draft, feats_out, grads_out, query_out, key_out, value_out, output_out = take(refs, 7)
    wt, wj, wq, wk, wv, wo = held = take(refs, 6)
    ca, sb, fa, ea, xa, qh, gh, kw, vw, kg, kgot, gq, at, jg, joined, kvs, qps, sums = take(refs, 18)
    s_loc, s_kv, r_kv, s_kg, r_kg, s_w = take(refs, 6)
    me = Place()
    x, y, z, c, t = me.x, me.y, me.z, me.c, me.t
    mv = Mover(me, s_loc.at[0])
    mine, half = rows(x * 64, 64), rows(c * 128, 128)
    plane = [me.at(x=rem(x + d % 4, 4), y=rem(y + d // 4, 4)) for d in range(1, 16)]
    line = [me.at(z=rem(z + d % 4, 4), c=rem(c + d // 4, 2)) for d in range(1, 8)]
    xn, back_ps, stage = sb.at[:, :, 1], sb.at[:, :, 0], sb.at[:, :, 2]
    context_rows = [
        GatherG(mv, "ctx", lambda q, core, l=l: ca.at[q, l, rows(core * 128, 128), :], *take(refs, 4)) for l in range(3)
    ]
    levels = [SumT(mv, sb.at[:, :, l], *take(refs, 20)) for l in range(3)]
    early_rows = GatherG(mv, "end", lambda q, core: ea.at[:, q, rows(core * 128, 128), :], *take(refs, 4))
    hidden_rows = GatherG(mv, "xa", lambda q, core: xa.at[q, rows(core * 128, 128), :], *take(refs, 4))
    grad_rows = GatherG(mv, "end", lambda q, core: jg.at[q, rows(core * 128, 128), :], *take(refs, 4))
    embed_stats, hidden_stats, inner_stats = (StatsT(mv, *take(refs, 3)) for _ in range(3))
    embed_rates, hidden_rates, factors = (TilesG(mv, line, *take(refs, 3)) for _ in range(3))
    back = SumT(mv, back_ps, *take(refs, 20))
    qkv = SumT(mv, qps, *take(refs, 20))
    line_sum = SumG(mv, *take(refs, 8))
    output = SumG(mv, *take(refs, 8))
    feats = [
        GatherT(mv, lambda h, q, p, lo, n, l=l: fa.at[h, q, l, pl.ds(pl.multiple_of(p * 64 + lo, 32), n), :], *take(refs, 4))
        for l in range(3)
    ]
    ends = GatherT(mv, lambda h, q, p, lo, n: gq.at[h, q, pl.ds(pl.multiple_of(p * 64 + lo, 32), n), :], *take(refs, 4))
    attends = DirectT(mv, lambda h, q, p, lo, n: at.at[h, q, pl.ds(pl.multiple_of(p * 64 + lo, 32), n), :], *take(refs, 4))
    assert not refs
    outs = []

    def local_out(src, dst):
        copy = pltpu.make_async_copy(src, dst, s_loc.at[1 + len(outs)])
        copy.start()
        outs.append(copy)

    loads = [pltpu.make_async_copy(src, dst, s_w.at[i]) for i, (src, dst) in enumerate(zip(weights, held))]
    for load in loads:
        load.start()
    greet(plane + line)

    q0 = group_of(z)

    def context_out(l):
        context_rows[l].to_sibling(0, ctx.at[l])
        context_rows[l].along_z(ctx.at[l])

    context_out(0)
    context_out(1)
    ca[q0, :, half, :] = ctx[...]
    ea[0, q0, half, :] = embedded[...]
    ea[1, q0, half, :] = cotangent[...]
    own_embedded = embedded[...].astype(F32)
    embed_stats.start(lanes(jnp.sum(own_embedded * own_embedded, -1, keepdims=True)))

    def context_in(l):
        for e in NEAR:
            context_rows[l].forward(e)
        for e in range(4):
            context_rows[l].whole(e)

    def target(l):
        for e in (2, 1, 3, 0):
            q = rem(y + e, 4)
            for j in range(4):
                part = dot(ca[q, l], wt[l, :, j * 256 : (j + 1) * 256])
                sb[j // 2, e, l, :, (j % 2) * 256 : (j % 2 + 1) * 256] = part.astype(BF16)
            levels[l].issue(e)

    def second(l):
        for e in (1, 3, 2, 0):
            levels[l].second(e)

    def collect(l):
        for e in (2, 1, 3, 0):
            levels[l].collect_x(e)
        levels[l].fold()

    def finish(l):
        for h in range(2):
            total = levels[l].finish(h)
            fa[h, y, l, mine, :] = (resid[l, :, h * 512 : (h + 1) * 512].astype(F32) + total).astype(BF16)
            feats[l].start(h)

    def both(step, *args):
        for h in range(2):
            step(h, *args)

    loads[0].wait()
    context_in(0)
    context_out(2)
    target(0)
    context_in(1)
    early_rows.to_sibling(0)
    early_rows.along_z()
    target(1)
    second(0)
    context_in(2)
    target(2)
    second(1)
    embed_rates.start(lax.rsqrt(embed_stats.total() / 8192.0 + epsilon))
    collect(0)
    second(2)
    for e in NEAR:
        early_rows.forward(e)
    finish(0)
    collect(1)
    both(feats[0].first)
    finish(1)
    both(feats[0].relay, 0)
    collect(2)
    both(feats[0].far)
    both(feats[1].first)
    finish(2)

    for e in range(4):
        early_rows.whole(e)
    embed_rates.whole()
    scale_e = gain_e[...].astype(F32)[None, :]
    scale_j = gain_j[...].astype(F32)[None, :]
    for l in range(3):
        mv.settle(levels[l])
    for load in loads[1:]:
        load.wait()

    def inputs_part(e, i, source, rates, scales):
        q = rem(y + e, 4)
        for k in range(2):
            part = slice(k * 128, (k + 1) * 128)
            xn[i, q, part, :] = (source(q)[part, :].astype(F32) * rates.column(q, k) * scales).astype(BF16)
        for h, first, there, width in (
            (0, 0, 0, 256), (0, 256, 256, 256), (0, 512, 512, 128), (1, 640, 0, 128), (1, 768, 128, 256), (1, 0, 384, 128), (1, 0, 512, 128),
        ):
            w = (wk if there == 384 else wv) if h == 1 and there >= 384 else wq
            total = dot(xn[i, q], w[i, :, first : first + width])
            if i:
                total = total + qps[h, e, :, there : there + width].astype(F32)
            qps[h, e, :, there : there + width] = total.astype(BF16)

    def embed_part(e):
        inputs_part(e, 0, lambda q: ea[0, q], embed_rates, scale_e)

    def back_part(e):
        q = rem(y + e, 4)
        for j in range(4):
            part = nt(ea[1, q], wo[j * 256 : (j + 1) * 256, :])
            back_ps[j // 2, e, :, (j % 2) * 256 : (j % 2 + 1) * 256] = part.astype(BF16)

    def join(l, e):
        q = feats[l].group(e)
        for j in range(2):
            columns = slice(j * 256, (j + 1) * 256)
            total = dot(fa[0, q, l], wj[l, 0:512, columns]) + dot(fa[1, q, l], wj[l, 512:1024, columns])
            if l:
                total = total + sums[e, :, columns]
            if l < 2:
                sums[e, :, columns] = total
            else:
                line_sum.refs[0][e, :, columns] = total.astype(BF16)
        if l == 2:
            line_sum.swap(e)

    both(feats[0].relay, 3)
    both(feats[0].relay, 1)
    embed_part(2)
    both(feats[1].relay, 0)
    both(feats[0].relay, 2)
    both(feats[1].far)
    both(feats[2].first)
    embed_part(1)
    both(feats[1].relay, 3)
    both(feats[1].relay, 1)
    both(feats[2].relay, 0)
    embed_part(3)
    both(feats[1].relay, 2)
    both(feats[2].far)
    embed_part(0)
    for e in (0, 1, 3, 2):
        join(0, e)
    both(feats[2].relay, 3)
    both(feats[2].relay, 1)
    for e in (2, 1, 3, 0):
        back_part(e)
    join(1, 0)
    join(1, 1)
    both(feats[2].relay, 2)
    join(1, 3)
    join(1, 2)
    join(2, 0)
    for e in (2, 1, 3, 0):
        back.issue(e)
    join(2, 1)
    line_sum.pair(0)
    join(2, 3)
    line_sum.pair(1)
    join(2, 2)
    line_sum.pair(3)
    line_sum.pair(2)
    local_out(fa, feats_out)
    value = line_sum.total()
    joined[...] = value

    xa[q0, half, :] = value.astype(BF16)
    hidden_rows.to_sibling(0)
    hidden_rows.along_z()
    hidden_stats.start(lanes(jnp.sum(value * value, -1, keepdims=True)))
    for e in (1, 3, 2, 0):
        back.second(e)
    for e in NEAR:
        hidden_rows.forward(e)
    hidden_rates.start(lax.rsqrt(hidden_stats.total() / 8192.0 + epsilon))
    for e in (2, 1, 3, 0):
        back.collect_x(e)
    for e in range(4):
        hidden_rows.whole(e)
    hidden_rates.whole()
    for e in (2, 1, 3, 0):
        inputs_part(e, 1, lambda q: xa[q], hidden_rates, scale_j)
        qkv.issue(e)
    back.fold()
    for e in (1, 3, 2, 0):
        qkv.second(e)
    for h in range(2):
        got = back.finish(h).astype(BF16)
        for i in range(4):
            gh[(4 * h + i) * 64 : (4 * h + i + 1) * 64, :] = got[:, i * 128 : (i + 1) * 128]
    for e in (2, 1, 3, 0):
        qkv.collect_x(e)
    qkv.fold()

    got = qkv.finish(1).astype(BF16)
    kw[0:64, :] = jnp.zeros((64, 128), BF16)
    vw[0:64, :] = jnp.zeros((64, 128), BF16)
    kw[192:256, :] = got[:, 384:512]
    vw[192:256, :] = got[:, 512:640]
    for i in range(1, 3):
        after = rem(t + i, 16)
        to = me.at(x=rem(after, 4), y=lax.div(after, jnp.int32(4)))
        place = slice(192 - 64 * i, 256 - 64 * i)
        mv.send(kw.at[192:256, :], kw.at[place, :], s_kv.at[0, i - 1], r_kv.at[0, i - 1], to)
        mv.send(vw.at[192:256, :], vw.at[place, :], s_kv.at[1, i - 1], r_kv.at[1, i - 1], to)
    for i in range(3):
        qh[(5 + i) * 64 : (6 + i) * 64, :] = got[:, i * 128 : (i + 1) * 128]
    got = qkv.finish(0).astype(BF16)
    for i in range(5):
        qh[i * 64 : (i + 1) * 64, :] = got[:, i * 128 : (i + 1) * 128]
    for i in range(1, 3):
        place = slice(192 - 64 * i, 256 - 64 * i)
        mv.arrived(kw.at[place, :], r_kv.at[0, i - 1])
        mv.arrived(vw.at[place, :], r_kv.at[1, i - 1])

    scale = 128.0**-0.5
    allowed = jnp.concatenate([attention_mask(segments, t)] * 4, axis=0) > 0.5
    for i in range(2):
        part = slice(i * 256, (i + 1) * 256)
        scores = jnp.where(allowed, nt(qh[part, :], kw[...]) * scale, -1e30)
        powers = jnp.exp(scores - jnp.max(scores, -1, keepdims=True))
        probs = powers / jnp.sum(powers, -1, keepdims=True)
        low = probs.astype(BF16)
        attended = dot(low, vw[...]).astype(BF16)
        for j in range(4):
            at[i, y, mine, j * 128 : (j + 1) * 128] = attended[j * 64 : (j + 1) * 64, :]
        value_grad = tn(low, gh[part, :])
        probs_grad = nt(gh[part, :], vw[...])
        score_grad = probs * (probs_grad - jnp.sum(probs_grad * probs, -1, keepdims=True)) * scale
        score_grad = score_grad.astype(BF16)
        query_grad = dot(score_grad, kw[...]).astype(BF16)
        for j in range(4):
            head = 4 * i + j
            h, at_head = (0, head) if head < 5 else (1, head - 5)
            gq[h, y, mine, at_head * 128 : (at_head + 1) * 128] = query_grad[j * 64 : (j + 1) * 64, :]
        key_grad = tn(score_grad, qh[part, :])
        if i == 0:
            kg[0, :, :] = key_grad
            kg[1, :, :] = value_grad
        else:
            kg[0, :, :] = kg[0, :, :] + key_grad
            kg[1, :, :] = kg[1, :, :] + value_grad
    for i in range(1, 3):
        before = rem(t + 16 - i, 16)
        to = me.at(x=rem(before, 4), y=lax.div(before, jnp.int32(4)))
        mv.send(kg.at[:, 192 - 64 * i : 256 - 64 * i, :], kgot.at[i - 1], s_kg.at[i - 1], r_kg.at[i - 1], to)
    ends.start(0)
    for i in range(2):
        mv.arrived(kgot.at[i], r_kg.at[i])
    for i in range(2):
        total = kg[i, 192:256, :] + kgot[0, i] + kgot[1, i]
        gq[1, y, mine, 384 + 128 * i : 512 + 128 * i] = total.astype(BF16)
    ends.start(1)
    mv.settle(line_sum)
    mv.settle("xa")
    mv.settle("ctx")
    mv.settle(back)
    ends.middle()
    both(attends.start)

    def hidden_part(e):
        q = ends.group(e)
        for j in range(2):
            columns = slice(j * 256, (j + 1) * 256)
            total = nt(gq[0, q], wq[1, columns, 0:640])
            total = total + nt(gq[1, q, :, 0:384], wq[1, columns, 640:1024])
            total = total + nt(gq[1, q, :, 384:512], wk[1, columns, :])
            total = total + nt(gq[1, q, :, 512:640], wv[1, columns, :])
            line_sum.refs[0][e, :, columns] = total.astype(BF16)
        line_sum.swap(e)

    def query_weight(h):
        for first in (0, 256, 512, 640, 896):
            width = 128 if first in (512, 896) else 256
            i, there = (0, first) if first < 640 else (1, first - 640)
            total = jnp.zeros((512, width), F32)
            for q in range(4):
                total = total + tn(xn[h, q], gq[i, q, :, there : there + width])
            total = total.astype(BF16)
            place = first % 512
            for k in range(2):
                stage[h, 2 * k + first // 512, :, place : place + width] = total[k * 256 : (k + 1) * 256, :]
        for k in range(4):
            local_out(stage.at[h, k], query_out.at[h, (k // 2) * 256 : (k // 2 + 1) * 256, (k % 2) * 512 : (k % 2 + 1) * 512])

    def key_value_weight(h):
        total = jnp.zeros((512, 256), F32)
        for q in range(4):
            total = total + tn(xn[h, q], gq[1, q, :, 384:640])
        kvs[0, h] = total[:, 0:128].astype(BF16)
        kvs[1, h] = total[:, 128:256].astype(BF16)
        local_out(kvs.at[0, h], key_out.at[h])
        local_out(kvs.at[1, h], value_out.at[h])

    def output_weight(h):
        for j in range(2):
            columns = slice(j * 256, (j + 1) * 256)
            total = jnp.zeros((512, 256), F32)
            for q in range(4):
                total = total + tn(at[h, q], ea[1, q, :, columns])
            total = total.astype(BF16)
            for k in range(2):
                back_ps[h, k, :, columns] = total[k * 256 : (k + 1) * 256, :]
        for k in range(2):
            local_out(back_ps.at[h, k], output_out.at[(2 * h + k) * 256 : (2 * h + k + 1) * 256, :])

    def output_part(e):
        q = attends.group(e)
        for j in range(2):
            columns = slice(j * 256, (j + 1) * 256)
            total = dot(at[0, q], wo[0:512, columns]) + dot(at[1, q], wo[512:1024, columns])
            output.refs[0][e, :, columns] = total.astype(BF16)
        output.swap(e)

    hidden_part(0)
    ends.end()
    hidden_part(1)
    both(attends.first)
    line_sum.pair(0)
    hidden_part(3)
    line_sum.pair(1)
    both(attends.relay, 0)
    both(attends.far)
    hidden_part(2)
    line_sum.pair(3)
    line_sum.pair(2)
    both(attends.relay, 3)
    key_value_weight(0)
    key_value_weight(1)
    both(attends.relay, 1)
    query_weight(0)
    hidden_grad = line_sum.total()
    scaled = hidden_grad * scale_j
    value = joined[...]
    inner_stats.start(lanes(jnp.sum(scaled * value, -1, keepdims=True)))
    own_rate = hidden_rates.tiles[2 * q0 + c]
    jg[q0, half, :] = (cotangent[...].astype(F32) + column(own_rate[0:1, :]) * scaled).astype(BF16)
    grad_rows.to_sibling(0)
    grad_rows.along_z()
    attends.end()
    query_weight(1)
    for e in (0, 1, 3, 2):
        output_part(e)
    mean = inner_stats.total() / 8192.0
    factors.start(own_rate * own_rate * own_rate * mean)
    for e in (0, 1, 3, 2):
        output.pair(e)
    for e in NEAR:
        grad_rows.forward(e)
    output_weight(0)
    output_weight(1)
    factors.whole()
    for e in (0, 1, 3, 2):
        grad_rows.whole(e)
        q = grad_rows.group[e]
        for k in range(2):
            part = slice(k * 128, (k + 1) * 128)
            grad = jg[q, part, :].astype(F32) - xa[q, part, :].astype(F32) * factors.column(q, k)
            xa[q, part, :] = grad.astype(BF16)
        local_out(xa.at[q], grads_out.at[q])
    draft[...] = (value + output.total()).astype(BF16)
    mv.drain()
    for copy in outs:
        copy.wait()


def step_call(*args):
    def gather_g():
        return [dma(3), dma(3), dma(4), dma(4)]

    shape = jax.ShapeDtypeStruct
    return pl.pallas_call(
        step_kernel,
        name="step",
        out_shape=(
            shape((128, 512), BF16),
            shape((2, 4, 3, 256, 512), BF16),
            shape((4, 256, 512), BF16),
            shape((2, 512, 1024), BF16),
            shape((2, 512, 128), BF16),
            shape((2, 512, 128), BF16),
            shape((1024, 512), BF16),
        ),
        in_specs=[IN_VMEM] * 7 + [ANYWHERE] * 6,
        out_specs=(IN_VMEM, *[ANYWHERE] * 6),
        scratch_shapes=[
            vmem(3, 512, 1024),
            vmem(3, 1024, 512),
            vmem(2, 512, 1024),
            vmem(2, 512, 128),
            vmem(2, 512, 128),
            vmem(1024, 512),
            vmem(4, 3, 256, 512),
            vmem(2, 4, 3, 256, 512),
            vmem(2, 4, 3, 256, 512),
            vmem(2, 4, 256, 512),
            vmem(4, 256, 512),
            vmem(512, 128),
            vmem(512, 128),
            vmem(256, 128),
            vmem(256, 128),
            vmem(2, 256, 128, dtype=F32),
            vmem(2, 2, 64, 128, dtype=F32),
            vmem(2, 4, 256, 640),
            vmem(2, 4, 256, 512),
            vmem(4, 256, 512),
            vmem(128, 512, dtype=F32),
            vmem(2, 2, 512, 128),
            vmem(2, 4, 256, 640),
            vmem(4, 256, 512, dtype=F32),
            dma(26), dma(2, 2), dma(2, 2), dma(2), dma(2), dma(6),
            *gather_g(), *gather_g(), *gather_g(),
            *SumT.scratch(512), *SumT.scratch(512), *SumT.scratch(512),
            *gather_g(), *gather_g(), *gather_g(),
            *StatsT.scratch(), *StatsT.scratch(), *StatsT.scratch(),
            *TilesG.scratch(), *TilesG.scratch(), *TilesG.scratch(),
            *SumT.scratch(512), *SumT.scratch(640), *SumG.scratch(), *SumG.scratch(),
            *GatherT.scratch(), *GatherT.scratch(), *GatherT.scratch(), *GatherT.scratch(), *GatherT.scratch(),
        ],
        compiler_params=pltpu.CompilerParams(
            collective_id=0, has_side_effects=True, vmem_limit_bytes=VMEM_LIMIT
        ),
        cost_estimate=pl.CostEstimate(flops=20000000000, bytes_accessed=24000000, transcendentals=0),
    )(*args)


def join_weight_kernel(feats, grads, *refs):
    given, join_out, results = refs[:5], refs[5], refs[6:11]
    fa, jg, stage, s_in, s_out, s_on = refs[11:17]
    held = refs[17:]
    taken = [pltpu.make_async_copy(src, dst, s_on.at[i]) for i, (src, dst) in enumerate(zip(given, held))]
    handed = [pltpu.make_async_copy(src, dst, s_on.at[5 + i]) for i, (src, dst) in enumerate(zip(held, results))]
    loads = [pltpu.make_async_copy(grads, jg, s_in.at[3])]
    loads += [pltpu.make_async_copy(feats.at[:, :, l], fa.at[:, :, l], s_in.at[l]) for l in range(3)]
    for copy in loads + taken:
        copy.start()
    loads[0].wait()
    outs = []
    for l in range(3):
        loads[1 + l].wait()
        if l == 1:
            for there, back in zip(taken, handed):
                there.wait()
                back.start()
        for h in range(2):
            for j in range(2):
                columns = slice(j * 256, (j + 1) * 256)
                total = jnp.zeros((512, 256), F32)
                for q in range(4):
                    total = total + tn(fa[h, q, l], jg[q, :, columns])
                stage[l, h, :, columns] = total.astype(BF16)
            copy = pltpu.make_async_copy(stage.at[l, h], join_out.at[l, h * 512 : (h + 1) * 512, :], s_out.at[2 * l + h])
            copy.start()
            outs.append(copy)
    for copy in outs + handed:
        copy.wait()


def join_weight_call(feats, grads, *given):
    return pl.pallas_call(
        join_weight_kernel,
        name="join_weight",
        out_shape=(
            jax.ShapeDtypeStruct((3, 1024, 512), BF16),
            *[jax.ShapeDtypeStruct(array.shape, array.dtype) for array in given],
        ),
        in_specs=[ANYWHERE] * (2 + len(given)),
        out_specs=tuple([ANYWHERE] * (1 + len(given))),
        scratch_shapes=[
            vmem(2, 4, 3, 256, 512), vmem(4, 256, 512), vmem(3, 2, 512, 512), dma(4), dma(6), dma(10),
            *[pltpu.VMEM(array.shape, array.dtype) for array in given],
        ],
        compiler_params=pltpu.CompilerParams(vmem_limit_bytes=VMEM_LIMIT),
        cost_estimate=pl.CostEstimate(flops=3300000000, bytes_accessed=20000000, transcendentals=0),
    )(feats, grads, *given)


def local(
    context,
    resid_in,
    target_out_w,
    embedded,
    join_w,
    embed_gain,
    joined_gain,
    query_w,
    key_w,
    value_w,
    out_w,
    segment_ids,
    grad_hidden,
):
    draft_hidden, feats, grads, *weights = step_call(
        context.transpose(1, 0, 2),
        resid_in.transpose(1, 0, 2),
        embedded,
        grad_hidden,
        embed_gain,
        joined_gain,
        segment_ids,
        target_out_w,
        join_w,
        query_w,
        key_w,
        value_w,
        out_w,
    )
    grad_join, draft_hidden, *weights = join_weight_call(feats, grads, draft_hidden, *weights)
    return (draft_hidden, grad_join, *weights)


def solution(mesh):
    in_specs = (
        P(("group", "seq"), None, "tensor"),
        P("tensor", None, ("group", "seq")),
        P(None, "tensor", ("group", "seq")),
        P(("group", "seq"), "tensor"),
        P(None, ("group", "seq"), "tensor"),
        P("tensor"),
        P("tensor"),
        P(None, "tensor", ("group", "seq")),
        P(None, "tensor", ("group", "seq")),
        P(None, "tensor", ("group", "seq")),
        P(("group", "seq"), "tensor"),
        P(),
        P(("group", "seq"), "tensor"),
    )
    out_specs = (
        P(("group", "seq"), "tensor"),
        P(None, ("group", "seq"), "tensor"),
        P(None, "tensor", ("group", "seq")),
        P(None, "tensor", ("group", "seq")),
        P(None, "tensor", ("group", "seq")),
        P(("group", "seq"), "tensor"),
    )
    return jax.shard_map(local, mesh=mesh, in_specs=in_specs, out_specs=out_specs, check_vma=False)
```
